32 devices in a mesh: tm: 8 (over z, y), row: 4 (over x, core).
Axes of the slice: x: 2, y: 2, z: 4, core: 2. Of those that a mesh axis runs over, the one named last changes fastest.
Arguments:
- edge_factor: float32 [8, 512, 512], P('tm', 'row'), may hold values from -0.25 to 0.25
- mass: float32 [8, 512], P('tm', 'row'), may hold values from 0.001 to 0.01
- rhs: float32 [8, 512, 512], P('tm', None, 'row'), may hold values from -0.25 to 0.25
Outputs:
- solution: float32 [8, 512, 512], P('tm', None, 'row')
The draws below stay inside these ranges and needn't reach their ends.
All inputs are finite; a program needn't handle non-finite values.
Results may differ from the reference program's by a relative error of at most 0.0003.
Values sent between devices are 32-bit elements; how exact they have to be, the bound alone decides.
No kernel may reach another device: no remote copies, remote signals or barrier semaphores. Data moves between devices by JAX's collectives and lax.ppermute only.
A program may use at most 128 MiB of HBM per device.

```python
import math
import jax
import jax.numpy as jnp
from jax import lax

NODES = 512
BLOCKS = 8
RHS = 512


def draw_rhs(key, part):
    shape_all = (BLOCKS, NODES, RHS)
    return jnp.clip(0.05 * jax.random.normal(key, shape_all, jnp.float32), -0.25, 0.25)


def shard_levels(stream_key, extent, shards, smallest, top_value):
    loudness, own = 1.0, jax.random.fold_in(stream_key, 6)
    for position, shards_of in shards:
        steps = jnp.exp(jax.random.uniform(jax.random.fold_in(own, position), (shards_of,), jnp.float32, smallest / len(shards), top_value / len(shards)))
        loudness = loudness * jnp.repeat(steps, extent[position] // shards_of).reshape([-1 if axis == position else 1 for axis in range(len(extent))])
    return loudness


def noise(stream_key, extent, scale, most, cuts=(), held_as=jnp.bfloat16):
    values = jax.random.normal(stream_key, extent, jnp.float32) * scale
    if len(cuts) > 0:
        values = shard_levels(stream_key, extent, cuts, -0.22, 0.18) * values
    return jnp.clip(values, min=-most, max=most).astype(held_as)


def setup_inputs(seed: int = 0) -> dict:
    keys = jax.random.split(jax.random.key(seed), 4)
    edge_factor = noise(keys[0], (BLOCKS, NODES, NODES), NODES ** -0.5, 0.25, ((0, 8), (1, 4)), jnp.float32)
    mass = jnp.clip(jnp.exp(math.log(0.01) - 2.30258502 * jax.random.uniform(keys[1], (BLOCKS, NODES), jnp.float32) ** shard_levels(keys[1], (BLOCKS, NODES), ((0, 8), (1, 4)), -0.2, 0.2)), 0.001, 0.01)
    rhs = draw_rhs(jax.random.fold_in(keys[3], 71), 0)
    return {"edge_factor": edge_factor, "mass": mass, "rhs": rhs}


exact_prec = lax.Precision.HIGHEST

def edge_gram(factor):
    return jnp.dot(factor.astype(jnp.float32), factor.T.astype(jnp.float32), precision=exact_prec, preferred_element_type=jnp.float32)

def solve_lower(factor, values):
    return jax.scipy.linalg.solve_triangular(factor, values, lower=True)

def reference(edge_factor, mass, rhs):
    edge_all = lax.map(edge_gram, edge_factor)
    zero_block = jnp.zeros((1, NODES, NODES), jnp.float32)
    edge_next = jnp.concatenate([edge_all[1:], zero_block], axis=0)
    mass_diag = jax.vmap(jnp.diag)(mass)
    diag_blocks = mass_diag + edge_all + edge_next
    keep_mask = (jnp.arange(BLOCKS) > 0).astype(jnp.float32)[:, None, None]
    low_blocks = -edge_all * keep_mask
    low_next = jnp.concatenate([low_blocks[1:], zero_block], axis=0)

    def forward(state_pair, step_in):
        factor_prev, carried = state_pair
        diag_block, low_block, rhs_block = step_in
        whitened = solve_lower(factor_prev, low_block.T)
        schur_block = diag_block - jnp.dot(whitened.T, whitened, precision=exact_prec)
        carried_solve = solve_lower(factor_prev, carried)
        reduced = rhs_block - jnp.dot(whitened.T, carried_solve, precision=exact_prec)
        factor = jnp.linalg.cholesky(schur_block)
        return ((factor, reduced), (factor, reduced))
    start_pair = (jnp.eye(NODES, dtype=jnp.float32), jnp.zeros((NODES, RHS), jnp.float32))
    _, (factors, reduced_all) = lax.scan(forward, start_pair, (diag_blocks, low_blocks, rhs))

    def backward(next_solution, step_in):
        factor, reduced, low_after = step_in
        rhs_value = reduced - jnp.dot(low_after.T, next_solution, precision=exact_prec)
        inner = solve_lower(factor, rhs_value)
        current = jax.scipy.linalg.solve_triangular(factor, inner, lower=True, trans=1)
        return (current, current)
    _, solution = lax.scan(backward, jnp.zeros((NODES, RHS), jnp.float32), (factors, reduced_all, low_next), reverse=True)
    return solution
```

```python
import functools

import jax
import jax.numpy as jnp
from jax import lax
from jax.experimental import pallas as pl
from jax.experimental.pallas import tpu as pltpu
from jax.sharding import PartitionSpec as P

exact_prec = lax.Precision.HIGHEST
lanes = 128
group = 8
vmem_bytes = 58 * 1024 * 1024


def dot(a, b):
    return lax.dot_general(
        a, b, (((1,), (0,)), ((), ())), precision=exact_prec, preferred_element_type=jnp.float32
    )


def dot_nt(a, b):
    return lax.dot_general(
        a, b, (((1,), (1,)), ((), ())), precision=exact_prec, preferred_element_type=jnp.float32
    )


def spread_rows(row):
    return jnp.broadcast_to(row, (group, lanes))


def inverse_8(cols, sub_ids):
    for k in range(0, group, 2):
        u, v = cols[k], cols[k + 1]
        a = spread_rows(u[k : k + 1])
        b = spread_rows(u[k + 1 : k + 2])
        c = spread_rows(v[k + 1 : k + 2])
        scale = 1.0 / (a * c - b * b)
        inv_a, inv_b, inv_c = c * scale, -b * scale, a * scale
        is_k, is_l = sub_ids == k, sub_ids == k + 1
        pair = is_k | is_l
        first = jnp.where(is_k, inv_a, jnp.where(is_l, inv_b, -(inv_a * u + inv_b * v)))
        second = jnp.where(is_k, inv_b, jnp.where(is_l, inv_c, -(inv_b * u + inv_c * v)))
        done = []
        for j in range(group):
            if j == k:
                done.append(first)
            elif j == k + 1:
                done.append(second)
            else:
                row_k = spread_rows(cols[j][k : k + 1])
                row_l = spread_rows(cols[j][k + 1 : k + 2])
                kept = jnp.where(pair, 0.0, cols[j])
                done.append(kept + (first * row_k + second * row_l))
        cols = done
    return cols


def inverse_128(block):
    slabs = [block[group * i : group * (i + 1)] for i in range(lanes // group)]
    sub_ids = lax.broadcasted_iota(jnp.int32, (group, lanes), 0)
    lane_ids = lax.broadcasted_iota(jnp.int32, (group, lanes), 1)
    for p in range(lanes // group):
        start = group * p
        own = (lane_ids >= start) & (lane_ids < start + group)
        unit = jnp.where(lane_ids == sub_ids + start, 1.0, 0.0)
        spread = lambda slab, j: jnp.broadcast_to(
            slab[:, start + j : start + j + 1], (group, lanes)
        )
        small = inverse_8([spread(slabs[p], j) for j in range(group)], sub_ids)
        pivot = jnp.where(own, unit, slabs[p])
        solved = small[0] * spread_rows(pivot[0:1])
        for j in range(1, group):
            solved = solved + small[j] * spread_rows(pivot[j : j + 1])
        solved_rows = [spread_rows(solved[j : j + 1]) for j in range(group)]
        done = []
        for i in range(lanes // group):
            if i == p:
                done.append(solved)
                continue
            change = spread(slabs[i], 0) * solved_rows[0]
            for j in range(1, group):
                change = change + spread(slabs[i], j) * solved_rows[j]
            done.append(jnp.where(own, 0.0, slabs[i]) - change)
        slabs = done
    return jnp.concatenate(slabs, axis=0)


def eliminate(table, size):
    panels = size // lanes
    for p in range(panels):
        at, after = lanes * p, lanes * (p + 1)
        inverse = inverse_128(table[at:after, at:after])
        solved = dot(inverse, table[at:after, after:])
        for q in range(panels):
            if q != p:
                rows = slice(lanes * q, lanes * (q + 1))
                table[rows, after:] = table[rows, after:] - dot(table[rows, at:after], solved)
        table[at:after, after:] = solved


def add_mass(table, gathered, block, size):
    quarter = gathered.shape[2] - group
    for s in range(size // quarter):
        rows = slice(quarter * s, quarter * (s + 1))
        mass = gathered[block, s, quarter : quarter + 1, :quarter]
        ids = (quarter, quarter)
        diag = lax.broadcasted_iota(jnp.int32, ids, 0) == lax.broadcasted_iota(jnp.int32, ids, 1)
        table[rows, rows] = table[rows, rows] + jnp.where(diag, mass, 0.0)


def factor_of(gathered, block, size):
    quarter = gathered.shape[2] - group
    return jnp.concatenate([gathered[block, s, :quarter, :] for s in range(size // quarter)], axis=0)


def chain_kernel(steps, side_ref, gathered, rhs, solved, carry, last_edge, table):
    size = table.shape[0]
    right = side_ref[0]
    start = factor_of(gathered, 0, size)
    start_gram = dot_nt(start, start)
    last_edge[...] = jnp.where(right == 0, start_gram, 0.0)
    carry[...] = jnp.zeros_like(carry)

    def step(i, _):
        block = jnp.where(right == 0, i, steps - i)
        edge_block = jnp.where(right == 0, i + 1, steps - i)
        factor = factor_of(gathered, edge_block, size)
        edge = dot_nt(factor, factor)
        table[:, :size] = last_edge[...] + edge - carry[:, :size]
        add_mass(table, gathered, block, size)
        table[:, size : 2 * size] = edge
        table[:, 2 * size :] = rhs[block] + carry[:, size:]
        last_edge[...] = edge
        eliminate(table, size)
        solved[i] = table[:, size:]
        carry[...] = dot(last_edge[...], table[:, size:])
        return 0

    lax.fori_loop(0, steps, step, 0)


def middle_kernel(steps, side_ref, gathered, from_right, rhs, carry, last_edge, reduced, sent, table, kept):
    size = table.shape[0]
    right = side_ref[0]
    block = jnp.where(right == 0, steps, 0)

    @pl.when(right == 0)
    def _():
        factor = factor_of(from_right, 0, size)
        table[:, size : 2 * size] = dot_nt(factor, factor)

    @pl.when(right != 0)
    def _():
        factor = factor_of(gathered, 0, size)
        table[:, size : 2 * size] = dot_nt(factor, factor)

    edge = table[:, size : 2 * size]
    table[:, :size] = last_edge[...] + edge - carry[:, :size]
    add_mass(table, gathered, block, size)
    table[:, 2 * size :] = rhs[block] + carry[:, size:]
    reduced[:, :size] = table[:, :size]
    reduced[:, size:] = table[:, 2 * size :]
    kept[...] = edge
    eliminate(table, size)
    sent[...] = dot(kept[...], table[:, size:])


def final_kernel(steps, side_ref, reduced, received, solved, out, table):
    size = table.shape[0]
    place = side_ref[1]
    table[:, :size] = reduced[:, :size] - received[:, :size]
    table[:, size:] = reduced[:, size:] + received[:, size:]
    eliminate(table, size)

    @pl.when(place == steps)
    def _():
        out[...] = table[:, size:]

    def back(n, _):
        i = steps - 1 - n
        here = solved[i, :, size:] + dot(solved[i, :, :size], table[:, size:])
        table[:, size:] = here

        @pl.when(place == i)
        def _():
            out[...] = here

        return 0

    lax.fori_loop(0, steps, back, 0)


def local(edge_factor, mass, rhs):
    _, quarter, size = edge_factor.shape
    cols = rhs.shape[2]
    blocks, parts = lax.axis_size("tm"), lax.axis_size("row")
    half = blocks // 2
    steps = half - 1
    mine = lax.axis_index("tm")
    right = (mine >= half).astype(jnp.int32)
    place = jnp.where(right == 0, mine, blocks - 1 - mine)
    side = jnp.stack([right, place]).astype(jnp.int32)

    halves = [[side_at * half + i for i in range(half)] for side_at in range(2)]
    halves_all = [[t * parts + r for t in ids for r in range(parts)] for ids in halves]
    mass_rows = jnp.pad(mass, ((0, group - 1), (0, size - quarter)))
    packed = jnp.concatenate([edge_factor[0], mass_rows], axis=0)
    gathered = lax.all_gather(packed, ("tm", "row"), axis_index_groups=halves_all)
    gathered = gathered.reshape(half, parts, quarter + group, size)
    rhs_half = lax.all_gather(rhs[0], "tm", axis_index_groups=halves)
    down = [(t + half, t) for t in range(half)]
    from_right = lax.ppermute(gathered[:1], "tm", down)

    smem = pl.BlockSpec(memory_space=pltpu.SMEM)
    vmem = pl.BlockSpec(memory_space=pltpu.VMEM)
    params = pltpu.CompilerParams(vmem_limit_bytes=vmem_bytes)
    f32 = lambda *shape: jax.ShapeDtypeStruct(shape, jnp.float32)
    scratch = lambda *shape: pltpu.VMEM(shape, jnp.float32)

    solved, carry, last_edge = pl.pallas_call(
        functools.partial(chain_kernel, steps),
        out_shape=(f32(steps, size, size + cols), f32(size, size + cols), f32(size, size)),
        in_specs=[smem, vmem, vmem],
        out_specs=(vmem, vmem, vmem),
        scratch_shapes=[scratch(size, 2 * size + cols)],
        compiler_params=params,
    )(side, gathered, rhs_half)

    reduced, sent = pl.pallas_call(
        functools.partial(middle_kernel, steps),
        out_shape=(f32(size, size + cols), f32(size, size + cols)),
        in_specs=[smem] + [vmem] * 5,
        out_specs=(vmem, vmem),
        scratch_shapes=[scratch(size, 2 * size + cols), scratch(size, size)],
        compiler_params=params,
    )(side, gathered, from_right, rhs_half, carry, last_edge)

    across = [(t, (t + half) % blocks) for t in range(blocks)]
    received = lax.ppermute(sent, "tm", across)

    solution = pl.pallas_call(
        functools.partial(final_kernel, steps),
        out_shape=f32(size, cols),
        in_specs=[smem] + [vmem] * 3,
        out_specs=vmem,
        scratch_shapes=[scratch(size, size + cols)],
        compiler_params=params,
    )(side, reduced, received, solved)
    return solution[None]


def solution(mesh):
    placed = (P("tm", "row", None), P("tm", "row"), P("tm", None, "row"))
    return jax.shard_map(
        local, mesh=mesh, in_specs=placed, out_specs=P("tm", None, "row"), check_vma=False
    )
```

```python
import functools

import jax
import jax.numpy as jnp
from jax import lax
from jax.experimental import pallas as pl
from jax.experimental.pallas import tpu as pltpu
from jax.sharding import PartitionSpec as P

lanes = 128
group = 8
vmem_bytes = 58 * 1024 * 1024
bf16 = jnp.bfloat16


def split(x):
    high = x.astype(bf16)
    rest = x - high.astype(jnp.float32)
    middle = rest.astype(bf16)
    low = (rest - middle.astype(jnp.float32)).astype(bf16)
    return high, middle, low


def left_terms(x):
    a, b, c = split(x)
    return jnp.concatenate([a, a, b, b, a, c], axis=1)


def right_terms(x, axis=0):
    a, b, c = split(x)
    return jnp.concatenate([a, b, a, b, c, a], axis=axis)


def dot(left, right, right_dim=0):
    return lax.dot_general(
        left, right, (((1,), (right_dim,)), ((), ())), preferred_element_type=jnp.float32
    )


def spread_row(block, row):
    return jnp.broadcast_to(block[row : row + 1], (group, lanes))


def spread_col(block, col):
    return jnp.broadcast_to(block[:, col : col + 1], (group, lanes))


def reciprocal(x):
    r = pl.reciprocal(x, approx=True)
    r = r * (2.0 - x * r)
    return r * (2.0 - x * r)


def total(terms):
    while len(terms) > 1:
        paired = [terms[i] + terms[i + 1] for i in range(0, len(terms) - 1, 2)]
        terms = paired + terms[len(paired) * 2 :]
    return terms[0]


def inverse_128(block, between):
    count = lanes // group
    slabs = [block[group * i : group * (i + 1)] for i in range(count)]
    sub_ids = lax.broadcasted_iota(jnp.int32, (group, lanes), 0)
    lane_ids = lax.broadcasted_iota(jnp.int32, (group, lanes), 1)
    ahead = [spread_col(slabs[0], j) for j in range(group)]
    for p in range(count):
        start = group * p
        more = p + 1 < count
        top = list(ahead)
        low = []
        if more:
            top += [spread_col(slabs[p], start + group + j) for j in range(group)]
            low = [spread_col(slabs[p + 1], start + j) for j in range(2 * group)]
        for k in range(0, group, 2):
            u, v = top[k], top[k + 1]
            a, b, c = spread_row(u, k), spread_row(u, k + 1), spread_row(v, k + 1)
            scale = reciprocal(a * c - b * b)
            is_k, is_l = sub_ids == k, sub_ids == k + 1
            first = jnp.where(is_k, -c, jnp.where(is_l, b, c * u - b * v))
            second = jnp.where(is_k, b, jnp.where(is_l, -a, a * v - b * u))
            if more:
                low_first = c * low[k] - b * low[k + 1]
                low_second = a * low[k + 1] - b * low[k]
            done = []
            for j in range(len(top)):
                if j == k:
                    done.append(-scale * first)
                elif j == k + 1:
                    done.append(-scale * second)
                else:
                    row_k, row_l = spread_row(top[j], k), spread_row(top[j], k + 1)
                    kept = top[j]
                    if j < group:
                        kept = jnp.where(is_k | is_l, 0.0, kept)
                    done.append(kept - scale * (first * row_k + second * row_l))
                    if more and j > k:
                        low[j] = low[j] - scale * (low_first * row_k + low_second * row_l)
            top = done
        small, ahead = top[:group], low[group:]
        own = (lane_ids >= start) & (lane_ids < start + group)
        unit = jnp.where(lane_ids == sub_ids + start, 1.0, 0.0)
        pivot = jnp.where(own, unit, slabs[p])
        solved = total([small[j] * spread_row(pivot, j) for j in range(group)])
        rows = [spread_row(solved, j) for j in range(group)]
        done = []
        for i in range(count):
            if i == p:
                done.append(solved)
            else:
                change = total([spread_col(slabs[i], start + j) * rows[j] for j in range(group)])
                done.append(jnp.where(own, 0.0, slabs[i]) - change)
        slabs = done
        between(p, count)
    return jnp.concatenate(slabs, axis=0)


class Queue:
    def __init__(self):
        self.tasks = []

    def add(self, task):
        self.tasks.append(task)

    def between(self, step, count):
        for _ in range(-(-len(self.tasks) // (count - step))):
            self.tasks.pop(0)()

    def flush(self):
        while self.tasks:
            self.tasks.pop(0)()


def span(first, last):
    return slice(lanes * first, lanes * last)


class System:
    def __init__(self, top, bottom, right, terms_left, terms_right):
        self.top, self.bottom, self.right = top, bottom, right
        self.terms_left, self.terms_right = terms_left, terms_right
        self.panels = top.shape[-2] // lanes
        self.blocks = top.shape[-1] // lanes

    def at(self, rows, cols):
        if rows[0] < self.panels:
            return self.top, (span(*rows), span(*cols))
        low = self.panels
        return self.bottom, (span(rows[0] - low, rows[1] - low), span(cols[0] - low, cols[1] - low))

    def load(self, rows, cols):
        ref, where = self.at(rows, cols)
        return ref[where]

    def store(self, rows, cols, value):
        ref, where = self.at(rows, cols)
        ref[where] = value

    def prepare(self, p, q):
        self.terms_left[span(q, q + 1), :] = left_terms(self.load((p, p + 1), (q, q + 1)).T)

    def solve(self, p, cols, inverse):
        solved = dot(inverse, right_terms(self.load((p, p + 1), cols)))
        self.store((p, p + 1), cols, solved)
        self.terms_right[:, span(*cols)] = right_terms(solved)

    def update(self, rows, cols):
        change = dot(self.terms_left[span(*rows), :], self.terms_right[:, span(*cols)])
        self.store(rows, cols, self.load(rows, cols) - change)

    def forward(self, p, inverse, out):
        here = left_terms(self.right[:, span(p, p + 1)])
        out[:, span(p, p + 1)] = dot(here, inverse)
        if p + 1 < self.blocks:
            later = span(p + 1, self.blocks)
            self.right[:, later] = self.right[:, later] - dot(here, self.terms_right[:, later])

    def eliminate(self, queue, out):
        for p in range(self.panels):
            inverse = inverse_128(self.load((p, p + 1), (p, p + 1)), queue.between)
            queue.flush()
            self.store((p, p + 1), (p, p + 1), inverse)
            terms = left_terms(inverse)
            after = p + 1
            if after < self.blocks:
                self.prepare(p, after)
                self.solve(p, (after, after + 1), terms)
                self.update((after, after + 1), (after, after + 1))
            strips = []
            q = after + 1
            while q < self.blocks:
                end = min(self.blocks, q + 2 if q % 2 == 0 else q + 1)
                strips.append((q, end))
                q = end
            for strip in strips:
                for q in range(*strip):
                    queue.add(functools.partial(self.prepare, p, q))
                queue.add(functools.partial(self.solve, p, strip, terms))
            for strip in strips:
                start = after
                while start < strip[1]:
                    end = min(strip[1], start + 4)
                    if start < self.panels:
                        end = min(end, self.panels)
                    queue.add(functools.partial(self.update, (start, end), strip))
                    start = end
            queue.add(functools.partial(self.forward, p, right_terms(inverse), out))
        queue.flush()

    def back(self, known, solved_right, x):
        for p in reversed(range(self.panels)):
            here = solved_right[:, span(p, p + 1)]
            if known is not None:
                factor = self.top[span(p, p + 1), span(self.panels, self.blocks)]
                here = here - dot(known, right_terms(factor, 1), 1)
            if p + 1 < self.panels:
                later = span(p + 1, self.panels)
                factor = self.top[span(p, p + 1), later]
                here = here - dot(left_terms(x[:, later]), right_terms(factor, 1), 1)
            x[:, span(p, p + 1)] = here


def gram_tasks(queue, slabs, out, terms_left, terms_right):
    rows = out.shape[0] // len(slabs)

    def load(s):
        value = slabs[s]()
        terms_left[rows * s : rows * (s + 1), :] = left_terms(value)
        terms_right[rows * s : rows * (s + 1), :] = right_terms(value, 1)

    def multiply(s):
        here = slice(rows * s, rows * (s + 1))
        out[here, :] = dot(terms_left[here, :], terms_right[...], 1)

    for s in range(len(slabs)):
        queue.add(functools.partial(load, s))
    for s in range(len(slabs)):
        queue.add(functools.partial(multiply, s))


def slabs_of(edge):
    rows = edge.shape[2] - group
    return [lambda s=s: edge[0, s, :rows, :] for s in range(edge.shape[1])]


def add_mass(table, mass, rows):
    for s in range(mass.shape[1]):
        here = slice(rows * s, rows * (s + 1))
        ids = (rows, rows)
        diag = lax.broadcasted_iota(jnp.int32, ids, 0) == lax.broadcasted_iota(jnp.int32, ids, 1)
        table[here, here] = table[here, here] + jnp.where(diag, mass[0, s, :1, :rows], 0.0)


def add_rhs(right, rhs, first):
    for q in range(rhs.shape[1] // lanes):
        right[:, span(first + q, first + q + 1)] = rhs[0, span(q, q + 1), :].T


def packed_pieces(size):
    panels = size // lanes
    order = [[p for p in range(panels) if p % 4 in (0, 3)], [p for p in range(panels) if p % 4 in (1, 2)]]
    return [[(p, p, panels) for p in rows] for rows in order]


def chain_kernel(
    side, start_edge, first_edge, next_edge, first_mass, next_mass, first_rhs, next_rhs,
    solved, solved_right, reduced, reduced_right, sent,
    edge, right_rows, edge_left, edge_right, terms_left, terms_right,
):
    size = reduced.shape[0]
    quarter = start_edge.shape[2] - group
    step, steps = pl.program_id(0), pl.num_programs(0)

    @pl.when(step == 0)
    def _():
        queue = Queue()
        gram_tasks(queue, slabs_of(start_edge), edge, edge_left, edge_right)
        queue.flush()
        reduced[...] = jnp.where(side[0] == 0, edge[...], 0.0)
        add_mass(reduced, first_mass, quarter)
        gram_tasks(queue, slabs_of(first_edge), edge, edge_left, edge_right)
        queue.flush()
        add_rhs(reduced_right, first_rhs, 0)

    top = solved.at[0]
    top[:, :size] = reduced[...] + edge[...]
    top[:, size:] = -edge[...]
    reduced[...] = edge[...]
    add_mass(reduced, next_mass, quarter)
    right_rows[:, :size] = reduced_right[...]
    add_rhs(right_rows, next_rhs, size // lanes)

    queue = Queue()
    gram_tasks(queue, slabs_of(next_edge), edge, edge_left, edge_right)
    system = System(top, reduced, right_rows, terms_left, terms_right)
    system.eliminate(queue, solved_right.at[0])
    reduced_right[...] = right_rows[:, size:]

    for part, pieces in enumerate(packed_pieces(size)):

        @pl.when((step == steps - 1) & (side[2] == part))
        def _():
            at = 0
            for p, first, last in pieces:
                width = lanes * (last - first)
                sent[:, at : at + width] = reduced[span(p, p + 1), span(first, last)]
                at += width
            sent[:, at:] = reduced_right[...]


def middle_kernel(
    side, own_edge, mine, other, reduced, reduced_right,
    solved, solved_right, target, target_right,
    right_rows, edge_left, edge_right, terms_left, terms_right,
):
    size = reduced.shape[0]
    quarter = own_edge.shape[2] - group
    per_part = mine.shape[0]

    def slab(s):
        sent = jnp.where(
            side[2] == s // per_part, mine[s % per_part, :quarter], other[s % per_part, :quarter]
        )
        return jnp.where(side[0] == 0, sent, own_edge[0, s, :quarter])

    queue = Queue()
    slabs = [functools.partial(slab, s) for s in range(own_edge.shape[1])]
    gram_tasks(queue, slabs, target, edge_left, edge_right)
    queue.flush()
    solved[:, :size] = reduced[...] + target[...]
    solved[:, size:] = -target[...]
    right_rows[:, :size] = reduced_right[...]
    right_rows[:, size:] = jnp.zeros_like(target_right)
    system = System(solved, target, right_rows, terms_left, terms_right)
    system.eliminate(queue, solved_right)
    target_right[...] = right_rows[:, size:]


def final_kernel(
    side, target, target_right, mine, other, middle, middle_right, chain, chain_right, out,
    top, right_rows, ended, x, terms_left, terms_right,
):
    size = target.shape[0]
    steps = chain.shape[0]
    place = side[1]
    half_cols = other.shape[1]
    for part, pieces in enumerate(packed_pieces(size)):
        at = 0
        for p, first, last in pieces:
            cols = slice(at, at + lanes * (last - first))
            received = jnp.where(side[2] == part, mine[:, cols], other[:, cols])
            here = (span(p, p + 1), span(first, last))
            top[here] = target[here] + received
            at = cols.stop
    right_rows[...] = target_right[...] + mine[:, half_cols:]
    system = System(top, None, right_rows, terms_left, terms_right)
    system.eliminate(Queue(), ended)
    system.back(None, ended, x)
    known = left_terms(x[...])
    System(middle, None, None, None, None).back(known, middle_right, x)

    def give():
        for q in range(size // lanes):
            out[span(q, q + 1), :] = x[:, span(q, q + 1)].T

    @pl.when(place == steps)
    def _():
        give()

    def walk(n, _):
        i = steps - 1 - n
        known = left_terms(x[...])
        System(chain.at[i], None, None, None, None).back(known, chain_right.at[i], x)

        @pl.when(place == i)
        def _():
            give()

        return 0

    lax.fori_loop(0, steps, walk, 0)


def local(edge_factor, mass, rhs):
    _, quarter, size = edge_factor.shape
    cols = rhs.shape[2]
    blocks, parts = lax.axis_size("tm"), lax.axis_size("row")
    half = blocks // 2
    steps = half - 1
    mine = lax.axis_index("tm")
    right = (mine >= half).astype(jnp.int32)
    place = jnp.where(right == 0, mine, blocks - 1 - mine)
    parity = lax.axis_index("row") % 2
    side = jnp.stack([right, place, parity, mine % half]).astype(jnp.int32)

    halves = [[part * half + i for i in range(half)] for part in range(2)]
    halves_all = [[t * parts + r for t in ids for r in range(parts)] for ids in halves]
    swap = [(r, r ^ 1) for r in range(parts)]
    mass_rows = jnp.pad(mass, ((0, group - 1), (0, size - quarter)))
    packed = jnp.concatenate([edge_factor[0], mass_rows], axis=0)
    gathered = lax.all_gather(packed, ("tm", "row"), axis_index_groups=halves_all)
    gathered = gathered.reshape(half, parts, quarter + group, size)
    rhs_slots = [rhs[0]] + [
        lax.ppermute(rhs[0], "tm", [(t, t ^ d) for t in range(blocks)]) for d in range(1, half)
    ]
    rhs_half = jnp.stack(rhs_slots)
    share = parts // 2
    down = [(t + half, t) for t in range(half)]
    edge_mine = lax.ppermute(
        lax.dynamic_slice_in_dim(gathered[0], parity * share, share), "tm", down
    )
    edge_other = lax.ppermute(edge_mine, "row", swap)

    vmem = pl.BlockSpec(memory_space=pltpu.VMEM)
    smem = pl.BlockSpec(memory_space=pltpu.SMEM)
    f32 = lambda *shape: jax.ShapeDtypeStruct(shape, jnp.float32)
    scratch = lambda *shape: pltpu.VMEM(shape, jnp.float32)
    terms = lambda *shape: pltpu.VMEM(shape, bf16)
    half_cols = sum(lanes * (b - a) for _, a, b in packed_pieces(size)[0])

    def edge_at(i, s):
        return jnp.where(s[0] == 0, i + 1, steps - i)

    def block_at(i, s):
        return jnp.where(s[0] == 0, i, steps - i)

    edge_block = (1, parts, quarter + group, size)
    mass_block = (1, parts, group, size)
    rhs_block = (1, size, cols)
    last = steps - 1
    chain, chain_right, reduced, reduced_right, sent = pl.pallas_call(
        chain_kernel,
        grid_spec=pltpu.PrefetchScalarGridSpec(
            num_scalar_prefetch=1,
            grid=(steps,),
            in_specs=[
                pl.BlockSpec(edge_block, lambda i, s: (0, 0, 0, 0)),
                pl.BlockSpec(edge_block, lambda i, s: (edge_at(0, s), 0, 0, 0)),
                pl.BlockSpec(edge_block, lambda i, s: (edge_at(jnp.minimum(i + 1, last), s), 0, 0, 0)),
                pl.BlockSpec(mass_block, lambda i, s: (block_at(0, s), 0, quarter // group, 0)),
                pl.BlockSpec(mass_block, lambda i, s: (block_at(i + 1, s), 0, quarter // group, 0)),
                pl.BlockSpec(rhs_block, lambda i, s: (block_at(0, s) ^ s[3], 0, 0)),
                pl.BlockSpec(rhs_block, lambda i, s: (block_at(i + 1, s) ^ s[3], 0, 0)),
            ],
            out_specs=(
                pl.BlockSpec((1, size, 2 * size), lambda i, s: (i, 0, 0)),
                pl.BlockSpec((1, cols, size), lambda i, s: (i, 0, 0)),
                pl.BlockSpec((size, size), lambda i, s: (0, 0)),
                pl.BlockSpec((cols, size), lambda i, s: (0, 0)),
                pl.BlockSpec((lanes, half_cols + size), lambda i, s: (0, 0)),
            ),
            scratch_shapes=[
                scratch(size, size),
                scratch(cols, 2 * size),
                terms(size, 6 * size),
                terms(size, 6 * size),
                terms(2 * size, 6 * lanes),
                terms(6 * lanes, 2 * size),
            ],
        ),
        out_shape=(
            f32(steps, size, 2 * size),
            f32(steps, cols, size),
            f32(size, size),
            f32(cols, size),
            f32(lanes, half_cols + size),
        ),
        compiler_params=pltpu.CompilerParams(vmem_limit_bytes=vmem_bytes),
    )(side, gathered, gathered, gathered, gathered, gathered, rhs_half, rhs_half)

    across = [(t, (t + half) % blocks) for t in range(blocks)]
    received = lax.ppermute(sent, "tm", across)
    received_other = lax.ppermute(received[:, :half_cols], "row", swap)

    middle, middle_right, target, target_right = pl.pallas_call(
        middle_kernel,
        out_shape=(f32(size, 2 * size), f32(cols, size), f32(size, size), f32(cols, size)),
        grid=(1,),
        in_specs=[smem, pl.BlockSpec(edge_block, lambda i: (0, 0, 0, 0))] + [vmem] * 4,
        out_specs=(vmem,) * 4,
        scratch_shapes=[
            scratch(cols, 2 * size),
            terms(size, 6 * size),
            terms(size, 6 * size),
            terms(2 * size, 6 * lanes),
            terms(6 * lanes, 2 * size),
        ],
        compiler_params=pltpu.CompilerParams(vmem_limit_bytes=vmem_bytes),
    )(side, gathered, edge_mine, edge_other, reduced, reduced_right)

    solution = pl.pallas_call(
        final_kernel,
        out_shape=f32(size, cols),
        in_specs=[smem] + [vmem] * 8,
        out_specs=vmem,
        scratch_shapes=[
            scratch(size, size),
            scratch(cols, size),
            scratch(cols, size),
            scratch(cols, size),
            terms(size, 6 * lanes),
            terms(6 * lanes, size),
        ],
        compiler_params=pltpu.CompilerParams(vmem_limit_bytes=vmem_bytes),
    )(side, target, target_right, received, received_other, middle, middle_right, chain, chain_right)
    return solution[None]


def solution(mesh):
    placed = (P("tm", "row", None), P("tm", "row"), P("tm", None, "row"))
    return jax.shard_map(
        local, mesh=mesh, in_specs=placed, out_specs=P("tm", None, "row"), check_vma=False
    )
```

```python
import functools

import jax
import jax.numpy as jnp
from jax import lax
from jax.experimental import pallas as pl
from jax.experimental.pallas import tpu as pltpu
from jax.sharding import PartitionSpec as P

lanes = 128
group = 8
vmem_bytes = 58 * 1024 * 1024
bf16 = jnp.bfloat16


def split(x):
    high = x.astype(bf16)
    rest = x - high.astype(jnp.float32)
    middle = rest.astype(bf16)
    low = (rest - middle.astype(jnp.float32)).astype(bf16)
    return high, middle, low


def left_terms(x):
    a, b, c = split(x)
    return jnp.concatenate([a, a, b, b, a, c], axis=1)


def right_terms(x, axis=0):
    a, b, c = split(x)
    return jnp.concatenate([a, b, a, b, c, a], axis=axis)


def dot(left, right, right_dim=0):
    return lax.dot_general(
        left, right, (((1,), (right_dim,)), ((), ())), preferred_element_type=jnp.float32
    )


def spread_row(block, row):
    return jnp.broadcast_to(block[row : row + 1], (group, lanes))


def spread_col(block, col):
    return jnp.broadcast_to(block[:, col : col + 1], (group, lanes))


def reciprocal(x):
    r = pl.reciprocal(x, approx=True)
    r = r * (2.0 - x * r)
    return r * (2.0 - x * r)


def total(terms):
    while len(terms) > 1:
        paired = [terms[i] + terms[i + 1] for i in range(0, len(terms) - 1, 2)]
        terms = paired + terms[len(paired) * 2 :]
    return terms[0]


def inverse_128(block, between):
    count = lanes // group
    inner = 4
    ride = 4
    slabs = [block[group * i : group * (i + 1)] for i in range(count)]
    sub_ids = lax.broadcasted_iota(jnp.int32, (group, lanes), 0)
    lane_ids = lax.broadcasted_iota(jnp.int32, (group, lanes), 1)
    late = None
    for b in range(count // inner):
        base = group * inner * b
        work = slabs[inner * b : inner * (b + 1)]
        ahead = []
        for s in range(inner):
            start = base + group * s
            more = s + 1 < inner
            top = ahead + [spread_col(work[s], start + j) for j in range(len(ahead), group)]
            riders, low = [], []
            if more:
                riders = [spread_col(work[s], start + group + j) for j in range(ride)]
                low = [spread_col(work[s + 1], start + group + j) for j in range(ride)]
            own = (lane_ids >= start) & (lane_ids < start + group)
            whole = jnp.where(own, jnp.where(lane_ids == sub_ids + start, 1.0, 0.0), work[s])
            factors = [
                None if i == s else [spread_col(work[i], start + j) for j in range(group)]
                for i in range(inner)
            ]
            for k in range(0, group, 2):
                u, v = top[k], top[k + 1]
                a, b_, c = spread_row(u, k), spread_row(u, k + 1), spread_row(v, k + 1)
                scale = reciprocal(a * c - b_ * b_)
                is_k, is_l = sub_ids == k, sub_ids == k + 1
                pair = is_k | is_l
                first = jnp.where(is_k, -c, jnp.where(is_l, b_, c * u - b_ * v))
                second = jnp.where(is_k, b_, jnp.where(is_l, -a, a * v - b_ * u))

                def pivoted(x):
                    row_k, row_l = spread_row(x, k), spread_row(x, k + 1)
                    return jnp.where(pair, 0.0, x) - scale * (first * row_k + second * row_l)

                top = [x if j <= k + 1 else pivoted(x) for j, x in enumerate(top)]
                riders = [pivoted(x) for x in riders]
                whole = pivoted(whole)
            rows = [spread_row(whole, j) for j in range(group)]
            ahead = [
                x - total([factors[s + 1][j] * spread_row(riders[n], j) for j in range(group)])
                for n, x in enumerate(low)
            ]
            for i in range(inner):
                if i != s:
                    change = total([factors[i][j] * rows[j] for j in range(group)])
                    work[i] = jnp.where(own, 0.0, work[i]) - change
            work[s] = whole
            if s == 1 and late is not None:
                late()
                late = None
            between(inner * b + s, count)
        slabs[inner * b : inner * (b + 1)] = work
        zero = jnp.zeros((group, lanes), jnp.float32)
        in_block = (lane_ids >= base) & (lane_ids < base + group * inner)
        solved = [zero] * (inner * b) + work + [zero] * (count - inner * (b + 1))
        solved = right_terms(jnp.concatenate(solved, axis=0))

        def merge(first, last, solved=solved, in_block=in_block):
            if first == last:
                return
            here = jnp.concatenate([jnp.where(in_block, x, 0.0) for x in slabs[first:last]], axis=0)
            change = dot(left_terms(here), solved)
            for i in range(first, last):
                at = group * (i - first)
                slabs[i] = jnp.where(in_block, 0.0, slabs[i]) - change[at : at + group]

        soon = min(inner * (b + 2), count)
        merge(inner * (b + 1), soon)

        def late(b=b, soon=soon, merge=merge):
            merge(0, inner * b)
            merge(soon, count)

    late()
    return jnp.concatenate(slabs, axis=0)


class Queue:
    def __init__(self):
        self.tasks = []

    def add(self, task):
        self.tasks.append(task)

    def between(self, step, count):
        for _ in range(-(-len(self.tasks) // (count - step))):
            self.tasks.pop(0)()

    def flush(self):
        while self.tasks:
            self.tasks.pop(0)()


def span(first, last):
    return slice(lanes * first, lanes * last)


class System:
    def __init__(self, top, bottom, right, terms_left, terms_right):
        self.top, self.bottom, self.right = top, bottom, right
        self.terms_left, self.terms_right = terms_left, terms_right
        self.panels = top.shape[-2] // lanes
        self.blocks = top.shape[-1] // lanes

    def at(self, rows, cols):
        if rows[0] < self.panels:
            return self.top, (span(*rows), span(*cols))
        low = self.panels
        return self.bottom, (span(rows[0] - low, rows[1] - low), span(cols[0] - low, cols[1] - low))

    def load(self, rows, cols):
        ref, where = self.at(rows, cols)
        return ref[where]

    def store(self, rows, cols, value):
        ref, where = self.at(rows, cols)
        ref[where] = value

    def prepare(self, p, q):
        self.terms_left[span(q, q + 1), :] = left_terms(self.load((p, p + 1), (q, q + 1)).T)

    def solve(self, p, cols, inverse):
        solved = dot(inverse, right_terms(self.load((p, p + 1), cols)))
        self.store((p, p + 1), cols, solved)
        self.terms_right[:, span(*cols)] = right_terms(solved)

    def update(self, rows, cols):
        change = dot(self.terms_left[span(*rows), :], self.terms_right[:, span(*cols)])
        self.store(rows, cols, self.load(rows, cols) - change)

    def forward(self, p, inverse, out):
        here = left_terms(self.right[:, span(p, p + 1)])
        out[:, span(p, p + 1)] = dot(here, inverse)
        if p + 1 < self.blocks:
            later = span(p + 1, self.blocks)
            self.right[:, later] = self.right[:, later] - dot(here, self.terms_right[:, later])

    def eliminate(self, queue, out):
        for p in range(self.panels):
            inverse = inverse_128(self.load((p, p + 1), (p, p + 1)), queue.between)
            queue.flush()
            self.store((p, p + 1), (p, p + 1), inverse)
            terms = left_terms(inverse)
            after = p + 1
            if after < self.blocks:
                self.prepare(p, after)
                self.solve(p, (after, after + 1), terms)
                self.update((after, after + 1), (after, after + 1))
            strips = []
            q = after + 1
            while q < self.blocks:
                end = min(self.blocks, q + 2 if q % 2 == 0 else q + 1)
                strips.append((q, end))
                q = end
            for strip in strips:
                for q in range(*strip):
                    queue.add(functools.partial(self.prepare, p, q))
                queue.add(functools.partial(self.solve, p, strip, terms))
            for strip in strips:
                start = after
                while start < strip[1]:
                    end = min(strip[1], start + 4)
                    if start < self.panels:
                        end = min(end, self.panels)
                    queue.add(functools.partial(self.update, (start, end), strip))
                    start = end
            queue.add(functools.partial(self.forward, p, right_terms(inverse), out))
        queue.flush()

    def back(self, known, solved_right, x):
        for p in reversed(range(self.panels)):
            here = solved_right[:, span(p, p + 1)]
            if known is not None:
                factor = self.top[span(p, p + 1), span(self.panels, self.blocks)]
                here = here - dot(known, right_terms(factor, 1), 1)
            if p + 1 < self.panels:
                later = span(p + 1, self.panels)
                factor = self.top[span(p, p + 1), later]
                here = here - dot(left_terms(x[:, later]), right_terms(factor, 1), 1)
            x[:, span(p, p + 1)] = here


def gram_tasks(queue, slabs, out, terms_left, terms_right):
    rows = out.shape[0] // len(slabs)

    def load(s):
        value = slabs[s]()
        terms_left[rows * s : rows * (s + 1), :] = left_terms(value)
        terms_right[rows * s : rows * (s + 1), :] = right_terms(value, 1)

    def multiply(s):
        here = slice(rows * s, rows * (s + 1))
        out[here, :] = dot(terms_left[here, :], terms_right[...], 1)

    for s in range(len(slabs)):
        queue.add(functools.partial(load, s))
    for s in range(len(slabs)):
        queue.add(functools.partial(multiply, s))


def slabs_of(edge):
    rows = edge.shape[2] - group
    return [lambda s=s: edge[0, s, :rows, :] for s in range(edge.shape[1])]


def add_mass(table, mass, rows):
    for s in range(mass.shape[1]):
        here = slice(rows * s, rows * (s + 1))
        ids = (rows, rows)
        diag = lax.broadcasted_iota(jnp.int32, ids, 0) == lax.broadcasted_iota(jnp.int32, ids, 1)
        table[here, here] = table[here, here] + jnp.where(diag, mass[0, s, :1, :rows], 0.0)


def add_rhs(right, rhs, first):
    for q in range(rhs.shape[1] // lanes):
        right[:, span(first + q, first + q + 1)] = rhs[0, span(q, q + 1), :].T


def packed_pieces(size):
    panels = size // lanes
    order = [[p for p in range(panels) if p % 4 in (0, 3)], [p for p in range(panels) if p % 4 in (1, 2)]]
    return [[(p, p, panels) for p in rows] for rows in order]


def chain_kernel(
    side, start_edge, first_edge, next_edge, first_mass, next_mass, first_rhs, next_rhs,
    solved, solved_right, reduced, reduced_right, sent,
    edge, right_rows, edge_left, edge_right, terms_left, terms_right,
):
    size = reduced.shape[0]
    quarter = start_edge.shape[2] - group
    step, steps = pl.program_id(0), pl.num_programs(0)

    @pl.when(step == 0)
    def _():
        queue = Queue()
        gram_tasks(queue, slabs_of(start_edge), edge, edge_left, edge_right)
        queue.flush()
        reduced[...] = jnp.where(side[0] == 0, edge[...], 0.0)
        add_mass(reduced, first_mass, quarter)
        gram_tasks(queue, slabs_of(first_edge), edge, edge_left, edge_right)
        queue.flush()
        add_rhs(reduced_right, first_rhs, 0)

    top = solved.at[0]
    top[:, :size] = reduced[...] + edge[...]
    top[:, size:] = -edge[...]
    reduced[...] = edge[...]
    add_mass(reduced, next_mass, quarter)
    right_rows[:, :size] = reduced_right[...]
    add_rhs(right_rows, next_rhs, size // lanes)

    queue = Queue()
    gram_tasks(queue, slabs_of(next_edge), edge, edge_left, edge_right)
    system = System(top, reduced, right_rows, terms_left, terms_right)
    system.eliminate(queue, solved_right.at[0])
    reduced_right[...] = right_rows[:, size:]

    for part, pieces in enumerate(packed_pieces(size)):

        @pl.when((step == steps - 1) & (side[2] == part))
        def _():
            at = 0
            for p, first, last in pieces:
                width = lanes * (last - first)
                sent[:, at : at + width] = reduced[span(p, p + 1), span(first, last)]
                at += width
            sent[:, at:] = reduced_right[...]


def middle_kernel(
    side, own_edge, mine, other, reduced, reduced_right,
    solved, solved_right, target, target_right,
    right_rows, edge_left, edge_right, terms_left, terms_right,
):
    size = reduced.shape[0]
    quarter = own_edge.shape[2] - group
    per_part = mine.shape[0]

    def slab(s):
        sent = jnp.where(
            side[2] == s // per_part, mine[s % per_part, :quarter], other[s % per_part, :quarter]
        )
        return jnp.where(side[0] == 0, sent, own_edge[0, s, :quarter])

    queue = Queue()
    slabs = [functools.partial(slab, s) for s in range(own_edge.shape[1])]
    gram_tasks(queue, slabs, target, edge_left, edge_right)
    queue.flush()
    solved[:, :size] = reduced[...] + target[...]
    solved[:, size:] = -target[...]
    right_rows[:, :size] = reduced_right[...]
    right_rows[:, size:] = jnp.zeros_like(target_right)
    system = System(solved, target, right_rows, terms_left, terms_right)
    system.eliminate(queue, solved_right)
    target_right[...] = right_rows[:, size:]


def final_kernel(
    side, target, target_right, mine, other, middle, middle_right, chain, chain_right, out,
    top, right_rows, ended, x, terms_left, terms_right,
):
    size = target.shape[0]
    steps = chain.shape[0]
    place = side[1]
    half_cols = other.shape[1]
    for part, pieces in enumerate(packed_pieces(size)):
        at = 0
        for p, first, last in pieces:
            cols = slice(at, at + lanes * (last - first))
            received = jnp.where(side[2] == part, mine[:, cols], other[:, cols])
            here = (span(p, p + 1), span(first, last))
            top[here] = target[here] + received
            at = cols.stop
    right_rows[...] = target_right[...] + mine[:, half_cols:]
    system = System(top, None, right_rows, terms_left, terms_right)
    system.eliminate(Queue(), ended)
    system.back(None, ended, x)
    known = left_terms(x[...])
    System(middle, None, None, None, None).back(known, middle_right, x)

    def give():
        for q in range(size // lanes):
            out[span(q, q + 1), :] = x[:, span(q, q + 1)].T

    @pl.when(place == steps)
    def _():
        give()

    def walk(n, _):
        i = steps - 1 - n
        known = left_terms(x[...])
        System(chain.at[i], None, None, None, None).back(known, chain_right.at[i], x)

        @pl.when(place == i)
        def _():
            give()

        return 0

    lax.fori_loop(0, steps, walk, 0)


def local(edge_factor, mass, rhs):
    _, quarter, size = edge_factor.shape
    cols = rhs.shape[2]
    blocks, parts = lax.axis_size("tm"), lax.axis_size("row")
    half = blocks // 2
    steps = half - 1
    mine = lax.axis_index("tm")
    right = (mine >= half).astype(jnp.int32)
    place = jnp.where(right == 0, mine, blocks - 1 - mine)
    parity = lax.axis_index("row") % 2
    side = jnp.stack([right, place, parity, mine % half]).astype(jnp.int32)

    halves = [[part * half + i for i in range(half)] for part in range(2)]
    halves_all = [[t * parts + r for t in ids for r in range(parts)] for ids in halves]
    swap = [(r, r ^ 1) for r in range(parts)]
    mass_rows = jnp.pad(mass, ((0, group - 1), (0, size - quarter)))
    packed = jnp.concatenate([edge_factor[0], mass_rows], axis=0)
    gathered = lax.all_gather(packed, ("tm", "row"), axis_index_groups=halves_all)
    gathered = gathered.reshape(half, parts, quarter + group, size)
    rhs_slots = [rhs[0]] + [
        lax.ppermute(rhs[0], "tm", [(t, t ^ d) for t in range(blocks)]) for d in range(1, half)
    ]
    rhs_half = jnp.stack(rhs_slots)
    share = parts // 2
    down = [(t + half, t) for t in range(half)]
    edge_mine = lax.ppermute(
        lax.dynamic_slice_in_dim(gathered[0], parity * share, share), "tm", down
    )
    edge_other = lax.ppermute(edge_mine, "row", swap)

    vmem = pl.BlockSpec(memory_space=pltpu.VMEM)
    smem = pl.BlockSpec(memory_space=pltpu.SMEM)
    f32 = lambda *shape: jax.ShapeDtypeStruct(shape, jnp.float32)
    scratch = lambda *shape: pltpu.VMEM(shape, jnp.float32)
    terms = lambda *shape: pltpu.VMEM(shape, bf16)
    half_cols = sum(lanes * (b - a) for _, a, b in packed_pieces(size)[0])

    def edge_at(i, s):
        return jnp.where(s[0] == 0, i + 1, steps - i)

    def block_at(i, s):
        return jnp.where(s[0] == 0, i, steps - i)

    edge_block = (1, parts, quarter + group, size)
    mass_block = (1, parts, group, size)
    rhs_block = (1, size, cols)
    last = steps - 1
    chain, chain_right, reduced, reduced_right, sent = pl.pallas_call(
        chain_kernel,
        grid_spec=pltpu.PrefetchScalarGridSpec(
            num_scalar_prefetch=1,
            grid=(steps,),
            in_specs=[
                pl.BlockSpec(edge_block, lambda i, s: (0, 0, 0, 0)),
                pl.BlockSpec(edge_block, lambda i, s: (edge_at(0, s), 0, 0, 0)),
                pl.BlockSpec(edge_block, lambda i, s: (edge_at(jnp.minimum(i + 1, last), s), 0, 0, 0)),
                pl.BlockSpec(mass_block, lambda i, s: (block_at(0, s), 0, quarter // group, 0)),
                pl.BlockSpec(mass_block, lambda i, s: (block_at(i + 1, s), 0, quarter // group, 0)),
                pl.BlockSpec(rhs_block, lambda i, s: (block_at(0, s) ^ s[3], 0, 0)),
                pl.BlockSpec(rhs_block, lambda i, s: (block_at(i + 1, s) ^ s[3], 0, 0)),
            ],
            out_specs=(
                pl.BlockSpec((1, size, 2 * size), lambda i, s: (i, 0, 0)),
                pl.BlockSpec((1, cols, size), lambda i, s: (i, 0, 0)),
                pl.BlockSpec((size, size), lambda i, s: (0, 0)),
                pl.BlockSpec((cols, size), lambda i, s: (0, 0)),
                pl.BlockSpec((lanes, half_cols + size), lambda i, s: (0, 0)),
            ),
            scratch_shapes=[
                scratch(size, size),
                scratch(cols, 2 * size),
                terms(size, 6 * size),
                terms(size, 6 * size),
                terms(2 * size, 6 * lanes),
                terms(6 * lanes, 2 * size),
            ],
        ),
        out_shape=(
            f32(steps, size, 2 * size),
            f32(steps, cols, size),
            f32(size, size),
            f32(cols, size),
            f32(lanes, half_cols + size),
        ),
        compiler_params=pltpu.CompilerParams(vmem_limit_bytes=vmem_bytes),
    )(side, gathered, gathered, gathered, gathered, gathered, rhs_half, rhs_half)

    across = [(t, (t + half) % blocks) for t in range(blocks)]
    received = lax.ppermute(sent, "tm", across)
    middle, middle_right, target, target_right = pl.pallas_call(
        middle_kernel,
        out_shape=(f32(size, 2 * size), f32(cols, size), f32(size, size), f32(cols, size)),
        grid=(1,),
        in_specs=[smem, pl.BlockSpec(edge_block, lambda i: (0, 0, 0, 0))] + [vmem] * 4,
        out_specs=(vmem,) * 4,
        scratch_shapes=[
            scratch(cols, 2 * size),
            terms(size, 6 * size),
            terms(size, 6 * size),
            terms(2 * size, 6 * lanes),
            terms(6 * lanes, 2 * size),
        ],
        compiler_params=pltpu.CompilerParams(vmem_limit_bytes=vmem_bytes),
    )(side, gathered, edge_mine, edge_other, reduced, reduced_right)

    received, target = lax.optimization_barrier((received, target))
    received_other = lax.ppermute(received[:, :half_cols], "row", swap)
    solution = pl.pallas_call(
        final_kernel,
        out_shape=f32(size, cols),
        in_specs=[smem] + [vmem] * 8,
        out_specs=vmem,
        scratch_shapes=[
            scratch(size, size),
            scratch(cols, size),
            scratch(cols, size),
            scratch(cols, size),
            terms(size, 6 * lanes),
            terms(6 * lanes, size),
        ],
        compiler_params=pltpu.CompilerParams(vmem_limit_bytes=vmem_bytes),
    )(side, target, target_right, received, received_other, middle, middle_right, chain, chain_right)
    return solution[None]


def solution(mesh):
    placed = (P("tm", "row", None), P("tm", "row"), P("tm", None, "row"))
    return jax.shard_map(
        local, mesh=mesh, in_specs=placed, out_specs=P("tm", None, "row"), check_vma=False
    )
```

```python
import functools

import jax
import jax.numpy as jnp
from jax import lax
from jax.experimental import pallas as pl
from jax.experimental.pallas import tpu as pltpu
from jax.sharding import PartitionSpec as P

lanes = 128
group = 8
vmem_bytes = 58 * 1024 * 1024
bf16 = jnp.bfloat16


def split(x):
    high = x.astype(bf16)
    rest = x - high.astype(jnp.float32)
    middle = rest.astype(bf16)
    low = (rest - middle.astype(jnp.float32)).astype(bf16)
    return high, middle, low


def left_terms(x):
    a, b, c = split(x)
    return jnp.concatenate([a, a, b, b, a, c], axis=1)


def right_terms(x, axis=0):
    a, b, c = split(x)
    return jnp.concatenate([a, b, a, b, c, a], axis=axis)


def store_split(ref, rows, cols, x):
    for n, part in enumerate(split(x)):
        ref[n, rows, cols] = part


def load_left(ref, rows, cols):
    a, b, c = (ref[n, rows, cols] for n in range(3))
    return jnp.concatenate([a, a, b, b, a, c], axis=1)


def load_right(ref, rows, cols, axis=0):
    a, b, c = (ref[n, rows, cols] for n in range(3))
    return jnp.concatenate([a, b, a, b, c, a], axis=axis)


whole = slice(None)


def dot(left, right, right_dim=0):
    return lax.dot_general(
        left, right, (((1,), (right_dim,)), ((), ())), preferred_element_type=jnp.float32
    )


def spread_row(block, row):
    return jnp.broadcast_to(block[row : row + 1], (group, lanes))


def spread_col(block, col):
    return jnp.broadcast_to(block[:, col : col + 1], (group, lanes))


def reciprocal(x):
    r = pl.reciprocal(x, approx=True)
    r = r * (2.0 - x * r)
    return r * (2.0 - x * r)


def total(terms):
    while len(terms) > 1:
        paired = [terms[i] + terms[i + 1] for i in range(0, len(terms) - 1, 2)]
        terms = paired + terms[len(paired) * 2 :]
    return terms[0]


def inverse_128(block):
    count = lanes // group
    inner = 4
    ride = 4
    slabs = [block[group * i : group * (i + 1)] for i in range(count)]
    sub_ids = lax.broadcasted_iota(jnp.int32, (group, lanes), 0)
    lane_ids = lax.broadcasted_iota(jnp.int32, (group, lanes), 1)
    late = None
    for b in range(count // inner):
        base = group * inner * b
        work = slabs[inner * b : inner * (b + 1)]
        ahead = []
        for s in range(inner):
            start = base + group * s
            more = s + 1 < inner
            top = ahead + [spread_col(work[s], start + j) for j in range(len(ahead), group)]
            riders, low = [], []
            if more:
                riders = [spread_col(work[s], start + group + j) for j in range(ride)]
                low = [spread_col(work[s + 1], start + group + j) for j in range(ride)]
            own = (lane_ids >= start) & (lane_ids < start + group)
            wide = jnp.where(own, jnp.where(lane_ids == sub_ids + start, 1.0, 0.0), work[s])
            factors = [
                None if i == s else [spread_col(work[i], start + j) for j in range(group)]
                for i in range(inner)
            ]
            for k in range(0, group, 2):
                u, v = top[k], top[k + 1]
                a, b_, c = spread_row(u, k), spread_row(u, k + 1), spread_row(v, k + 1)
                scale = reciprocal(a * c - b_ * b_)
                is_k, is_l = sub_ids == k, sub_ids == k + 1
                pair = is_k | is_l
                first = jnp.where(is_k, -c, jnp.where(is_l, b_, c * u - b_ * v))
                second = jnp.where(is_k, b_, jnp.where(is_l, -a, a * v - b_ * u))

                def pivoted(x):
                    row_k, row_l = spread_row(x, k), spread_row(x, k + 1)
                    return jnp.where(pair, 0.0, x) - scale * (first * row_k + second * row_l)

                top = [x if j <= k + 1 else pivoted(x) for j, x in enumerate(top)]
                riders = [pivoted(x) for x in riders]
                wide = pivoted(wide)
                yield
            rows = [spread_row(wide, j) for j in range(group)]
            ahead = [
                x - total([factors[s + 1][j] * spread_row(riders[n], j) for j in range(group)])
                for n, x in enumerate(low)
            ]
            for i in range(inner):
                if i != s:
                    change = total([factors[i][j] * rows[j] for j in range(group)])
                    work[i] = jnp.where(own, 0.0, work[i]) - change
            work[s] = wide
            if s == 1 and late is not None:
                late()
                late = None
            yield
        slabs[inner * b : inner * (b + 1)] = work
        zero = jnp.zeros((group, lanes), jnp.float32)
        in_block = (lane_ids >= base) & (lane_ids < base + group * inner)
        solved = [zero] * (inner * b) + work + [zero] * (count - inner * (b + 1))
        solved = right_terms(jnp.concatenate(solved, axis=0))

        def merge(first, last, solved=solved, in_block=in_block):
            if first == last:
                return
            here = jnp.concatenate([jnp.where(in_block, x, 0.0) for x in slabs[first:last]], axis=0)
            change = dot(left_terms(here), solved)
            for i in range(first, last):
                at = group * (i - first)
                slabs[i] = jnp.where(in_block, 0.0, slabs[i]) - change[at : at + group]

        soon = min(inner * (b + 2), count)
        merge(inner * (b + 1), soon)

        def late(b=b, soon=soon, merge=merge):
            merge(0, inner * b)
            merge(soon, count)

    late()
    return jnp.concatenate(slabs, axis=0)


inverse_yields = 80


class Queue:
    def __init__(self):
        self.tasks = []

    def add(self, task):
        self.tasks.append(task)

    def between(self, left, keep=0):
        for _ in range(-(-(len(self.tasks) - keep) // max(left, 1))):
            if self.tasks:
                self.tasks.pop(0)()

    def flush(self, keep=0):
        while len(self.tasks) > keep:
            self.tasks.pop(0)()


def inverses(blocks, queue, keep):
    runs = [inverse_128(block) for block in blocks]
    results = [None] * len(runs)
    left = inverse_yields // 5
    count = 0
    while any(result is None for result in results):
        for n, run in enumerate(runs):
            try:
                next(run)
            except StopIteration as stop:
                results[n] = stop.value
        count += 1
        if count % 5 == 0:
            queue.between(left, keep)
            left -= 1
    queue.flush(keep)
    return results


def span(first, last):
    return slice(lanes * first, lanes * last)


class System:
    def __init__(self, top, bottom, right, out, terms_left, terms_right):
        self.top, self.bottom, self.right, self.out = top, bottom, right, out
        self.terms_left, self.terms_right = terms_left, terms_right
        self.panels = top.shape[-2] // lanes
        self.blocks = top.shape[-1] // lanes

    def at(self, rows, cols):
        if rows[0] < self.panels:
            return self.top, (span(*rows), span(*cols))
        low = self.panels
        return self.bottom, (span(rows[0] - low, rows[1] - low), span(cols[0] - low, cols[1] - low))

    def load(self, rows, cols):
        ref, where = self.at(rows, cols)
        return ref[where]

    def store(self, rows, cols, value):
        ref, where = self.at(rows, cols)
        ref[where] = value

    def prepare(self, p, q):
        store_split(self.terms_left, span(q, q + 1), whole, self.load((p, p + 1), (q, q + 1)).T)

    def solve(self, p, cols, inverse):
        solved = dot(inverse, right_terms(self.load((p, p + 1), cols)))
        self.store((p, p + 1), cols, solved)
        store_split(self.terms_right, whole, span(*cols), solved)

    def update(self, rows, cols):
        change = dot(
            load_left(self.terms_left, span(*rows), whole),
            load_right(self.terms_right, whole, span(*cols)),
        )
        self.store(rows, cols, self.load(rows, cols) - change)

    def forward(self, p, inverse):
        here = left_terms(self.right[:, span(p, p + 1)])
        self.out[:, span(p, p + 1)] = dot(here, inverse)
        if p + 1 < self.blocks:
            later = span(p + 1, self.blocks)
            change = dot(here, load_right(self.terms_right, whole, later))
            self.right[:, later] = self.right[:, later] - change

    def diagonal(self, p):
        return self.load((p, p + 1), (p, p + 1))

    def next_pivot(self, p, inverse):
        self.store((p, p + 1), (p, p + 1), inverse)
        after = p + 1
        if after < self.blocks:
            self.prepare(p, after)
            self.solve(p, (after, after + 1), left_terms(inverse))
            self.update((after, after + 1), (after, after + 1))

    def background(self, p, inverse, queue):
        terms = left_terms(inverse)
        after = p + 1
        strips = []
        q = after + 1
        while q < self.blocks:
            end = min(self.blocks, q + 2 if q % 2 == 0 else q + 1)
            strips.append((q, end))
            q = end
        for strip in strips:
            for q in range(*strip):
                queue.add(functools.partial(self.prepare, p, q))
            queue.add(functools.partial(self.solve, p, strip, terms))
        for strip in strips:
            start = after
            while start < strip[1]:
                end = min(strip[1], start + 4)
                if start < self.panels:
                    end = min(end, self.panels)
                queue.add(functools.partial(self.update, (start, end), strip))
                start = end
        queue.add(functools.partial(self.forward, p, right_terms(inverse)))

    def back(self, known, x):
        for p in reversed(range(self.panels)):
            here = self.out[:, span(p, p + 1)]
            for n, terms in enumerate(known):
                low = self.panels * (n + 1)
                factor = self.top[span(p, p + 1), span(low, low + self.panels)]
                here = here - dot(terms, right_terms(factor, 1), 1)
            if p + 1 < self.panels:
                later = span(p + 1, self.panels)
                factor = self.top[span(p, p + 1), later]
                here = here - dot(left_terms(x[:, later]), right_terms(factor, 1), 1)
            x[:, span(p, p + 1)] = here


def eliminate(systems, queue, keep_first=0):
    for p in range(systems[0].panels):
        keep = keep_first if p == 0 else 0
        found = inverses([system.diagonal(p) for system in systems], queue, keep)
        for system, inverse in zip(systems, found):
            system.next_pivot(p, inverse)
        for system, inverse in zip(systems, found):
            system.background(p, inverse, queue)
    queue.flush()


def load_factor(slab, terms, s):
    value = slab(s)
    store_split(terms, slice(value.shape[0] * s, value.shape[0] * (s + 1)), whole, value)


def gram_rows(terms, rows):
    return dot(load_left(terms, rows, whole), load_right(terms, whole, whole, 1), 1)


def gram_tasks(queue, slab, parts, out, terms):
    rows = out.shape[0] // parts

    def multiply(s):
        here = slice(rows * s, rows * (s + 1))
        out[here, :] = gram_rows(terms, here)

    for s in range(parts):
        queue.add(functools.partial(load_factor, slab, terms, s))
    for s in range(parts):
        queue.add(functools.partial(multiply, s))


def slab_of(edge, block=0):
    rows = edge.shape[2] - group
    return lambda s: edge[block, s, :rows, :]


def on_diagonal(mass, rows):
    ids = (rows, rows)
    diag = lax.broadcasted_iota(jnp.int32, ids, 0) == lax.broadcasted_iota(jnp.int32, ids, 1)
    return jnp.where(diag, mass, 0.0)


def add_mass(table, mass, rows):
    for s in range(mass.shape[1]):
        here = slice(rows * s, rows * (s + 1))
        table[here, here] = table[here, here] + on_diagonal(mass[0, s, :1, :rows], rows)


def add_rhs(right, rhs, first, block=0):
    for q in range(rhs.shape[1] // lanes):
        right[:, span(first + q, first + q + 1)] = rhs[block, span(q, q + 1), :].T


def pack_sent(side, sent, reduced, reduced_right, ready):
    for part, pieces in enumerate(packed_pieces(reduced.shape[0])):

        @pl.when(ready & (side[2] == part))
        def _():
            at = 0
            for p, first, last in pieces:
                width = lanes * (last - first)
                sent[:, at : at + width] = reduced[span(p, p + 1), span(first, last)]
                at += width
            sent[:, at:] = reduced_right[...]


def packed_pieces(size):
    panels = size // lanes
    order = [[p for p in range(panels) if p % 4 in (0, 3)], [p for p in range(panels) if p % 4 in (1, 2)]]
    return [[(p, p, panels) for p in rows] for rows in order]


def chain_kernel(
    side, start_edge, first_edge, next_edge, first_mass, next_mass, first_rhs, next_rhs,
    solved, solved_right, reduced, reduced_right, sent,
    edge, right_rows, edge_terms, terms_left, terms_right,
):
    size = reduced.shape[0]
    parts = start_edge.shape[1]
    quarter = start_edge.shape[2] - group
    step, steps = pl.program_id(0), pl.num_programs(0)

    @pl.when(step == 0)
    def _():
        queue = Queue()
        gram_tasks(queue, slab_of(start_edge), parts, edge, edge_terms)
        queue.flush()
        reduced[...] = jnp.where(side[0] == 0, edge[...], 0.0)
        add_mass(reduced, first_mass, quarter)
        gram_tasks(queue, slab_of(first_edge), parts, edge, edge_terms)
        queue.flush()
        add_rhs(reduced_right, first_rhs, 0)

    top = solved.at[0]
    top[:, :size] = reduced[...] + edge[...]
    top[:, size:] = -edge[...]
    reduced[...] = edge[...]
    add_mass(reduced, next_mass, quarter)
    right_rows[:, :size] = reduced_right[...]
    add_rhs(right_rows, next_rhs, size // lanes)

    queue = Queue()
    gram_tasks(queue, slab_of(next_edge), parts, edge, edge_terms)
    system = System(top, reduced, right_rows, solved_right.at[0], terms_left, terms_right)
    eliminate([system], queue)
    reduced_right[...] = right_rows[:, size:]
    pack_sent(side, sent, reduced, reduced_right, step == steps - 1)


def pair_kernel(
    side, gathered, rhs,
    first_hbm, third_hbm, second_hbm, first_right, third_right, second_right,
    reduced, reduced_right, sent,
    first_top, third_top, rest, rights, *scratch,
):
    edge_terms, terms, sems = scratch[:4], scratch[4:8], scratch[8]
    size = reduced.shape[0]
    parts = gathered.shape[1]
    quarter = gathered.shape[2] - group
    steps = gathered.shape[0] - 1
    own, after = slice(0, size), slice(size, 2 * size)
    edges = [jnp.where(side[0] == 0, i + 1, steps - i) for i in range(steps)]
    blocks = [jnp.where(side[0] == 0, i, steps - i) for i in range(steps + 1)]

    def strip(n, s):
        here = slice(quarter * s, quarter * (s + 1))
        low = slice(size + here.start, size + here.stop)
        gram = gram_rows(edge_terms[n], here)

        def with_mass(ref, rows, cols, i):
            mass = gathered[blocks[i], s, quarter : quarter + 1, :quarter]
            ref[rows, cols] = ref[rows, cols] + on_diagonal(mass, quarter)

        if n == 0:
            first_top[here, own] = jnp.where(side[0] == 0, gram, 0.0)
            with_mass(first_top, here, here, 0)
        elif n == 1:
            first_top[here, own] = first_top[here, own] + gram
            first_top[here, after] = -gram
            rest[here, own] = gram
            with_mass(rest, here, here, 1)
        elif n == 2:
            rest[here, own] = rest[here, own] + gram
            third_top[here, own] = gram
            third_top[here, after] = -gram
            with_mass(third_top, here, here, 2)
        else:
            third_top[here, own] = third_top[here, own] + gram
            third_top[here, 2 * size :] = -gram
            rest[here, after] = jnp.zeros((quarter, size), jnp.float32)
            rest[low, after] = gram
            with_mass(rest, low, low, 3)

    for n in range(4):
        for s in range(parts):
            load_factor(slab_of(gathered, 0 if n == 0 else edges[n - 1]), edge_terms[n], s)
        strip(n, 0)
    rights[0, :, 2 * size :] = jnp.zeros_like(reduced_right)
    rights[0, :, after] = jnp.zeros_like(reduced_right)
    for n, first, i in ((0, 0, 0), (1, 0, 2), (1, 1, 1), (1, 2, 3)):
        add_rhs(rights.at[n], rhs, first * (size // lanes), blocks[i] ^ side[3])

    queue = Queue()
    for s in range(1, parts):
        for n in range(4):
            queue.add(functools.partial(strip, n, s))
    first = System(
        first_top, rest.at[own, own], rights.at[0, :, : 2 * size], first_right, terms[0], terms[1]
    )
    third = System(third_top, rest, rights.at[1], third_right, terms[2], terms[3])
    eliminate([first, third], queue, 4 * (parts - 2))
    leaving = [
        pltpu.make_async_copy(first_top, first_hbm, sems.at[0]),
        pltpu.make_async_copy(third_top, third_hbm, sems.at[1]),
    ]
    for copy in leaving:
        copy.start()
    rights[1, :, after] = rights[1, :, after] + rights[0, :, after]
    second = System(
        rest.at[own, :], rest.at[after, after], rights.at[1, :, size:], second_right, terms[0], terms[1]
    )
    eliminate([second], Queue())
    leaving.append(pltpu.make_async_copy(rest.at[own, :], second_hbm, sems.at[2]))
    leaving[-1].start()
    reduced[...] = rest[after, after]
    reduced_right[...] = rights[1, :, 2 * size :]
    pack_sent(side, sent, reduced, reduced_right, True)
    for copy in leaving:
        copy.wait()


def middle_kernel(
    side, own_edge, mine, other, reduced, reduced_right,
    solved, solved_right, target, target_right,
    right_rows, edge_terms, terms_left, terms_right,
):
    size = reduced.shape[0]
    parts = own_edge.shape[1]
    quarter = own_edge.shape[2] - group
    per_part = mine.shape[0]

    def slab(s):
        sent = jnp.where(
            side[2] == s // per_part, mine[s % per_part, :quarter], other[s % per_part, :quarter]
        )
        return jnp.where(side[0] == 0, sent, own_edge[0, s, :quarter])

    queue = Queue()
    gram_tasks(queue, slab, parts, target, edge_terms)
    queue.flush()
    solved[:, :size] = reduced[...] + target[...]
    solved[:, size:] = -target[...]
    right_rows[:, :size] = reduced_right[...]
    right_rows[:, size:] = jnp.zeros_like(target_right)
    eliminate([System(solved, target, right_rows, solved_right, terms_left, terms_right)], Queue())
    target_right[...] = right_rows[:, size:]


def final_kernel(
    side, target, target_right, mine, other, middle, middle_right, *refs
):
    stored, (out, top, right_rows, ended, x, terms_left, terms_right) = refs[:-7], refs[-7:]
    size = target.shape[0]
    place = side[1]
    half_cols = other.shape[1]
    for part, pieces in enumerate(packed_pieces(size)):
        at = 0
        for p, first, last in pieces:
            cols = slice(at, at + lanes * (last - first))
            received = jnp.where(side[2] == part, mine[:, cols], other[:, cols])
            here = (span(p, p + 1), span(first, last))
            top[here] = target[here] + received
            at = cols.stop
    right_rows[...] = target_right[...] + mine[:, half_cols:]
    eliminate([System(top, None, right_rows, ended, terms_left, terms_right)], Queue())

    def give(i):
        @pl.when(place == i)
        def _():
            for q in range(size // lanes):
                out[span(q, q + 1), :] = x[:, span(q, q + 1)].T

    def back(top, right, known):
        System(top, None, None, right, None, None).back(known, x)
        return left_terms(x[...])

    known = back(top, ended, [])
    known = back(middle, middle_right, [known])
    if len(stored) == 2:
        chain, chain_right = stored
        steps = chain.shape[0]
        give(steps)

        def walk(n, _):
            i = steps - 1 - n
            back(chain.at[i], chain_right.at[i], [left_terms(x[...])])
            give(i)
            return 0

        lax.fori_loop(0, steps, walk, 0)
    else:
        first, third, second, first_right, third_right, second_right = stored
        give(3)
        near = back(second, second_right, [known])
        give(1)

        @pl.when(place == 0)
        def _():
            back(first, first_right, [near])
            give(0)

        @pl.when(place == 2)
        def _():
            back(third, third_right, [near, known])
            give(2)


def local(edge_factor, mass, rhs):
    _, quarter, size = edge_factor.shape
    cols = rhs.shape[2]
    blocks, parts = lax.axis_size("tm"), lax.axis_size("row")
    half = blocks // 2
    steps = half - 1
    mine = lax.axis_index("tm")
    right = (mine >= half).astype(jnp.int32)
    place = jnp.where(right == 0, mine, blocks - 1 - mine)
    parity = lax.axis_index("row") % 2
    side = jnp.stack([right, place, parity, mine % half]).astype(jnp.int32)

    halves = [[part * half + i for i in range(half)] for part in range(2)]
    halves_all = [[t * parts + r for t in ids for r in range(parts)] for ids in halves]
    swap = [(r, r ^ 1) for r in range(parts)]
    mass_rows = jnp.pad(mass, ((0, group - 1), (0, size - quarter)))
    packed = jnp.concatenate([edge_factor[0], mass_rows], axis=0)
    gathered = lax.all_gather(packed, ("tm", "row"), axis_index_groups=halves_all)
    gathered = gathered.reshape(half, parts, quarter + group, size)
    rhs_slots = [rhs[0]] + [
        lax.ppermute(rhs[0], "tm", [(t, t ^ d) for t in range(blocks)]) for d in range(1, half)
    ]
    rhs_half = jnp.stack(rhs_slots)
    share = parts // 2
    gathered, rhs_half = lax.optimization_barrier((gathered, rhs_half))
    down = [(t + half, t) for t in range(half)]
    edge_mine = lax.ppermute(
        lax.dynamic_slice_in_dim(gathered[0], parity * share, share), "tm", down
    )
    edge_other = lax.ppermute(edge_mine, "row", swap)

    vmem = pl.BlockSpec(memory_space=pltpu.VMEM)
    smem = pl.BlockSpec(memory_space=pltpu.SMEM)
    f32 = lambda *shape: jax.ShapeDtypeStruct(shape, jnp.float32)
    scratch = lambda *shape: pltpu.VMEM(shape, jnp.float32)
    terms = lambda *shape: pltpu.VMEM(shape, bf16)
    half_cols = sum(lanes * (b - a) for _, a, b in packed_pieces(size)[0])

    def edge_at(i, s):
        return jnp.where(s[0] == 0, i + 1, steps - i)

    def block_at(i, s):
        return jnp.where(s[0] == 0, i, steps - i)

    edge_block = (1, parts, quarter + group, size)
    mass_block = (1, parts, group, size)
    rhs_block = (1, size, cols)
    last = steps - 1
    if steps == 3:
        *stored, reduced, reduced_right, sent = pl.pallas_call(
            pair_kernel,
            in_specs=[smem, vmem, vmem],
            out_specs=(pl.BlockSpec(memory_space=pl.ANY),) * 3 + (vmem,) * 6,
            out_shape=(
                f32(size, 2 * size),
                f32(size, 3 * size),
                f32(size, 2 * size),
                f32(cols, size),
                f32(cols, size),
                f32(cols, size),
                f32(size, size),
                f32(cols, size),
                f32(lanes, half_cols + size),
            ),
            scratch_shapes=[
                scratch(size, 2 * size),
                scratch(size, 3 * size),
                scratch(2 * size, 2 * size),
                scratch(2, cols, 3 * size),
            ]
            + [terms(3, size, size)] * 4
            + [terms(3, 2 * size, lanes), terms(3, lanes, 2 * size)]
            + [terms(3, 3 * size, lanes), terms(3, lanes, 3 * size)]
            + [pltpu.SemaphoreType.DMA((3,))],
            compiler_params=pltpu.CompilerParams(vmem_limit_bytes=vmem_bytes),
        )(side, gathered, rhs_half)
    else:
        *stored, reduced, reduced_right, sent = pl.pallas_call(
            chain_kernel,
            grid_spec=pltpu.PrefetchScalarGridSpec(
                num_scalar_prefetch=1,
                grid=(steps,),
                in_specs=[
                    pl.BlockSpec(edge_block, lambda i, s: (0, 0, 0, 0)),
                    pl.BlockSpec(edge_block, lambda i, s: (edge_at(0, s), 0, 0, 0)),
                    pl.BlockSpec(edge_block, lambda i, s: (edge_at(jnp.minimum(i + 1, last), s), 0, 0, 0)),
                    pl.BlockSpec(mass_block, lambda i, s: (block_at(0, s), 0, quarter // group, 0)),
                    pl.BlockSpec(mass_block, lambda i, s: (block_at(i + 1, s), 0, quarter // group, 0)),
                    pl.BlockSpec(rhs_block, lambda i, s: (block_at(0, s) ^ s[3], 0, 0)),
                    pl.BlockSpec(rhs_block, lambda i, s: (block_at(i + 1, s) ^ s[3], 0, 0)),
                ],
                out_specs=(
                    pl.BlockSpec((1, size, 2 * size), lambda i, s: (i, 0, 0)),
                    pl.BlockSpec((1, cols, size), lambda i, s: (i, 0, 0)),
                    pl.BlockSpec((size, size), lambda i, s: (0, 0)),
                    pl.BlockSpec((cols, size), lambda i, s: (0, 0)),
                    pl.BlockSpec((lanes, half_cols + size), lambda i, s: (0, 0)),
                ),
                scratch_shapes=[
                    scratch(size, size),
                    scratch(cols, 2 * size),
                    terms(3, size, size),
                    terms(3, 2 * size, lanes),
                    terms(3, lanes, 2 * size),
                ],
            ),
            out_shape=(
                f32(steps, size, 2 * size),
                f32(steps, cols, size),
                f32(size, size),
                f32(cols, size),
                f32(lanes, half_cols + size),
            ),
            compiler_params=pltpu.CompilerParams(vmem_limit_bytes=vmem_bytes),
        )(side, gathered, gathered, gathered, gathered, gathered, rhs_half, rhs_half)

    across = [(t, (t + half) % blocks) for t in range(blocks)]
    received = lax.ppermute(sent, "tm", across)
    middle, middle_right, target, target_right = pl.pallas_call(
        middle_kernel,
        out_shape=(f32(size, 2 * size), f32(cols, size), f32(size, size), f32(cols, size)),
        grid=(1,),
        in_specs=[smem, pl.BlockSpec(edge_block, lambda i: (0, 0, 0, 0))] + [vmem] * 4,
        out_specs=(vmem,) * 4,
        scratch_shapes=[
            scratch(cols, 2 * size),
            terms(3, size, size),
            terms(3, 2 * size, lanes),
            terms(3, lanes, 2 * size),
        ],
        compiler_params=pltpu.CompilerParams(vmem_limit_bytes=vmem_bytes),
    )(side, gathered, edge_mine, edge_other, reduced, reduced_right)

    received, target = lax.optimization_barrier((received, target))
    received_other = lax.ppermute(received[:, :half_cols], "row", swap)
    solution = pl.pallas_call(
        final_kernel,
        out_shape=f32(size, cols),
        in_specs=[smem] + [vmem] * (6 + len(stored)),
        out_specs=vmem,
        scratch_shapes=[
            scratch(size, size),
            scratch(cols, size),
            scratch(cols, size),
            scratch(cols, size),
            terms(3, size, lanes),
            terms(3, lanes, size),
        ],
        compiler_params=pltpu.CompilerParams(vmem_limit_bytes=vmem_bytes),
    )(side, target, target_right, received, received_other, middle, middle_right, *stored)
    return solution[None]


def solution(mesh):
    placed = (P("tm", "row", None), P("tm", "row"), P("tm", None, "row"))
    return jax.shard_map(
        local, mesh=mesh, in_specs=placed, out_specs=P("tm", None, "row"), check_vma=False
    )
```

```python
import functools

import jax
import jax.numpy as jnp
from jax import lax
from jax.experimental import pallas as pl
from jax.experimental.pallas import tpu as pltpu
from jax.sharding import PartitionSpec as P

lanes = 128
group = 8
vmem_bytes = 58 * 1024 * 1024
bf16 = jnp.bfloat16


def split(x):
    high = x.astype(bf16)
    rest = x - high.astype(jnp.float32)
    middle = rest.astype(bf16)
    low = (rest - middle.astype(jnp.float32)).astype(bf16)
    return high, middle, low


def left_terms(x):
    a, b, c = split(x)
    return jnp.concatenate([a, a, b, b, a, c], axis=1)


def right_terms(x, axis=0):
    a, b, c = split(x)
    return jnp.concatenate([a, b, a, b, c, a], axis=axis)


def store_split(ref, rows, cols, x):
    for n, part in enumerate(split(x)):
        ref[n, rows, cols] = part


def load_left(ref, rows, cols):
    a, b, c = (ref[n, rows, cols] for n in range(3))
    return jnp.concatenate([a, a, b, b, a, c], axis=1)


def load_right(ref, rows, cols, axis=0):
    a, b, c = (ref[n, rows, cols] for n in range(3))
    return jnp.concatenate([a, b, a, b, c, a], axis=axis)


whole = slice(None)


def dot(left, right, right_dim=0):
    return lax.dot_general(
        left, right, (((1,), (right_dim,)), ((), ())), preferred_element_type=jnp.float32
    )


def spread_row(block, row):
    return jnp.broadcast_to(block[row : row + 1], (group, lanes))


def spread_col(block, col):
    return jnp.broadcast_to(block[:, col : col + 1], (group, lanes))


def total(terms):
    while len(terms) > 1:
        paired = [terms[i] + terms[i + 1] for i in range(0, len(terms) - 1, 2)]
        terms = paired + terms[len(paired) * 2 :]
    return terms[0]


def inverse_128(block):
    count = lanes // group
    inner = 4
    ride = 4
    slabs = [block[group * i : group * (i + 1)] for i in range(count)]
    sub_ids = lax.broadcasted_iota(jnp.int32, (group, lanes), 0)
    lane_ids = lax.broadcasted_iota(jnp.int32, (group, lanes), 1)
    late = None
    for b in range(count // inner):
        base = group * inner * b
        work = slabs[inner * b : inner * (b + 1)]
        ahead = []
        for s in range(inner):
            start = base + group * s
            more = s + 1 < inner
            top = ahead + [spread_col(work[s], start + j) for j in range(len(ahead), group)]
            riders, low = [], []
            if more:
                riders = [spread_col(work[s], start + group + j) for j in range(ride)]
                low = [spread_col(work[s + 1], start + group + j) for j in range(ride)]
            own = (lane_ids >= start) & (lane_ids < start + group)
            wide = jnp.where(own, jnp.where(lane_ids == sub_ids + start, 1.0, 0.0), work[s])
            factors = [
                None if i == s else [spread_col(work[i], start + j) for j in range(group)]
                for i in range(inner)
            ]
            for k in range(0, group, 2):
                u, v = top[k], top[k + 1]
                a, b_, c = spread_row(u, k), spread_row(u, k + 1), spread_row(v, k + 1)
                scale = pl.reciprocal(a * c - b_ * b_, approx=True)
                is_k, is_l = sub_ids == k, sub_ids == k + 1
                pair = is_k | is_l
                first = jnp.where(is_k, -c, jnp.where(is_l, b_, c * u - b_ * v))
                second = jnp.where(is_k, b_, jnp.where(is_l, -a, a * v - b_ * u))

                def pivoted(x):
                    row_k, row_l = spread_row(x, k), spread_row(x, k + 1)
                    return jnp.where(pair, 0.0, x) - scale * (first * row_k + second * row_l)

                top = [x if j <= k + 1 else pivoted(x) for j, x in enumerate(top)]
                riders = [pivoted(x) for x in riders]
                wide = pivoted(wide)
                yield
            rows = [spread_row(wide, j) for j in range(group)]
            ahead = [
                x - total([factors[s + 1][j] * spread_row(riders[n], j) for j in range(group)])
                for n, x in enumerate(low)
            ]
            for i in range(inner):
                if i != s:
                    change = total([factors[i][j] * rows[j] for j in range(group)])
                    work[i] = jnp.where(own, 0.0, work[i]) - change
            work[s] = wide
            if s == 1 and late is not None:
                late()
                late = None
            yield
        slabs[inner * b : inner * (b + 1)] = work
        zero = jnp.zeros((group, lanes), jnp.float32)
        in_block = (lane_ids >= base) & (lane_ids < base + group * inner)
        solved = [zero] * (inner * b) + work + [zero] * (count - inner * (b + 1))
        solved = right_terms(jnp.concatenate(solved, axis=0))

        def merge(first, last, solved=solved, in_block=in_block):
            if first == last:
                return
            here = jnp.concatenate([jnp.where(in_block, x, 0.0) for x in slabs[first:last]], axis=0)
            change = dot(left_terms(here), solved)
            for i in range(first, last):
                at = group * (i - first)
                slabs[i] = jnp.where(in_block, 0.0, slabs[i]) - change[at : at + group]

        soon = min(inner * (b + 2), count)
        merge(inner * (b + 1), soon)

        def late(b=b, soon=soon, merge=merge):
            merge(0, inner * b)
            merge(soon, count)

    late()
    return jnp.concatenate(slabs, axis=0)


inverse_yields = 80


class Queue:
    def __init__(self):
        self.tasks = []

    def add(self, task):
        self.tasks.append(task)

    def between(self, left, keep=0):
        for _ in range(-(-(len(self.tasks) - keep) // max(left, 1))):
            if self.tasks:
                self.tasks.pop(0)()

    def flush(self, keep=0):
        while len(self.tasks) > keep:
            self.tasks.pop(0)()


def inverses(blocks, queue, keep):
    runs = [inverse_128(block) for block in blocks]
    results = [None] * len(runs)
    left = inverse_yields // 5
    count = 0
    while any(result is None for result in results):
        for n, run in enumerate(runs):
            try:
                next(run)
            except StopIteration as stop:
                results[n] = stop.value
        count += 1
        if count % 5 == 0:
            queue.between(left, keep)
            left -= 1
    queue.flush(keep)
    return results


def span(first, last):
    return slice(lanes * first, lanes * last)


class System:
    def __init__(self, top, bottom, right, out, terms_left, terms_right):
        self.top, self.bottom, self.right, self.out = top, bottom, right, out
        self.terms_left, self.terms_right = terms_left, terms_right
        self.panels = top.shape[-2] // lanes
        self.blocks = top.shape[-1] // lanes

    def at(self, rows, cols):
        if rows[0] < self.panels:
            return self.top, (span(*rows), span(*cols))
        low = self.panels
        return self.bottom, (span(rows[0] - low, rows[1] - low), span(cols[0] - low, cols[1] - low))

    def load(self, rows, cols):
        ref, where = self.at(rows, cols)
        return ref[where]

    def store(self, rows, cols, value):
        ref, where = self.at(rows, cols)
        ref[where] = value

    def prepare(self, p, q):
        store_split(self.terms_left, span(q, q + 1), whole, self.load((p, p + 1), (q, q + 1)).T)

    def solve(self, p, cols, inverse):
        solved = dot(inverse, right_terms(self.load((p, p + 1), cols)))
        self.store((p, p + 1), cols, solved)
        store_split(self.terms_right, whole, span(*cols), solved)

    def update(self, rows, cols):
        change = dot(
            load_left(self.terms_left, span(*rows), whole),
            load_right(self.terms_right, whole, span(*cols)),
        )
        self.store(rows, cols, self.load(rows, cols) - change)

    def forward(self, p, inverse):
        here = left_terms(self.right[:, span(p, p + 1)])
        self.out[:, span(p, p + 1)] = dot(here, inverse)
        if p + 1 < self.blocks:
            later = span(p + 1, self.blocks)
            change = dot(here, load_right(self.terms_right, whole, later))
            self.right[:, later] = self.right[:, later] - change

    def diagonal(self, p):
        return self.load((p, p + 1), (p, p + 1))

    def ready(self, p):
        if p + 1 < self.blocks:
            self.prepare(p, p + 1)
            block = self.load((p, p + 1), (p + 1, p + 2))
            store_split(self.terms_right, whole, span(p + 1, p + 2), block)

    def next_pivot(self, p, inverse):
        after = (p + 1, p + 2)
        if p + 1 < self.blocks:
            solved = dot(left_terms(inverse), load_right(self.terms_right, whole, span(*after)))
            terms = right_terms(solved)
            change = dot(load_left(self.terms_left, span(*after), whole), terms)
            self.store(after, after, self.load(after, after) - change)
            self.store((p, p + 1), after, solved)
            store_split(self.terms_right, whole, span(*after), solved)
        self.store((p, p + 1), (p, p + 1), inverse)

    def background(self, p, inverse, queue):
        terms = left_terms(inverse)
        after = p + 1
        strips = []
        q = after + 1
        while q < self.blocks:
            end = min(self.blocks, q + 2 if q % 2 == 0 else q + 1)
            strips.append((q, end))
            q = end
        for strip in strips:
            for q in range(*strip):
                queue.add(functools.partial(self.prepare, p, q))
            queue.add(functools.partial(self.solve, p, strip, terms))
        for strip in strips:
            start = after
            while start < strip[1]:
                end = min(strip[1], start + 4)
                if start < self.panels:
                    end = min(end, self.panels)
                queue.add(functools.partial(self.update, (start, end), strip))
                start = end
        queue.add(functools.partial(self.forward, p, right_terms(inverse)))

    def back(self, known, x):
        for p in reversed(range(self.panels)):
            here = self.out[:, span(p, p + 1)]
            for n, terms in enumerate(known):
                low = self.panels * (n + 1)
                factor = self.top[span(p, p + 1), span(low, low + self.panels)]
                here = here - dot(terms, right_terms(factor, 1), 1)
            if p + 1 < self.panels:
                later = span(p + 1, self.panels)
                factor = self.top[span(p, p + 1), later]
                here = here - dot(left_terms(x[:, later]), right_terms(factor, 1), 1)
            x[:, span(p, p + 1)] = here


def eliminate(systems, queue, keep_first=0, fresh=True):
    for p in range(systems[0].panels):
        keep = keep_first if p == 0 else 0
        for system in systems:
            if p == 0 and fresh:
                system.ready(p)
            else:
                queue.add(functools.partial(system.ready, p))
        found = inverses([system.diagonal(p) for system in systems], queue, keep)
        for system, inverse in zip(systems, found):
            system.next_pivot(p, inverse)
        for system, inverse in zip(systems, found):
            system.background(p, inverse, queue)


def load_factor(slab, terms, s):
    value = slab(s)
    store_split(terms, slice(value.shape[0] * s, value.shape[0] * (s + 1)), whole, value)


def gram_rows(terms, rows):
    return dot(load_left(terms, rows, whole), load_right(terms, whole, whole, 1), 1)


def gram_tasks(queue, slab, parts, out, terms):
    rows = out.shape[0] // parts

    def multiply(s):
        here = slice(rows * s, rows * (s + 1))
        out[here, :] = gram_rows(terms, here)

    for s in range(parts):
        queue.add(functools.partial(load_factor, slab, terms, s))
    for s in range(parts):
        queue.add(functools.partial(multiply, s))


def slab_of(edge, block=0):
    rows = edge.shape[2] - group
    return lambda s: edge[block, s, :rows, :]


def on_diagonal(mass, rows):
    ids = (rows, rows)
    diag = lax.broadcasted_iota(jnp.int32, ids, 0) == lax.broadcasted_iota(jnp.int32, ids, 1)
    return jnp.where(diag, mass, 0.0)


def add_mass(table, mass, rows):
    for s in range(mass.shape[1]):
        here = slice(rows * s, rows * (s + 1))
        table[here, here] = table[here, here] + on_diagonal(mass[0, s, :1, :rows], rows)


def add_rhs(right, rhs, first, block=0):
    for q in range(rhs.shape[1] // lanes):
        right[:, span(first + q, first + q + 1)] = rhs[block, span(q, q + 1), :].T


def pack_sent(side, sent, reduced, reduced_right, ready):
    for part, pieces in enumerate(packed_pieces(reduced.shape[0])):

        @pl.when(ready & (side[2] == part))
        def _():
            at = 0
            for p, first, last in pieces:
                width = lanes * (last - first)
                sent[:, at : at + width] = reduced[span(p, p + 1), span(first, last)]
                at += width
            sent[:, at:] = reduced_right[...]


def packed_pieces(size):
    panels = size // lanes
    order = [[p for p in range(panels) if p % 4 in (0, 3)], [p for p in range(panels) if p % 4 in (1, 2)]]
    return [[(p, p, panels) for p in rows] for rows in order]


def chain_kernel(
    side, start_edge, first_edge, next_edge, first_mass, next_mass, first_rhs, next_rhs,
    solved, solved_right, reduced, reduced_right, sent,
    edge, right_rows, edge_terms, terms_left, terms_right,
):
    size = reduced.shape[0]
    parts = start_edge.shape[1]
    quarter = start_edge.shape[2] - group
    step, steps = pl.program_id(0), pl.num_programs(0)

    @pl.when(step == 0)
    def _():
        queue = Queue()
        gram_tasks(queue, slab_of(start_edge), parts, edge, edge_terms)
        queue.flush()
        reduced[...] = jnp.where(side[0] == 0, edge[...], 0.0)
        add_mass(reduced, first_mass, quarter)
        gram_tasks(queue, slab_of(first_edge), parts, edge, edge_terms)
        queue.flush()
        add_rhs(reduced_right, first_rhs, 0)

    top = solved.at[0]
    top[:, :size] = reduced[...] + edge[...]
    top[:, size:] = -edge[...]
    reduced[...] = edge[...]
    add_mass(reduced, next_mass, quarter)
    right_rows[:, :size] = reduced_right[...]
    add_rhs(right_rows, next_rhs, size // lanes)

    queue = Queue()
    gram_tasks(queue, slab_of(next_edge), parts, edge, edge_terms)
    system = System(top, reduced, right_rows, solved_right.at[0], terms_left, terms_right)
    eliminate([system], queue)
    queue.flush()
    reduced_right[...] = right_rows[:, size:]
    pack_sent(side, sent, reduced, reduced_right, step == steps - 1)


def pair_kernel(
    side, gathered, rhs,
    first_hbm, third_hbm, second_hbm, first_right, third_right, second_right,
    reduced, reduced_right, sent,
    first_top, third_top, rest, rights, *scratch,
):
    edge_terms, terms, sems = scratch[:4], scratch[4:8], scratch[8]
    size = reduced.shape[0]
    parts = gathered.shape[1]
    quarter = gathered.shape[2] - group
    steps = gathered.shape[0] - 1
    own, after = slice(0, size), slice(size, 2 * size)
    edges = [jnp.where(side[0] == 0, i + 1, steps - i) for i in range(steps)]
    blocks = [jnp.where(side[0] == 0, i, steps - i) for i in range(steps + 1)]

    def strip(n, s):
        here = slice(quarter * s, quarter * (s + 1))
        low = slice(size + here.start, size + here.stop)
        gram = gram_rows(edge_terms[n], here)

        def with_mass(ref, rows, cols, i):
            mass = gathered[blocks[i], s, quarter : quarter + 1, :quarter]
            ref[rows, cols] = ref[rows, cols] + on_diagonal(mass, quarter)

        if n == 0:
            first_top[here, own] = jnp.where(side[0] == 0, gram, 0.0)
            with_mass(first_top, here, here, 0)
        elif n == 1:
            first_top[here, own] = first_top[here, own] + gram
            first_top[here, after] = -gram
            rest[here, own] = gram
            with_mass(rest, here, here, 1)
        elif n == 2:
            rest[here, own] = rest[here, own] + gram
            third_top[here, own] = gram
            third_top[here, after] = -gram
            with_mass(third_top, here, here, 2)
        else:
            third_top[here, own] = third_top[here, own] + gram
            third_top[here, 2 * size :] = -gram
            rest[here, after] = jnp.zeros((quarter, size), jnp.float32)
            rest[low, after] = gram
            with_mass(rest, low, low, 3)

    for n in range(4):
        for s in range(parts):
            load_factor(slab_of(gathered, 0 if n == 0 else edges[n - 1]), edge_terms[n], s)
        strip(n, 0)
    rights[0, :, 2 * size :] = jnp.zeros_like(reduced_right)
    rights[0, :, after] = jnp.zeros_like(reduced_right)
    for n, first, i in ((0, 0, 0), (1, 0, 2), (1, 1, 1), (1, 2, 3)):
        add_rhs(rights.at[n], rhs, first * (size // lanes), blocks[i] ^ side[3])

    queue = Queue()
    for s in range(1, parts):
        for n in range(4):
            queue.add(functools.partial(strip, n, s))
    first = System(
        first_top, rest.at[own, own], rights.at[0, :, : 2 * size], first_right, terms[0], terms[1]
    )
    third = System(third_top, rest, rights.at[1], third_right, terms[2], terms[3])
    eliminate([first, third], queue, 4 * (parts - 2))

    def hand_over():
        rights[1, :, after] = rights[1, :, after] + rights[0, :, after]

    leaving = [
        pltpu.make_async_copy(first_top, first_hbm, sems.at[0]),
        pltpu.make_async_copy(third_top, third_hbm, sems.at[1]),
        pltpu.make_async_copy(rest.at[own, :], second_hbm, sems.at[2]),
    ]
    queue.add(hand_over)
    queue.add(leaving[0].start)
    queue.add(leaving[1].start)
    second = System(
        rest.at[own, :], rest.at[after, after], rights.at[1, :, size:], second_right, terms[0], terms[1]
    )
    eliminate([second], queue, 0, False)
    queue.flush()
    leaving[2].start()
    reduced[...] = rest[after, after]
    reduced_right[...] = rights[1, :, 2 * size :]
    pack_sent(side, sent, reduced, reduced_right, True)
    for copy in leaving:
        copy.wait()


def middle_kernel(
    side, own_edge, sent_edge, reduced, reduced_right,
    solved, solved_right, target, target_right,
    right_rows, edge_terms, terms_left, terms_right,
):
    size = reduced.shape[0]
    parts = own_edge.shape[1]
    quarter = own_edge.shape[2] - group
    own, sent = slab_of(own_edge), slab_of(sent_edge)

    def strip(s):
        here = slice(quarter * s, quarter * (s + 1))
        gram = gram_rows(edge_terms, here)
        solved[here, :size] = reduced[here, :] + gram
        solved[here, size:] = -gram
        target[here, :] = gram

    for s in range(parts):
        load_factor(lambda s: jnp.where(side[0] == 0, sent(s), own(s)), edge_terms, s)
    strip(0)
    right_rows[:, :size] = reduced_right[...]
    right_rows[:, size:] = jnp.zeros_like(target_right)
    queue = Queue()
    for s in range(1, parts):
        queue.add(functools.partial(strip, s))
    system = System(solved, target, right_rows, solved_right, terms_left, terms_right)
    eliminate([system], queue, parts - 2)
    queue.flush()
    target_right[...] = right_rows[:, size:]


def receive(side, top, right_rows, target, target_right, mine, other):
    half_cols = other.shape[1]
    for part, pieces in enumerate(packed_pieces(target.shape[0])):
        at = 0
        for p, first, last in pieces:
            cols = slice(at, at + lanes * (last - first))
            received = jnp.where(side[2] == part, mine[:, cols], other[:, cols])
            here = (span(p, p + 1), span(first, last))
            top[here] = target[here] + received
            at = cols.stop
    right_rows[...] = target_right[...] + mine[:, half_cols:]


def hand_out(out, x):
    for q in range(out.shape[0] // lanes):
        out[span(q, q + 1), :] = x[:, span(q, q + 1)].T


def pair_final_kernel(
    side, target, target_right, mine, other, middle_right, first_right, third_right, second_right,
    middle_hbm, first_hbm, third_hbm, second_hbm,
    out, top, right_rows, ended, x, terms_left, terms_right,
    middle, first, third, second, sems, top_terms, middle_terms, second_terms, last_terms,
):
    size = target.shape[0]
    panels = size // lanes
    place = side[1]
    pairs = ((middle_hbm, middle), (first_hbm, first), (third_hbm, third), (second_hbm, second))
    coming = [pltpu.make_async_copy(a, b, sems.at[n]) for n, (a, b) in enumerate(pairs)]
    for copy in coming:
        copy.start()
    receive(side, top, right_rows, target, target_right, mine, other)
    system = System(top, None, right_rows, ended, terms_left, terms_right)
    queue = Queue()
    for copy in coming:
        queue.add(copy.wait)

    def split_rows(ref, terms, p, cols):
        store_split(terms, span(p, p + 1), cols, ref[span(p, p + 1), cols])

    def split_last(p, cols):
        here = span(p, p + 1)
        value = third[here, cols]
        if cols.start < 2 * size:
            value = jnp.where(place == 2, value, first[here, cols])
        else:
            value = jnp.where(place == 2, value, 0.0)
        store_split(last_terms, here, cols, value)

    for p in range(panels):
        later = slice(lanes * (p + 1), 2 * size)
        queue.add(functools.partial(split_rows, middle, middle_terms, p, later))
        queue.add(functools.partial(split_rows, second, second_terms, p, later))
        queue.add(functools.partial(split_last, p, later))
        queue.add(functools.partial(split_last, p, slice(2 * size, 3 * size)))
    eliminate([system], queue)
    queue.flush()
    for p in range(panels - 1):
        split_rows(top, top_terms, p, slice(lanes * (p + 1), size))

    def back(right, terms, known):
        here = right
        for n, value in enumerate(known):
            low = size * (n + 1)
            here = here - dot(value, load_right(terms, whole, slice(low, low + size), 1), 1)
        for p in reversed(range(panels)):
            at = slice(lanes * p, lanes * (p + 1))
            x[:, at] = here[:, at]
            if p > 0:
                above = slice(0, lanes * p)
                change = dot(left_terms(here[:, at]), load_right(terms, above, at, 1), 1)
                here = here[:, above] - change
        return left_terms(x[...])

    def give(i):
        @pl.when(place == i)
        def _():
            hand_out(out, x)

    far = back(ended[...], top_terms, [])
    near = back(middle_right[...], middle_terms, [far])
    give(3)
    last = back(second_right[...], second_terms, [near])
    give(1)

    @pl.when(place % 2 == 0)
    def _():
        right = jnp.where(place == 2, third_right[...], first_right[...])
        back(right, last_terms, [last, near])
        hand_out(out, x)


def final_kernel(
    side, target, target_right, mine, other, middle, middle_right, chain, chain_right,
    out, top, right_rows, ended, x, terms_left, terms_right,
):
    place = side[1]
    steps = chain.shape[0]
    receive(side, top, right_rows, target, target_right, mine, other)
    queue = Queue()
    eliminate([System(top, None, right_rows, ended, terms_left, terms_right)], queue)
    queue.flush()

    def back(top, right, known):
        System(top, None, None, right, None, None).back(known, x)
        return left_terms(x[...])

    def give(i):
        @pl.when(place == i)
        def _():
            hand_out(out, x)

    known = back(top, ended, [])
    back(middle, middle_right, [known])
    give(steps)

    def walk(n, _):
        i = steps - 1 - n
        back(chain.at[i], chain_right.at[i], [left_terms(x[...])])
        give(i)
        return 0

    lax.fori_loop(0, steps, walk, 0)


def local(edge_factor, mass, rhs):
    _, quarter, size = edge_factor.shape
    cols = rhs.shape[2]
    blocks, parts = lax.axis_size("tm"), lax.axis_size("row")
    half = blocks // 2
    steps = half - 1
    mine = lax.axis_index("tm")
    right = (mine >= half).astype(jnp.int32)
    place = jnp.where(right == 0, mine, blocks - 1 - mine)
    parity = lax.axis_index("row") % 2
    side = jnp.stack([right, place, parity, mine % half]).astype(jnp.int32)

    halves = [[part * half + i for i in range(half)] for part in range(2)]
    halves_all = [[t * parts + r for t in ids for r in range(parts)] for ids in halves]
    swap = [(r, r ^ 1) for r in range(parts)]
    mass_rows = jnp.pad(mass, ((0, group - 1), (0, size - quarter)))
    packed = jnp.concatenate([edge_factor[0], mass_rows], axis=0)
    gathered = lax.all_gather(packed, ("tm", "row"), axis_index_groups=halves_all)
    gathered = gathered.reshape(half, parts, quarter + group, size)
    rhs_slots = [rhs[0]] + [
        lax.ppermute(rhs[0], "tm", [(t, t ^ d) for t in range(blocks)]) for d in range(1, half)
    ]
    rhs_half = jnp.stack(rhs_slots)
    gathered, rhs_half = lax.optimization_barrier((gathered, rhs_half))
    down = [(t + half, t) for t in range(half)]
    sent_edge = lax.ppermute(gathered[:1], "tm", down)

    vmem = pl.BlockSpec(memory_space=pltpu.VMEM)
    smem = pl.BlockSpec(memory_space=pltpu.SMEM)
    f32 = lambda *shape: jax.ShapeDtypeStruct(shape, jnp.float32)
    scratch = lambda *shape: pltpu.VMEM(shape, jnp.float32)
    terms = lambda *shape: pltpu.VMEM(shape, bf16)
    half_cols = sum(lanes * (b - a) for _, a, b in packed_pieces(size)[0])

    def edge_at(i, s):
        return jnp.where(s[0] == 0, i + 1, steps - i)

    def block_at(i, s):
        return jnp.where(s[0] == 0, i, steps - i)

    edge_block = (1, parts, quarter + group, size)
    mass_block = (1, parts, group, size)
    rhs_block = (1, size, cols)
    last = steps - 1
    if steps == 3:
        *stored, reduced, reduced_right, sent = pl.pallas_call(
            pair_kernel,
            in_specs=[smem, vmem, vmem],
            out_specs=(pl.BlockSpec(memory_space=pl.ANY),) * 3 + (vmem,) * 6,
            out_shape=(
                f32(size, 2 * size),
                f32(size, 3 * size),
                f32(size, 2 * size),
                f32(cols, size),
                f32(cols, size),
                f32(cols, size),
                f32(size, size),
                f32(cols, size),
                f32(lanes, half_cols + size),
            ),
            scratch_shapes=[
                scratch(size, 2 * size),
                scratch(size, 3 * size),
                scratch(2 * size, 2 * size),
                scratch(2, cols, 3 * size),
            ]
            + [terms(3, size, size)] * 4
            + [terms(3, 2 * size, lanes), terms(3, lanes, 2 * size)]
            + [terms(3, 3 * size, lanes), terms(3, lanes, 3 * size)]
            + [pltpu.SemaphoreType.DMA((3,))],
            compiler_params=pltpu.CompilerParams(vmem_limit_bytes=vmem_bytes),
        )(side, gathered, rhs_half)
    else:
        *stored, reduced, reduced_right, sent = pl.pallas_call(
            chain_kernel,
            grid_spec=pltpu.PrefetchScalarGridSpec(
                num_scalar_prefetch=1,
                grid=(steps,),
                in_specs=[
                    pl.BlockSpec(edge_block, lambda i, s: (0, 0, 0, 0)),
                    pl.BlockSpec(edge_block, lambda i, s: (edge_at(0, s), 0, 0, 0)),
                    pl.BlockSpec(edge_block, lambda i, s: (edge_at(jnp.minimum(i + 1, last), s), 0, 0, 0)),
                    pl.BlockSpec(mass_block, lambda i, s: (block_at(0, s), 0, quarter // group, 0)),
                    pl.BlockSpec(mass_block, lambda i, s: (block_at(i + 1, s), 0, quarter // group, 0)),
                    pl.BlockSpec(rhs_block, lambda i, s: (block_at(0, s) ^ s[3], 0, 0)),
                    pl.BlockSpec(rhs_block, lambda i, s: (block_at(i + 1, s) ^ s[3], 0, 0)),
                ],
                out_specs=(
                    pl.BlockSpec((1, size, 2 * size), lambda i, s: (i, 0, 0)),
                    pl.BlockSpec((1, cols, size), lambda i, s: (i, 0, 0)),
                    pl.BlockSpec((size, size), lambda i, s: (0, 0)),
                    pl.BlockSpec((cols, size), lambda i, s: (0, 0)),
                    pl.BlockSpec((lanes, half_cols + size), lambda i, s: (0, 0)),
                ),
                scratch_shapes=[
                    scratch(size, size),
                    scratch(cols, 2 * size),
                    terms(3, size, size),
                    terms(3, 2 * size, lanes),
                    terms(3, lanes, 2 * size),
                ],
            ),
            out_shape=(
                f32(steps, size, 2 * size),
                f32(steps, cols, size),
                f32(size, size),
                f32(cols, size),
                f32(lanes, half_cols + size),
            ),
            compiler_params=pltpu.CompilerParams(vmem_limit_bytes=vmem_bytes),
        )(side, gathered, gathered, gathered, gathered, gathered, rhs_half, rhs_half)

    across = [(t, (t + half) % blocks) for t in range(blocks)]
    received = lax.ppermute(sent, "tm", across)
    middle, middle_right, target, target_right = pl.pallas_call(
        middle_kernel,
        out_shape=(f32(size, 2 * size), f32(cols, size), f32(size, size), f32(cols, size)),
        grid=(1,),
        in_specs=[smem, pl.BlockSpec(edge_block, lambda i: (0, 0, 0, 0))] + [vmem] * 3,
        out_specs=(vmem,) * 4,
        scratch_shapes=[
            scratch(cols, 2 * size),
            terms(3, size, size),
            terms(3, 2 * size, lanes),
            terms(3, lanes, 2 * size),
        ],
        compiler_params=pltpu.CompilerParams(vmem_limit_bytes=vmem_bytes),
    )(side, gathered, sent_edge, reduced, reduced_right)

    received, target = lax.optimization_barrier((received, target))
    received_other = lax.ppermute(received[:, :half_cols], "row", swap)
    final_scratch = [
        scratch(size, size),
        scratch(cols, size),
        scratch(cols, size),
        scratch(cols, size),
        terms(3, size, lanes),
        terms(3, lanes, size),
    ]
    arrived = (target, target_right, received, received_other)
    if steps == 3:
        first, third, second, first_right, third_right, second_right = stored
        solution = pl.pallas_call(
            pair_final_kernel,
            out_shape=f32(size, cols),
            in_specs=[smem] + [vmem] * 8 + [pl.BlockSpec(memory_space=pl.ANY)] * 4,
            out_specs=vmem,
            scratch_shapes=final_scratch
            + [scratch(size, 2 * size), scratch(size, 2 * size)]
            + [scratch(size, 3 * size), scratch(size, 2 * size)]
            + [pltpu.SemaphoreType.DMA((4,))]
            + [terms(3, size, size), terms(3, size, 2 * size)]
            + [terms(3, size, 2 * size), terms(3, size, 3 * size)],
            compiler_params=pltpu.CompilerParams(vmem_limit_bytes=vmem_bytes),
        )(
            side, *arrived, middle_right, first_right, third_right, second_right,
            middle, first, third, second,
        )
    else:
        solution = pl.pallas_call(
            final_kernel,
            out_shape=f32(size, cols),
            in_specs=[smem] + [vmem] * 8,
            out_specs=vmem,
            scratch_shapes=final_scratch,
            compiler_params=pltpu.CompilerParams(vmem_limit_bytes=vmem_bytes),
        )(side, *arrived, middle, middle_right, *stored)
    return solution[None]


def solution(mesh):
    placed = (P("tm", "row", None), P("tm", "row"), P("tm", None, "row"))
    return jax.shard_map(
        local, mesh=mesh, in_specs=placed, out_specs=P("tm", None, "row"), check_vma=False
    )
```

```python
import functools

import jax
import jax.numpy as jnp
from jax import lax
from jax.experimental import pallas as pl
from jax.experimental.pallas import tpu as pltpu
from jax.sharding import PartitionSpec as P

lanes = 128
group = 8
vmem_bytes = 58 * 1024 * 1024
bf16 = jnp.bfloat16


def split(x):
    high = x.astype(bf16)
    rest = x - high.astype(jnp.float32)
    middle = rest.astype(bf16)
    low = (rest - middle.astype(jnp.float32)).astype(bf16)
    return high, middle, low


def left_terms(x):
    a, b, c = split(x)
    return jnp.concatenate([a, a, b, b, a, c], axis=1)


def right_terms(x, axis=0):
    a, b, c = split(x)
    return jnp.concatenate([a, b, a, b, c, a], axis=axis)


def store_split(ref, rows, cols, x):
    for n, part in enumerate(split(x)):
        ref[n, rows, cols] = part


def load_left(ref, rows, cols):
    a, b, c = (ref[n, rows, cols] for n in range(3))
    return jnp.concatenate([a, a, b, b, a, c], axis=1)


def load_right(ref, rows, cols, axis=0):
    a, b, c = (ref[n, rows, cols] for n in range(3))
    return jnp.concatenate([a, b, a, b, c, a], axis=axis)


whole = slice(None)


def dot(left, right, right_dim=0):
    return lax.dot_general(
        left, right, (((1,), (right_dim,)), ((), ())), preferred_element_type=jnp.float32
    )


def spread_row(block, row):
    return jnp.broadcast_to(block[row : row + 1], (group, lanes))


def spread_col(block, col):
    return jnp.broadcast_to(block[:, col : col + 1], (group, lanes))


def total(terms):
    while len(terms) > 1:
        paired = [terms[i] + terms[i + 1] for i in range(0, len(terms) - 1, 2)]
        terms = paired + terms[len(paired) * 2 :]
    return terms[0]


def spread_lane(block, index):
    return jnp.take_along_axis(block, index, axis=1, mode="promise_in_bounds")


ride = 4


def eight_pivots(start, slabs, ahead, sub_ids, lane_ids):
    lane = [jnp.full((group, lanes), start + j, jnp.int32) for j in range(group)]
    next_lane = [jnp.full((group, lanes), (start + group + j) % lanes) for j in range(ride)]
    top = list(ahead) + [spread_lane(slabs[0], lane[j]) for j in range(ride, group)]
    riders = [spread_lane(slabs[0], index) for index in next_lane]
    low = [spread_lane(slabs[1], index) for index in next_lane]
    own = (lane_ids >= start) & (lane_ids < start + group)
    wide = jnp.where(own, jnp.where(lane_ids == sub_ids + start, 1.0, 0.0), slabs[0])
    for k in range(0, group, 2):
        u, v = top[k], top[k + 1]
        a, b, c = spread_row(u, k), spread_row(u, k + 1), spread_row(v, k + 1)
        scale = pl.reciprocal(a * c - b * b, approx=True)
        is_k, is_l = sub_ids == k, sub_ids == k + 1
        pair = is_k | is_l
        first = jnp.where(is_k, -c, jnp.where(is_l, b, c * u - b * v))
        second = jnp.where(is_k, b, jnp.where(is_l, -a, a * v - b * u))

        def pivoted(x):
            row_k, row_l = spread_row(x, k), spread_row(x, k + 1)
            return jnp.where(pair, 0.0, x) - scale * (first * row_k + second * row_l)

        top = [x if j <= k + 1 else pivoted(x) for j, x in enumerate(top)]
        riders = [pivoted(x) for x in riders]
        wide = pivoted(wide)
    rows = [spread_row(wide, j) for j in range(group)]
    done = []
    for i, slab in enumerate(slabs[1:]):
        factors = [spread_lane(slab, index) for index in lane]
        if i == 0:
            ahead = [
                x - total([f * spread_row(riders[n], j) for j, f in enumerate(factors)])
                for n, x in enumerate(low)
            ]
        change = total([f * row for f, row in zip(factors, rows)])
        done.append(jnp.where(own, 0.0, slab) - change)
    return done + [wide], ahead


def inverses(blocks):
    count = lanes // group
    sub_ids = lax.broadcasted_iota(jnp.int32, (group, lanes), 0)
    lane_ids = lax.broadcasted_iota(jnp.int32, (group, lanes), 1)
    carry = []
    for block in blocks:
        slabs = [block[group * i : group * (i + 1)] for i in range(count)]
        carry.append((slabs, [spread_col(slabs[0], j) for j in range(ride)]))

    def step(i, carry):
        return [eight_pivots(group * i, *state, sub_ids, lane_ids) for state in carry]

    carry = lax.fori_loop(0, count, step, carry)
    return [jnp.concatenate(slabs, axis=0) for slabs, _ in carry]


class Queue:
    def __init__(self):
        self.tasks = []

    def add(self, task):
        self.tasks.append(task)

    def flush(self, keep=0):
        while len(self.tasks) > keep:
            self.tasks.pop(0)()


def span(first, last):
    return slice(lanes * first, lanes * last)


class System:
    def __init__(self, top, bottom, right, out, terms_left, terms_right):
        self.top, self.bottom, self.right, self.out = top, bottom, right, out
        self.terms_left, self.terms_right = terms_left, terms_right
        self.panels = top.shape[-2] // lanes
        self.blocks = top.shape[-1] // lanes

    def at(self, rows, cols):
        if rows[0] < self.panels:
            return self.top, (span(*rows), span(*cols))
        low = self.panels
        return self.bottom, (span(rows[0] - low, rows[1] - low), span(cols[0] - low, cols[1] - low))

    def load(self, rows, cols):
        ref, where = self.at(rows, cols)
        return ref[where]

    def store(self, rows, cols, value):
        ref, where = self.at(rows, cols)
        ref[where] = value

    def prepare(self, p, q):
        store_split(self.terms_left, span(q, q + 1), whole, self.load((p, p + 1), (q, q + 1)).T)

    def solve(self, p, cols, inverse):
        solved = dot(inverse, right_terms(self.load((p, p + 1), cols)))
        self.store((p, p + 1), cols, solved)
        store_split(self.terms_right, whole, span(*cols), solved)

    def update(self, rows, cols):
        change = dot(
            load_left(self.terms_left, span(*rows), whole),
            load_right(self.terms_right, whole, span(*cols)),
        )
        self.store(rows, cols, self.load(rows, cols) - change)

    def forward(self, p, inverse):
        here = left_terms(self.right[:, span(p, p + 1)])
        self.out[:, span(p, p + 1)] = dot(here, inverse)
        if p + 1 < self.blocks:
            later = span(p + 1, self.blocks)
            change = dot(here, load_right(self.terms_right, whole, later))
            self.right[:, later] = self.right[:, later] - change

    def diagonal(self, p):
        return self.load((p, p + 1), (p, p + 1))

    def ready(self, p):
        if p + 1 < self.blocks:
            self.prepare(p, p + 1)
            block = self.load((p, p + 1), (p + 1, p + 2))
            store_split(self.terms_right, whole, span(p + 1, p + 2), block)

    def next_pivot(self, p, inverse):
        after = (p + 1, p + 2)
        if p + 1 < self.blocks:
            solved = dot(left_terms(inverse), load_right(self.terms_right, whole, span(*after)))
            terms = right_terms(solved)
            change = dot(load_left(self.terms_left, span(*after), whole), terms)
            self.store(after, after, self.load(after, after) - change)
            self.store((p, p + 1), after, solved)
            store_split(self.terms_right, whole, span(*after), solved)
        self.store((p, p + 1), (p, p + 1), inverse)

    def background(self, p, inverse, queue):
        terms = left_terms(inverse)
        after = p + 1
        strips = []
        q = after + 1
        while q < self.blocks:
            end = min(self.blocks, q + 2 if q % 2 == 0 else q + 1)
            strips.append((q, end))
            q = end
        for strip in strips:
            for q in range(*strip):
                queue.add(functools.partial(self.prepare, p, q))
            queue.add(functools.partial(self.solve, p, strip, terms))
        for strip in strips:
            start = after
            while start < strip[1]:
                end = min(strip[1], start + 4)
                if start < self.panels:
                    end = min(end, self.panels)
                queue.add(functools.partial(self.update, (start, end), strip))
                start = end
        queue.add(functools.partial(self.forward, p, right_terms(inverse)))

    def back(self, known, x):
        for p in reversed(range(self.panels)):
            here = self.out[:, span(p, p + 1)]
            for n, terms in enumerate(known):
                low = self.panels * (n + 1)
                factor = self.top[span(p, p + 1), span(low, low + self.panels)]
                here = here - dot(terms, right_terms(factor, 1), 1)
            if p + 1 < self.panels:
                later = span(p + 1, self.panels)
                factor = self.top[span(p, p + 1), later]
                here = here - dot(left_terms(x[:, later]), right_terms(factor, 1), 1)
            x[:, span(p, p + 1)] = here


def eliminate(systems, queue, keep_first=0, fresh=True):
    for p in range(systems[0].panels):
        keep = keep_first if p == 0 else 0
        for system in systems:
            if p == 0 and fresh:
                system.ready(p)
            else:
                queue.add(functools.partial(system.ready, p))
        found = inverses([system.diagonal(p) for system in systems])
        queue.flush(keep)
        for system, inverse in zip(systems, found):
            system.next_pivot(p, inverse)
        for system, inverse in zip(systems, found):
            system.background(p, inverse, queue)


def load_factor(slab, terms, s):
    value = slab(s)
    store_split(terms, slice(value.shape[0] * s, value.shape[0] * (s + 1)), whole, value)


def gram_rows(terms, rows):
    return dot(load_left(terms, rows, whole), load_right(terms, whole, whole, 1), 1)


def gram_tasks(queue, slab, parts, out, terms):
    rows = out.shape[0] // parts

    def multiply(s):
        here = slice(rows * s, rows * (s + 1))
        out[here, :] = gram_rows(terms, here)

    for s in range(parts):
        queue.add(functools.partial(load_factor, slab, terms, s))
    for s in range(parts):
        queue.add(functools.partial(multiply, s))


def slab_of(edge, block=0):
    rows = edge.shape[2] - group
    return lambda s: edge[block, s, :rows, :]


def on_diagonal(mass, rows):
    ids = (rows, rows)
    diag = lax.broadcasted_iota(jnp.int32, ids, 0) == lax.broadcasted_iota(jnp.int32, ids, 1)
    return jnp.where(diag, mass, 0.0)


def add_mass(table, mass, rows):
    for s in range(mass.shape[1]):
        here = slice(rows * s, rows * (s + 1))
        table[here, here] = table[here, here] + on_diagonal(mass[0, s, :1, :rows], rows)


def add_rhs(right, rhs, first, block=0):
    for q in range(rhs.shape[1] // lanes):
        right[:, span(first + q, first + q + 1)] = rhs[block, span(q, q + 1), :].T


def pack_sent(side, sent, reduced, reduced_right, ready):
    for part, pieces in enumerate(packed_pieces(reduced.shape[0])):

        @pl.when(ready & (side[2] == part))
        def _():
            at = 0
            for p, first, last in pieces:
                width = lanes * (last - first)
                sent[:, at : at + width] = reduced[span(p, p + 1), span(first, last)]
                at += width
            sent[:, at:] = reduced_right[...]


def packed_pieces(size):
    panels = size // lanes
    order = [[p for p in range(panels) if p % 4 in (0, 3)], [p for p in range(panels) if p % 4 in (1, 2)]]
    return [[(p, p, panels) for p in rows] for rows in order]


def chain_kernel(
    side, start_edge, first_edge, next_edge, first_mass, next_mass, first_rhs, next_rhs,
    solved, solved_right, reduced, reduced_right, sent,
    edge, right_rows, edge_terms, terms_left, terms_right,
):
    size = reduced.shape[0]
    parts = start_edge.shape[1]
    quarter = start_edge.shape[2] - group
    step, steps = pl.program_id(0), pl.num_programs(0)

    @pl.when(step == 0)
    def _():
        queue = Queue()
        gram_tasks(queue, slab_of(start_edge), parts, edge, edge_terms)
        queue.flush()
        reduced[...] = jnp.where(side[0] == 0, edge[...], 0.0)
        add_mass(reduced, first_mass, quarter)
        gram_tasks(queue, slab_of(first_edge), parts, edge, edge_terms)
        queue.flush()
        add_rhs(reduced_right, first_rhs, 0)

    top = solved.at[0]
    top[:, :size] = reduced[...] + edge[...]
    top[:, size:] = -edge[...]
    reduced[...] = edge[...]
    add_mass(reduced, next_mass, quarter)
    right_rows[:, :size] = reduced_right[...]
    add_rhs(right_rows, next_rhs, size // lanes)

    queue = Queue()
    gram_tasks(queue, slab_of(next_edge), parts, edge, edge_terms)
    system = System(top, reduced, right_rows, solved_right.at[0], terms_left, terms_right)
    eliminate([system], queue)
    queue.flush()
    reduced_right[...] = right_rows[:, size:]
    pack_sent(side, sent, reduced, reduced_right, step == steps - 1)


def pair_kernel(
    side, gathered, rhs,
    first_hbm, third_hbm, second_hbm, first_right, third_right, second_right,
    reduced, reduced_right, sent,
    first_top, third_top, rest, rights, *scratch,
):
    edge_terms, terms, sems = scratch[:4], scratch[4:8], scratch[8]
    size = reduced.shape[0]
    parts = gathered.shape[1]
    quarter = gathered.shape[2] - group
    steps = gathered.shape[0] - 1
    own, after = slice(0, size), slice(size, 2 * size)
    edges = [jnp.where(side[0] == 0, i + 1, steps - i) for i in range(steps)]
    blocks = [jnp.where(side[0] == 0, i, steps - i) for i in range(steps + 1)]

    def strip(n, s):
        here = slice(quarter * s, quarter * (s + 1))
        low = slice(size + here.start, size + here.stop)
        gram = gram_rows(edge_terms[n], here)

        def with_mass(ref, rows, cols, i):
            mass = gathered[blocks[i], s, quarter : quarter + 1, :quarter]
            ref[rows, cols] = ref[rows, cols] + on_diagonal(mass, quarter)

        if n == 0:
            first_top[here, own] = jnp.where(side[0] == 0, gram, 0.0)
            with_mass(first_top, here, here, 0)
        elif n == 1:
            first_top[here, own] = first_top[here, own] + gram
            first_top[here, after] = -gram
            rest[here, own] = gram
            with_mass(rest, here, here, 1)
        elif n == 2:
            rest[here, own] = rest[here, own] + gram
            third_top[here, own] = gram
            third_top[here, after] = -gram
            with_mass(third_top, here, here, 2)
        else:
            third_top[here, own] = third_top[here, own] + gram
            third_top[here, 2 * size :] = -gram
            rest[here, after] = jnp.zeros((quarter, size), jnp.float32)
            rest[low, after] = gram
            with_mass(rest, low, low, 3)

    for n in range(4):
        for s in range(parts):
            load_factor(slab_of(gathered, 0 if n == 0 else edges[n - 1]), edge_terms[n], s)
        strip(n, 0)
    rights[0, :, 2 * size :] = jnp.zeros_like(reduced_right)
    rights[0, :, after] = jnp.zeros_like(reduced_right)
    for n, first, i in ((0, 0, 0), (1, 0, 2), (1, 1, 1), (1, 2, 3)):
        add_rhs(rights.at[n], rhs, first * (size // lanes), blocks[i] ^ side[3])

    queue = Queue()
    for s in range(1, parts):
        for n in range(4):
            queue.add(functools.partial(strip, n, s))
    first = System(
        first_top, rest.at[own, own], rights.at[0, :, : 2 * size], first_right, terms[0], terms[1]
    )
    third = System(third_top, rest, rights.at[1], third_right, terms[2], terms[3])
    eliminate([first, third], queue, 4 * (parts - 2))

    def hand_over():
        rights[1, :, after] = rights[1, :, after] + rights[0, :, after]

    leaving = [
        pltpu.make_async_copy(first_top, first_hbm, sems.at[0]),
        pltpu.make_async_copy(third_top, third_hbm, sems.at[1]),
        pltpu.make_async_copy(rest.at[own, :], second_hbm, sems.at[2]),
    ]
    queue.add(hand_over)
    queue.add(leaving[0].start)
    queue.add(leaving[1].start)
    second = System(
        rest.at[own, :], rest.at[after, after], rights.at[1, :, size:], second_right, terms[0], terms[1]
    )
    eliminate([second], queue, 0, False)
    queue.flush()
    leaving[2].start()
    reduced[...] = rest[after, after]
    reduced_right[...] = rights[1, :, 2 * size :]
    pack_sent(side, sent, reduced, reduced_right, True)
    for copy in leaving:
        copy.wait()


def middle_kernel(
    side, own_edge, sent_edge, reduced, reduced_right,
    solved, solved_right, target, target_right,
    right_rows, edge_terms, terms_left, terms_right,
):
    size = reduced.shape[0]
    parts = own_edge.shape[1]
    quarter = own_edge.shape[2] - group
    own, sent = slab_of(own_edge), slab_of(sent_edge)

    def strip(s):
        here = slice(quarter * s, quarter * (s + 1))
        gram = gram_rows(edge_terms, here)
        solved[here, :size] = reduced[here, :] + gram
        solved[here, size:] = -gram
        target[here, :] = gram

    for s in range(parts):
        load_factor(lambda s: jnp.where(side[0] == 0, sent(s), own(s)), edge_terms, s)
    strip(0)
    right_rows[:, :size] = reduced_right[...]
    right_rows[:, size:] = jnp.zeros_like(target_right)
    queue = Queue()
    for s in range(1, parts):
        queue.add(functools.partial(strip, s))
    system = System(solved, target, right_rows, solved_right, terms_left, terms_right)
    eliminate([system], queue, parts - 2)
    queue.flush()
    target_right[...] = right_rows[:, size:]


def receive(side, top, right_rows, target, target_right, mine, other):
    half_cols = other.shape[1]
    for part, pieces in enumerate(packed_pieces(target.shape[0])):
        at = 0
        for p, first, last in pieces:
            cols = slice(at, at + lanes * (last - first))
            received = jnp.where(side[2] == part, mine[:, cols], other[:, cols])
            here = (span(p, p + 1), span(first, last))
            top[here] = target[here] + received
            at = cols.stop
    right_rows[...] = target_right[...] + mine[:, half_cols:]


def hand_out(out, x):
    for q in range(out.shape[0] // lanes):
        out[span(q, q + 1), :] = x[:, span(q, q + 1)].T


def pair_final_kernel(
    side, target, target_right, mine, other, middle_right, first_right, third_right, second_right,
    middle_hbm, first_hbm, third_hbm, second_hbm,
    out, top, right_rows, ended, x, terms_left, terms_right,
    middle, first, third, second, sems, top_terms, middle_terms, second_terms, last_terms,
):
    size = target.shape[0]
    panels = size // lanes
    place = side[1]
    pairs = ((middle_hbm, middle), (first_hbm, first), (third_hbm, third), (second_hbm, second))
    coming = [pltpu.make_async_copy(a, b, sems.at[n]) for n, (a, b) in enumerate(pairs)]
    for copy in coming:
        copy.start()
    receive(side, top, right_rows, target, target_right, mine, other)
    system = System(top, None, right_rows, ended, terms_left, terms_right)
    queue = Queue()
    for copy in coming:
        queue.add(copy.wait)

    def split_rows(ref, terms, p, cols):
        store_split(terms, span(p, p + 1), cols, ref[span(p, p + 1), cols])

    def split_last(p, cols):
        here = span(p, p + 1)
        value = third[here, cols]
        if cols.start < 2 * size:
            value = jnp.where(place == 2, value, first[here, cols])
        else:
            value = jnp.where(place == 2, value, 0.0)
        store_split(last_terms, here, cols, value)

    for p in range(panels):
        later = slice(lanes * (p + 1), 2 * size)
        queue.add(functools.partial(split_rows, middle, middle_terms, p, later))
        queue.add(functools.partial(split_rows, second, second_terms, p, later))
        queue.add(functools.partial(split_last, p, later))
        queue.add(functools.partial(split_last, p, slice(2 * size, 3 * size)))
    eliminate([system], queue)
    queue.flush()
    for p in range(panels - 1):
        split_rows(top, top_terms, p, slice(lanes * (p + 1), size))

    def back(right, terms, known):
        here = right
        for n, value in enumerate(known):
            low = size * (n + 1)
            here = here - dot(value, load_right(terms, whole, slice(low, low + size), 1), 1)
        for p in reversed(range(panels)):
            at = slice(lanes * p, lanes * (p + 1))
            x[:, at] = here[:, at]
            if p > 0:
                above = slice(0, lanes * p)
                change = dot(left_terms(here[:, at]), load_right(terms, above, at, 1), 1)
                here = here[:, above] - change
        return left_terms(x[...])

    def give(i):
        @pl.when(place == i)
        def _():
            hand_out(out, x)

    far = back(ended[...], top_terms, [])
    near = back(middle_right[...], middle_terms, [far])
    give(3)
    last = back(second_right[...], second_terms, [near])
    give(1)

    @pl.when(place % 2 == 0)
    def _():
        right = jnp.where(place == 2, third_right[...], first_right[...])
        back(right, last_terms, [last, near])
        hand_out(out, x)


def final_kernel(
    side, target, target_right, mine, other, middle, middle_right, chain, chain_right,
    out, top, right_rows, ended, x, terms_left, terms_right,
):
    place = side[1]
    steps = chain.shape[0]
    receive(side, top, right_rows, target, target_right, mine, other)
    queue = Queue()
    eliminate([System(top, None, right_rows, ended, terms_left, terms_right)], queue)
    queue.flush()

    def back(top, right, known):
        System(top, None, None, right, None, None).back(known, x)
        return left_terms(x[...])

    def give(i):
        @pl.when(place == i)
        def _():
            hand_out(out, x)

    known = back(top, ended, [])
    back(middle, middle_right, [known])
    give(steps)

    def walk(n, _):
        i = steps - 1 - n
        back(chain.at[i], chain_right.at[i], [left_terms(x[...])])
        give(i)
        return 0

    lax.fori_loop(0, steps, walk, 0)


def local(edge_factor, mass, rhs):
    _, quarter, size = edge_factor.shape
    cols = rhs.shape[2]
    blocks, parts = lax.axis_size("tm"), lax.axis_size("row")
    half = blocks // 2
    steps = half - 1
    mine = lax.axis_index("tm")
    right = (mine >= half).astype(jnp.int32)
    place = jnp.where(right == 0, mine, blocks - 1 - mine)
    parity = lax.axis_index("row") % 2
    side = jnp.stack([right, place, parity, mine % half]).astype(jnp.int32)

    halves = [[part * half + i for i in range(half)] for part in range(2)]
    halves_all = [[t * parts + r for t in ids for r in range(parts)] for ids in halves]
    swap = [(r, r ^ 1) for r in range(parts)]
    mass_rows = jnp.pad(mass, ((0, group - 1), (0, size - quarter)))
    packed = jnp.concatenate([edge_factor[0], mass_rows], axis=0)
    gathered = lax.all_gather(packed, ("tm", "row"), axis_index_groups=halves_all)
    gathered = gathered.reshape(half, parts, quarter + group, size)
    rhs_slots = [rhs[0]] + [
        lax.ppermute(rhs[0], "tm", [(t, t ^ d) for t in range(blocks)]) for d in range(1, half)
    ]
    rhs_half = jnp.stack(rhs_slots)
    gathered, rhs_half = lax.optimization_barrier((gathered, rhs_half))
    down = [(t + half, t) for t in range(half)]
    sent_edge = lax.ppermute(gathered[:1], "tm", down)

    vmem = pl.BlockSpec(memory_space=pltpu.VMEM)
    smem = pl.BlockSpec(memory_space=pltpu.SMEM)
    f32 = lambda *shape: jax.ShapeDtypeStruct(shape, jnp.float32)
    scratch = lambda *shape: pltpu.VMEM(shape, jnp.float32)
    terms = lambda *shape: pltpu.VMEM(shape, bf16)
    half_cols = sum(lanes * (b - a) for _, a, b in packed_pieces(size)[0])

    def edge_at(i, s):
        return jnp.where(s[0] == 0, i + 1, steps - i)

    def block_at(i, s):
        return jnp.where(s[0] == 0, i, steps - i)

    edge_block = (1, parts, quarter + group, size)
    mass_block = (1, parts, group, size)
    rhs_block = (1, size, cols)
    last = steps - 1
    if steps == 3:
        *stored, reduced, reduced_right, sent = pl.pallas_call(
            pair_kernel,
            in_specs=[smem, vmem, vmem],
            out_specs=(pl.BlockSpec(memory_space=pl.ANY),) * 3 + (vmem,) * 6,
            out_shape=(
                f32(size, 2 * size),
                f32(size, 3 * size),
                f32(size, 2 * size),
                f32(cols, size),
                f32(cols, size),
                f32(cols, size),
                f32(size, size),
                f32(cols, size),
                f32(lanes, half_cols + size),
            ),
            scratch_shapes=[
                scratch(size, 2 * size),
                scratch(size, 3 * size),
                scratch(2 * size, 2 * size),
                scratch(2, cols, 3 * size),
            ]
            + [terms(3, size, size)] * 4
            + [terms(3, 2 * size, lanes), terms(3, lanes, 2 * size)]
            + [terms(3, 3 * size, lanes), terms(3, lanes, 3 * size)]
            + [pltpu.SemaphoreType.DMA((3,))],
            compiler_params=pltpu.CompilerParams(vmem_limit_bytes=vmem_bytes),
        )(side, gathered, rhs_half)
    else:
        *stored, reduced, reduced_right, sent = pl.pallas_call(
            chain_kernel,
            grid_spec=pltpu.PrefetchScalarGridSpec(
                num_scalar_prefetch=1,
                grid=(steps,),
                in_specs=[
                    pl.BlockSpec(edge_block, lambda i, s: (0, 0, 0, 0)),
                    pl.BlockSpec(edge_block, lambda i, s: (edge_at(0, s), 0, 0, 0)),
                    pl.BlockSpec(edge_block, lambda i, s: (edge_at(jnp.minimum(i + 1, last), s), 0, 0, 0)),
                    pl.BlockSpec(mass_block, lambda i, s: (block_at(0, s), 0, quarter // group, 0)),
                    pl.BlockSpec(mass_block, lambda i, s: (block_at(i + 1, s), 0, quarter // group, 0)),
                    pl.BlockSpec(rhs_block, lambda i, s: (block_at(0, s) ^ s[3], 0, 0)),
                    pl.BlockSpec(rhs_block, lambda i, s: (block_at(i + 1, s) ^ s[3], 0, 0)),
                ],
                out_specs=(
                    pl.BlockSpec((1, size, 2 * size), lambda i, s: (i, 0, 0)),
                    pl.BlockSpec((1, cols, size), lambda i, s: (i, 0, 0)),
                    pl.BlockSpec((size, size), lambda i, s: (0, 0)),
                    pl.BlockSpec((cols, size), lambda i, s: (0, 0)),
                    pl.BlockSpec((lanes, half_cols + size), lambda i, s: (0, 0)),
                ),
                scratch_shapes=[
                    scratch(size, size),
                    scratch(cols, 2 * size),
                    terms(3, size, size),
                    terms(3, 2 * size, lanes),
                    terms(3, lanes, 2 * size),
                ],
            ),
            out_shape=(
                f32(steps, size, 2 * size),
                f32(steps, cols, size),
                f32(size, size),
                f32(cols, size),
                f32(lanes, half_cols + size),
            ),
            compiler_params=pltpu.CompilerParams(vmem_limit_bytes=vmem_bytes),
        )(side, gathered, gathered, gathered, gathered, gathered, rhs_half, rhs_half)

    across = [(t, (t + half) % blocks) for t in range(blocks)]
    received = lax.ppermute(sent, "tm", across)
    middle, middle_right, target, target_right = pl.pallas_call(
        middle_kernel,
        out_shape=(f32(size, 2 * size), f32(cols, size), f32(size, size), f32(cols, size)),
        grid=(1,),
        in_specs=[smem, pl.BlockSpec(edge_block, lambda i: (0, 0, 0, 0))] + [vmem] * 3,
        out_specs=(vmem,) * 4,
        scratch_shapes=[
            scratch(cols, 2 * size),
            terms(3, size, size),
            terms(3, 2 * size, lanes),
            terms(3, lanes, 2 * size),
        ],
        compiler_params=pltpu.CompilerParams(vmem_limit_bytes=vmem_bytes),
    )(side, gathered, sent_edge, reduced, reduced_right)

    received, target = lax.optimization_barrier((received, target))
    received_other = lax.ppermute(received[:, :half_cols], "row", swap)
    final_scratch = [
        scratch(size, size),
        scratch(cols, size),
        scratch(cols, size),
        scratch(cols, size),
        terms(3, size, lanes),
        terms(3, lanes, size),
    ]
    arrived = (target, target_right, received, received_other)
    if steps == 3:
        first, third, second, first_right, third_right, second_right = stored
        solution = pl.pallas_call(
            pair_final_kernel,
            out_shape=f32(size, cols),
            in_specs=[smem] + [vmem] * 8 + [pl.BlockSpec(memory_space=pl.ANY)] * 4,
            out_specs=vmem,
            scratch_shapes=final_scratch
            + [scratch(size, 2 * size), scratch(size, 2 * size)]
            + [scratch(size, 3 * size), scratch(size, 2 * size)]
            + [pltpu.SemaphoreType.DMA((4,))]
            + [terms(3, size, size), terms(3, size, 2 * size)]
            + [terms(3, size, 2 * size), terms(3, size, 3 * size)],
            compiler_params=pltpu.CompilerParams(vmem_limit_bytes=vmem_bytes),
        )(
            side, *arrived, middle_right, first_right, third_right, second_right,
            middle, first, third, second,
        )
    else:
        solution = pl.pallas_call(
            final_kernel,
            out_shape=f32(size, cols),
            in_specs=[smem] + [vmem] * 8,
            out_specs=vmem,
            scratch_shapes=final_scratch,
            compiler_params=pltpu.CompilerParams(vmem_limit_bytes=vmem_bytes),
        )(side, *arrived, middle, middle_right, *stored)
    return solution[None]


def solution(mesh):
    placed = (P("tm", "row", None), P("tm", "row"), P("tm", None, "row"))
    return jax.shard_map(
        local, mesh=mesh, in_specs=placed, out_specs=P("tm", None, "row"), check_vma=False
    )
```

```python
import functools

import jax
import jax.numpy as jnp
from jax import lax
from jax.experimental import pallas as pl
from jax.experimental.pallas import tpu as pltpu
from jax.sharding import PartitionSpec as P

lanes = 128
group = 8
vmem_bytes = 58 * 1024 * 1024
bf16 = jnp.bfloat16


def split(x):
    high = x.astype(bf16)
    rest = x - high.astype(jnp.float32)
    middle = rest.astype(bf16)
    low = (rest - middle.astype(jnp.float32)).astype(bf16)
    return high, middle, low


def left_terms(x):
    a, b, c = split(x)
    return jnp.concatenate([a, a, b, b, a, c], axis=1)


def right_terms(x, axis=0):
    a, b, c = split(x)
    return jnp.concatenate([a, b, a, b, c, a], axis=axis)


def store_split(ref, rows, cols, x):
    for n, part in enumerate(split(x)):
        ref[n, rows, cols] = part


def load_left(ref, rows, cols):
    a, b, c = (ref[n, rows, cols] for n in range(3))
    return jnp.concatenate([a, a, b, b, a, c], axis=1)


def load_right(ref, rows, cols, axis=0):
    a, b, c = (ref[n, rows, cols] for n in range(3))
    return jnp.concatenate([a, b, a, b, c, a], axis=axis)


whole = slice(None)


def dot(left, right, right_dim=0):
    return lax.dot_general(
        left, right, (((1,), (right_dim,)), ((), ())), preferred_element_type=jnp.float32
    )


def spread_row(block, row):
    return jnp.broadcast_to(block[row : row + 1], (group, lanes))


def spread_col(block, col):
    return jnp.broadcast_to(block[:, col : col + 1], (group, lanes))


def total(terms):
    while len(terms) > 1:
        paired = [terms[i] + terms[i + 1] for i in range(0, len(terms) - 1, 2)]
        terms = paired + terms[len(paired) * 2 :]
    return terms[0]


def inverse_128(block, ride):
    count = lanes // group
    inner = 4
    slabs = [block[group * i : group * (i + 1)] for i in range(count)]
    sub_ids = lax.broadcasted_iota(jnp.int32, (group, lanes), 0)
    lane_ids = lax.broadcasted_iota(jnp.int32, (group, lanes), 1)
    late = None
    for b in range(count // inner):
        base = group * inner * b
        work = slabs[inner * b : inner * (b + 1)]
        ahead = []
        for s in range(inner):
            start = base + group * s
            more = s + 1 < inner
            top = ahead + [spread_col(work[s], start + j) for j in range(len(ahead), group)]
            riders, low = [], []
            if more:
                riders = [spread_col(work[s], start + group + j) for j in range(ride)]
                low = [spread_col(work[s + 1], start + group + j) for j in range(ride)]
            own = (lane_ids >= start) & (lane_ids < start + group)
            wide = jnp.where(own, jnp.where(lane_ids == sub_ids + start, 1.0, 0.0), work[s])
            factors = [
                None if i == s else [spread_col(work[i], start + j) for j in range(group)]
                for i in range(inner)
            ]
            for k in range(0, group, 2):
                u, v = top[k], top[k + 1]
                a, b_, c = spread_row(u, k), spread_row(u, k + 1), spread_row(v, k + 1)
                scale = pl.reciprocal(a * c - b_ * b_, approx=True)
                is_k, is_l = sub_ids == k, sub_ids == k + 1
                pair = is_k | is_l
                first = jnp.where(is_k, -c, jnp.where(is_l, b_, c * u - b_ * v))
                second = jnp.where(is_k, b_, jnp.where(is_l, -a, a * v - b_ * u))

                def pivoted(x):
                    row_k, row_l = spread_row(x, k), spread_row(x, k + 1)
                    return jnp.where(pair, 0.0, x) - scale * (first * row_k + second * row_l)

                top = [x if j <= k + 1 else pivoted(x) for j, x in enumerate(top)]
                riders = [pivoted(x) for x in riders]
                wide = pivoted(wide)
                yield
            rows = [spread_row(wide, j) for j in range(group)]
            ahead = [
                x - total([factors[s + 1][j] * spread_row(riders[n], j) for j in range(group)])
                for n, x in enumerate(low)
            ]
            for i in range(inner):
                if i != s:
                    change = total([factors[i][j] * rows[j] for j in range(group)])
                    work[i] = jnp.where(own, 0.0, work[i]) - change
            work[s] = wide
            if s == 1 and late is not None:
                late()
                late = None
            yield
        slabs[inner * b : inner * (b + 1)] = work
        zero = jnp.zeros((group, lanes), jnp.float32)
        in_block = (lane_ids >= base) & (lane_ids < base + group * inner)
        solved = [zero] * (inner * b) + work + [zero] * (count - inner * (b + 1))
        solved = right_terms(jnp.concatenate(solved, axis=0))

        def merge(first, last, solved=solved, in_block=in_block):
            if first == last:
                return
            here = jnp.concatenate([jnp.where(in_block, x, 0.0) for x in slabs[first:last]], axis=0)
            change = dot(left_terms(here), solved)
            for i in range(first, last):
                at = group * (i - first)
                slabs[i] = jnp.where(in_block, 0.0, slabs[i]) - change[at : at + group]

        soon = min(inner * (b + 2), count)
        merge(inner * (b + 1), soon)

        def late(b=b, soon=soon, merge=merge):
            merge(0, inner * b)
            merge(soon, count)

    late()
    return jnp.concatenate(slabs, axis=0)


inverse_yields = 80


class Queue:
    def __init__(self):
        self.tasks = []

    def add(self, task):
        self.tasks.append(task)

    def between(self, left, keep=0):
        for _ in range(-(-(len(self.tasks) - keep) // max(left, 1))):
            if self.tasks:
                self.tasks.pop(0)()

    def flush(self, keep=0):
        while len(self.tasks) > keep:
            self.tasks.pop(0)()


def inverses(blocks, queue, keep):
    ride = 4 if len(blocks) == 1 else 0
    runs = [inverse_128(block, ride) for block in blocks]
    results = [None] * len(runs)
    left = inverse_yields // 5
    count = 0
    while any(result is None for result in results):
        for n, run in enumerate(runs):
            try:
                next(run)
            except StopIteration as stop:
                results[n] = stop.value
        count += 1
        if count % 5 == 0:
            queue.between(left, keep)
            left -= 1
    queue.flush(keep)
    return results


def span(first, last):
    return slice(lanes * first, lanes * last)


class System:
    def __init__(self, top, bottom, right, out, terms_left, terms_right):
        self.top, self.bottom, self.right, self.out = top, bottom, right, out
        self.terms_left, self.terms_right = terms_left, terms_right
        self.panels = top.shape[-2] // lanes
        self.blocks = top.shape[-1] // lanes

    def at(self, rows, cols):
        if rows[0] < self.panels:
            return self.top, (span(*rows), span(*cols))
        low = self.panels
        return self.bottom, (span(rows[0] - low, rows[1] - low), span(cols[0] - low, cols[1] - low))

    def load(self, rows, cols):
        ref, where = self.at(rows, cols)
        return ref[where]

    def store(self, rows, cols, value):
        ref, where = self.at(rows, cols)
        ref[where] = value

    def prepare(self, p, q):
        store_split(self.terms_left, span(q, q + 1), whole, self.load((p, p + 1), (q, q + 1)).T)

    def solve(self, p, cols, inverse):
        solved = dot(inverse, right_terms(self.load((p, p + 1), cols)))
        self.store((p, p + 1), cols, solved)
        store_split(self.terms_right, whole, span(*cols), solved)

    def update(self, rows, cols):
        change = dot(
            load_left(self.terms_left, span(*rows), whole),
            load_right(self.terms_right, whole, span(*cols)),
        )
        self.store(rows, cols, self.load(rows, cols) - change)

    def forward(self, p, inverse):
        here = left_terms(self.right[:, span(p, p + 1)])
        self.out[:, span(p, p + 1)] = dot(here, inverse)
        if p + 1 < self.blocks:
            later = span(p + 1, self.blocks)
            change = dot(here, load_right(self.terms_right, whole, later))
            self.right[:, later] = self.right[:, later] - change

    def diagonal(self, p):
        return self.load((p, p + 1), (p, p + 1))

    def ready(self, p):
        if p + 1 < self.blocks:
            self.prepare(p, p + 1)
            block = self.load((p, p + 1), (p + 1, p + 2))
            store_split(self.terms_right, whole, span(p + 1, p + 2), block)

    def next_pivot(self, p, inverse):
        after = (p + 1, p + 2)
        if p + 1 < self.blocks:
            solved = dot(left_terms(inverse), load_right(self.terms_right, whole, span(*after)))
            terms = right_terms(solved)
            change = dot(load_left(self.terms_left, span(*after), whole), terms)
            self.store(after, after, self.load(after, after) - change)
            self.store((p, p + 1), after, solved)
            store_split(self.terms_right, whole, span(*after), solved)
        self.store((p, p + 1), (p, p + 1), inverse)

    def background(self, p, inverse, queue):
        terms = left_terms(inverse)
        after = p + 1
        strips = []
        q = after + 1
        while q < self.blocks:
            end = min(self.blocks, q + 2 if q % 2 == 0 else q + 1)
            strips.append((q, end))
            q = end
        for strip in strips:
            for q in range(*strip):
                queue.add(functools.partial(self.prepare, p, q))
            queue.add(functools.partial(self.solve, p, strip, terms))
        for strip in strips:
            start = after
            while start < strip[1]:
                end = min(strip[1], start + 4)
                if start < self.panels:
                    end = min(end, self.panels)
                queue.add(functools.partial(self.update, (start, end), strip))
                start = end
        queue.add(functools.partial(self.forward, p, right_terms(inverse)))

    def back(self, known, x):
        for p in reversed(range(self.panels)):
            here = self.out[:, span(p, p + 1)]
            for n, terms in enumerate(known):
                low = self.panels * (n + 1)
                factor = self.top[span(p, p + 1), span(low, low + self.panels)]
                here = here - dot(terms, right_terms(factor, 1), 1)
            if p + 1 < self.panels:
                later = span(p + 1, self.panels)
                factor = self.top[span(p, p + 1), later]
                here = here - dot(left_terms(x[:, later]), right_terms(factor, 1), 1)
            x[:, span(p, p + 1)] = here


def eliminate(systems, queue, keep_first=0, fresh=True):
    for p in range(systems[0].panels):
        keep = keep_first if p == 0 else 0
        for system in systems:
            if p == 0 and fresh:
                system.ready(p)
            else:
                queue.add(functools.partial(system.ready, p))
        found = inverses([system.diagonal(p) for system in systems], queue, keep)
        for system, inverse in zip(systems, found):
            system.next_pivot(p, inverse)
        for system, inverse in zip(systems, found):
            system.background(p, inverse, queue)


def load_factor(slab, terms, s):
    value = slab(s)
    store_split(terms, slice(value.shape[0] * s, value.shape[0] * (s + 1)), whole, value)


def gram_rows(terms, rows):
    return dot(load_left(terms, rows, whole), load_right(terms, whole, whole, 1), 1)


def gram_tasks(queue, slab, parts, out, terms):
    rows = out.shape[0] // parts

    def multiply(s):
        here = slice(rows * s, rows * (s + 1))
        out[here, :] = gram_rows(terms, here)

    for s in range(parts):
        queue.add(functools.partial(load_factor, slab, terms, s))
    for s in range(parts):
        queue.add(functools.partial(multiply, s))


def slab_of(edge, block=0):
    rows = edge.shape[2] - group
    return lambda s: edge[block, s, :rows, :]


def on_diagonal(mass, rows):
    ids = (rows, rows)
    diag = lax.broadcasted_iota(jnp.int32, ids, 0) == lax.broadcasted_iota(jnp.int32, ids, 1)
    return jnp.where(diag, mass, 0.0)


def add_mass(table, mass, rows):
    for s in range(mass.shape[1]):
        here = slice(rows * s, rows * (s + 1))
        table[here, here] = table[here, here] + on_diagonal(mass[0, s, :1, :rows], rows)


def add_rhs(right, rhs, first, block=0):
    for q in range(rhs.shape[1] // lanes):
        right[:, span(first + q, first + q + 1)] = rhs[block, span(q, q + 1), :].T


def pack_sent(side, sent, reduced, reduced_right, ready):
    for part, pieces in enumerate(packed_pieces(reduced.shape[0])):

        @pl.when(ready & (side[2] == part))
        def _():
            at = 0
            for p, first, last in pieces:
                width = lanes * (last - first)
                sent[:, at : at + width] = reduced[span(p, p + 1), span(first, last)]
                at += width
            sent[:, at:] = reduced_right[...]


def packed_pieces(size):
    panels = size // lanes
    order = [[p for p in range(panels) if p % 4 in (0, 3)], [p for p in range(panels) if p % 4 in (1, 2)]]
    return [[(p, p, panels) for p in rows] for rows in order]


def chain_kernel(
    side, start_edge, first_edge, next_edge, first_mass, next_mass, first_rhs, next_rhs,
    solved, solved_right, reduced, reduced_right, sent,
    edge, right_rows, edge_terms, terms_left, terms_right,
):
    size = reduced.shape[0]
    parts = start_edge.shape[1]
    quarter = start_edge.shape[2] - group
    step, steps = pl.program_id(0), pl.num_programs(0)

    @pl.when(step == 0)
    def _():
        queue = Queue()
        gram_tasks(queue, slab_of(start_edge), parts, edge, edge_terms)
        queue.flush()
        reduced[...] = jnp.where(side[0] == 0, edge[...], 0.0)
        add_mass(reduced, first_mass, quarter)
        gram_tasks(queue, slab_of(first_edge), parts, edge, edge_terms)
        queue.flush()
        add_rhs(reduced_right, first_rhs, 0)

    top = solved.at[0]
    top[:, :size] = reduced[...] + edge[...]
    top[:, size:] = -edge[...]
    reduced[...] = edge[...]
    add_mass(reduced, next_mass, quarter)
    right_rows[:, :size] = reduced_right[...]
    add_rhs(right_rows, next_rhs, size // lanes)

    queue = Queue()
    gram_tasks(queue, slab_of(next_edge), parts, edge, edge_terms)
    system = System(top, reduced, right_rows, solved_right.at[0], terms_left, terms_right)
    eliminate([system], queue)
    queue.flush()
    reduced_right[...] = right_rows[:, size:]
    pack_sent(side, sent, reduced, reduced_right, step == steps - 1)


def pair_kernel(
    side, gathered, rhs,
    first_hbm, third_hbm, second_hbm, first_right, third_right, second_right,
    reduced, reduced_right, sent,
    first_top, third_top, rest, rights, *scratch,
):
    edge_terms, terms, sems = scratch[:4], scratch[4:8], scratch[8]
    size = reduced.shape[0]
    parts = gathered.shape[1]
    quarter = gathered.shape[2] - group
    steps = gathered.shape[0] - 1
    own, after = slice(0, size), slice(size, 2 * size)
    edges = [jnp.where(side[0] == 0, i + 1, steps - i) for i in range(steps)]
    blocks = [jnp.where(side[0] == 0, i, steps - i) for i in range(steps + 1)]

    def strip(n, s):
        here = slice(quarter * s, quarter * (s + 1))
        low = slice(size + here.start, size + here.stop)
        gram = gram_rows(edge_terms[n], here)

        def with_mass(ref, rows, cols, i):
            mass = gathered[blocks[i], s, quarter : quarter + 1, :quarter]
            ref[rows, cols] = ref[rows, cols] + on_diagonal(mass, quarter)

        if n == 0:
            first_top[here, own] = jnp.where(side[0] == 0, gram, 0.0)
            with_mass(first_top, here, here, 0)
        elif n == 1:
            first_top[here, own] = first_top[here, own] + gram
            first_top[here, after] = -gram
            rest[here, own] = gram
            with_mass(rest, here, here, 1)
        elif n == 2:
            rest[here, own] = rest[here, own] + gram
            third_top[here, own] = gram
            third_top[here, after] = -gram
            with_mass(third_top, here, here, 2)
        else:
            third_top[here, own] = third_top[here, own] + gram
            third_top[here, 2 * size :] = -gram
            rest[here, after] = jnp.zeros((quarter, size), jnp.float32)
            rest[low, after] = gram
            with_mass(rest, low, low, 3)

    for n in range(4):
        for s in range(parts):
            load_factor(slab_of(gathered, 0 if n == 0 else edges[n - 1]), edge_terms[n], s)
        strip(n, 0)
    rights[0, :, 2 * size :] = jnp.zeros_like(reduced_right)
    rights[0, :, after] = jnp.zeros_like(reduced_right)
    for n, first, i in ((0, 0, 0), (1, 0, 2), (1, 1, 1), (1, 2, 3)):
        add_rhs(rights.at[n], rhs, first * (size // lanes), blocks[i] ^ side[3])

    queue = Queue()
    for s in range(1, parts):
        for n in range(4):
            queue.add(functools.partial(strip, n, s))
    first = System(
        first_top, rest.at[own, own], rights.at[0, :, : 2 * size], first_right, terms[0], terms[1]
    )
    third = System(third_top, rest, rights.at[1], third_right, terms[2], terms[3])
    eliminate([first, third], queue, 4 * (parts - 2))

    def hand_over():
        rights[1, :, after] = rights[1, :, after] + rights[0, :, after]

    leaving = [
        pltpu.make_async_copy(first_top, first_hbm, sems.at[0]),
        pltpu.make_async_copy(third_top, third_hbm, sems.at[1]),
        pltpu.make_async_copy(rest.at[own, :], second_hbm, sems.at[2]),
    ]
    queue.add(hand_over)
    queue.add(leaving[0].start)
    queue.add(leaving[1].start)
    second = System(
        rest.at[own, :], rest.at[after, after], rights.at[1, :, size:], second_right, terms[0], terms[1]
    )
    eliminate([second], queue, 0, False)
    queue.flush()
    leaving[2].start()
    reduced[...] = rest[after, after]
    reduced_right[...] = rights[1, :, 2 * size :]
    pack_sent(side, sent, reduced, reduced_right, True)
    for copy in leaving:
        copy.wait()


def middle_kernel(
    side, own_edge, sent_edge, reduced, reduced_right,
    solved, solved_right, target, target_right,
    right_rows, edge_terms, terms_left, terms_right,
):
    size = reduced.shape[0]
    parts = own_edge.shape[1]
    quarter = own_edge.shape[2] - group
    own, sent = slab_of(own_edge), slab_of(sent_edge)

    def strip(s):
        here = slice(quarter * s, quarter * (s + 1))
        gram = gram_rows(edge_terms, here)
        solved[here, :size] = reduced[here, :] + gram
        solved[here, size:] = -gram
        target[here, :] = gram

    for s in range(parts):
        load_factor(lambda s: jnp.where(side[0] == 0, sent(s), own(s)), edge_terms, s)
    strip(0)
    right_rows[:, :size] = reduced_right[...]
    right_rows[:, size:] = jnp.zeros_like(target_right)
    queue = Queue()
    for s in range(1, parts):
        queue.add(functools.partial(strip, s))
    system = System(solved, target, right_rows, solved_right, terms_left, terms_right)
    eliminate([system], queue, parts - 2)
    queue.flush()
    target_right[...] = right_rows[:, size:]


def receive(side, top, right_rows, target, target_right, mine, other):
    half_cols = other.shape[1]
    for part, pieces in enumerate(packed_pieces(target.shape[0])):
        at = 0
        for p, first, last in pieces:
            cols = slice(at, at + lanes * (last - first))
            received = jnp.where(side[2] == part, mine[:, cols], other[:, cols])
            here = (span(p, p + 1), span(first, last))
            top[here] = target[here] + received
            at = cols.stop
    right_rows[...] = target_right[...] + mine[:, half_cols:]


def hand_out(out, x):
    for q in range(out.shape[0] // lanes):
        out[span(q, q + 1), :] = x[:, span(q, q + 1)].T


def pair_final_kernel(
    side, target, target_right, mine, other, middle_right, first_right, third_right, second_right,
    middle_hbm, first_hbm, third_hbm, second_hbm,
    out, top, right_rows, ended, x, terms_left, terms_right, middle, first, third, second, sems,
):
    place = side[1]
    pairs = ((middle_hbm, middle), (first_hbm, first), (third_hbm, third), (second_hbm, second))
    coming = [pltpu.make_async_copy(a, b, sems.at[n]) for n, (a, b) in enumerate(pairs)]
    for copy in coming:
        copy.start()
    receive(side, top, right_rows, target, target_right, mine, other)
    queue = Queue()
    eliminate([System(top, None, right_rows, ended, terms_left, terms_right)], queue)
    queue.flush()
    for copy in coming:
        copy.wait()

    def back(top, right, known):
        System(top, None, None, right, None, None).back(known, x)
        return left_terms(x[...])

    def give(i):
        @pl.when(place == i)
        def _():
            hand_out(out, x)

    far = back(top, ended, [])
    near = back(middle, middle_right, [far])
    give(3)
    last = back(second, second_right, [near])
    give(1)

    @pl.when(place == 0)
    def _():
        back(first, first_right, [last])
        hand_out(out, x)

    @pl.when(place == 2)
    def _():
        back(third, third_right, [last, near])
        hand_out(out, x)


def final_kernel(
    side, target, target_right, mine, other, middle, middle_right, chain, chain_right,
    out, top, right_rows, ended, x, terms_left, terms_right,
):
    place = side[1]
    steps = chain.shape[0]
    receive(side, top, right_rows, target, target_right, mine, other)
    queue = Queue()
    eliminate([System(top, None, right_rows, ended, terms_left, terms_right)], queue)
    queue.flush()

    def back(top, right, known):
        System(top, None, None, right, None, None).back(known, x)
        return left_terms(x[...])

    def give(i):
        @pl.when(place == i)
        def _():
            hand_out(out, x)

    known = back(top, ended, [])
    back(middle, middle_right, [known])
    give(steps)

    def walk(n, _):
        i = steps - 1 - n
        back(chain.at[i], chain_right.at[i], [left_terms(x[...])])
        give(i)
        return 0

    lax.fori_loop(0, steps, walk, 0)


def local(edge_factor, mass, rhs):
    _, quarter, size = edge_factor.shape
    cols = rhs.shape[2]
    blocks, parts = lax.axis_size("tm"), lax.axis_size("row")
    half = blocks // 2
    steps = half - 1
    mine = lax.axis_index("tm")
    right = (mine >= half).astype(jnp.int32)
    place = jnp.where(right == 0, mine, blocks - 1 - mine)
    parity = lax.axis_index("row") % 2
    side = jnp.stack([right, place, parity, mine % half]).astype(jnp.int32)

    halves = [[part * half + i for i in range(half)] for part in range(2)]
    halves_all = [[t * parts + r for t in ids for r in range(parts)] for ids in halves]
    swap = [(r, r ^ 1) for r in range(parts)]
    mass_rows = jnp.pad(mass, ((0, group - 1), (0, size - quarter)))
    packed = jnp.concatenate([edge_factor[0], mass_rows], axis=0)
    gathered = lax.all_gather(packed, ("tm", "row"), axis_index_groups=halves_all)
    gathered = gathered.reshape(half, parts, quarter + group, size)
    rhs_slots = [rhs[0]] + [
        lax.ppermute(rhs[0], "tm", [(t, t ^ d) for t in range(blocks)]) for d in range(1, half)
    ]
    rhs_half = jnp.stack(rhs_slots)
    gathered, rhs_half = lax.optimization_barrier((gathered, rhs_half))
    down = [(t + half, t) for t in range(half)]
    sent_edge = lax.ppermute(gathered[:1], "tm", down)

    vmem = pl.BlockSpec(memory_space=pltpu.VMEM)
    smem = pl.BlockSpec(memory_space=pltpu.SMEM)
    f32 = lambda *shape: jax.ShapeDtypeStruct(shape, jnp.float32)
    scratch = lambda *shape: pltpu.VMEM(shape, jnp.float32)
    terms = lambda *shape: pltpu.VMEM(shape, bf16)
    half_cols = sum(lanes * (b - a) for _, a, b in packed_pieces(size)[0])

    def edge_at(i, s):
        return jnp.where(s[0] == 0, i + 1, steps - i)

    def block_at(i, s):
        return jnp.where(s[0] == 0, i, steps - i)

    edge_block = (1, parts, quarter + group, size)
    mass_block = (1, parts, group, size)
    rhs_block = (1, size, cols)
    last = steps - 1
    if steps == 3:
        *stored, reduced, reduced_right, sent = pl.pallas_call(
            pair_kernel,
            in_specs=[smem, vmem, vmem],
            out_specs=(pl.BlockSpec(memory_space=pl.ANY),) * 3 + (vmem,) * 6,
            out_shape=(
                f32(size, 2 * size),
                f32(size, 3 * size),
                f32(size, 2 * size),
                f32(cols, size),
                f32(cols, size),
                f32(cols, size),
                f32(size, size),
                f32(cols, size),
                f32(lanes, half_cols + size),
            ),
            scratch_shapes=[
                scratch(size, 2 * size),
                scratch(size, 3 * size),
                scratch(2 * size, 2 * size),
                scratch(2, cols, 3 * size),
            ]
            + [terms(3, size, size)] * 4
            + [terms(3, 2 * size, lanes), terms(3, lanes, 2 * size)]
            + [terms(3, 3 * size, lanes), terms(3, lanes, 3 * size)]
            + [pltpu.SemaphoreType.DMA((3,))],
            compiler_params=pltpu.CompilerParams(vmem_limit_bytes=vmem_bytes),
        )(side, gathered, rhs_half)
    else:
        *stored, reduced, reduced_right, sent = pl.pallas_call(
            chain_kernel,
            grid_spec=pltpu.PrefetchScalarGridSpec(
                num_scalar_prefetch=1,
                grid=(steps,),
                in_specs=[
                    pl.BlockSpec(edge_block, lambda i, s: (0, 0, 0, 0)),
                    pl.BlockSpec(edge_block, lambda i, s: (edge_at(0, s), 0, 0, 0)),
                    pl.BlockSpec(edge_block, lambda i, s: (edge_at(jnp.minimum(i + 1, last), s), 0, 0, 0)),
                    pl.BlockSpec(mass_block, lambda i, s: (block_at(0, s), 0, quarter // group, 0)),
                    pl.BlockSpec(mass_block, lambda i, s: (block_at(i + 1, s), 0, quarter // group, 0)),
                    pl.BlockSpec(rhs_block, lambda i, s: (block_at(0, s) ^ s[3], 0, 0)),
                    pl.BlockSpec(rhs_block, lambda i, s: (block_at(i + 1, s) ^ s[3], 0, 0)),
                ],
                out_specs=(
                    pl.BlockSpec((1, size, 2 * size), lambda i, s: (i, 0, 0)),
                    pl.BlockSpec((1, cols, size), lambda i, s: (i, 0, 0)),
                    pl.BlockSpec((size, size), lambda i, s: (0, 0)),
                    pl.BlockSpec((cols, size), lambda i, s: (0, 0)),
                    pl.BlockSpec((lanes, half_cols + size), lambda i, s: (0, 0)),
                ),
                scratch_shapes=[
                    scratch(size, size),
                    scratch(cols, 2 * size),
                    terms(3, size, size),
                    terms(3, 2 * size, lanes),
                    terms(3, lanes, 2 * size),
                ],
            ),
            out_shape=(
                f32(steps, size, 2 * size),
                f32(steps, cols, size),
                f32(size, size),
                f32(cols, size),
                f32(lanes, half_cols + size),
            ),
            compiler_params=pltpu.CompilerParams(vmem_limit_bytes=vmem_bytes),
        )(side, gathered, gathered, gathered, gathered, gathered, rhs_half, rhs_half)

    across = [(t, (t + half) % blocks) for t in range(blocks)]
    received = lax.ppermute(sent, "tm", across)
    middle, middle_right, target, target_right = pl.pallas_call(
        middle_kernel,
        out_shape=(f32(size, 2 * size), f32(cols, size), f32(size, size), f32(cols, size)),
        grid=(1,),
        in_specs=[smem, pl.BlockSpec(edge_block, lambda i: (0, 0, 0, 0))] + [vmem] * 3,
        out_specs=(vmem,) * 4,
        scratch_shapes=[
            scratch(cols, 2 * size),
            terms(3, size, size),
            terms(3, 2 * size, lanes),
            terms(3, lanes, 2 * size),
        ],
        compiler_params=pltpu.CompilerParams(vmem_limit_bytes=vmem_bytes),
    )(side, gathered, sent_edge, reduced, reduced_right)

    received, target = lax.optimization_barrier((received, target))
    received_other = lax.ppermute(received[:, :half_cols], "row", swap)
    final_scratch = [
        scratch(size, size),
        scratch(cols, size),
        scratch(cols, size),
        scratch(cols, size),
        terms(3, size, lanes),
        terms(3, lanes, size),
    ]
    arrived = (target, target_right, received, received_other)
    if steps == 3:
        first, third, second, first_right, third_right, second_right = stored
        solution = pl.pallas_call(
            pair_final_kernel,
            out_shape=f32(size, cols),
            in_specs=[smem] + [vmem] * 8 + [pl.BlockSpec(memory_space=pl.ANY)] * 4,
            out_specs=vmem,
            scratch_shapes=final_scratch
            + [scratch(size, 2 * size), scratch(size, 2 * size)]
            + [scratch(size, 3 * size), scratch(size, 2 * size)]
            + [pltpu.SemaphoreType.DMA((4,))],
            compiler_params=pltpu.CompilerParams(vmem_limit_bytes=vmem_bytes),
        )(
            side, *arrived, middle_right, first_right, third_right, second_right,
            middle, first, third, second,
        )
    else:
        solution = pl.pallas_call(
            final_kernel,
            out_shape=f32(size, cols),
            in_specs=[smem] + [vmem] * 8,
            out_specs=vmem,
            scratch_shapes=final_scratch,
            compiler_params=pltpu.CompilerParams(vmem_limit_bytes=vmem_bytes),
        )(side, *arrived, middle, middle_right, *stored)
    return solution[None]


def solution(mesh):
    placed = (P("tm", "row", None), P("tm", "row"), P("tm", None, "row"))
    return jax.shard_map(
        local, mesh=mesh, in_specs=placed, out_specs=P("tm", None, "row"), check_vma=False
    )
```

```python
import functools

import jax
import jax.numpy as jnp
from jax import lax
from jax.experimental import pallas as pl
from jax.experimental.pallas import tpu as pltpu
from jax.sharding import PartitionSpec as P

lanes = 128
group = 8
vmem_bytes = 58 * 1024 * 1024
bf16 = jnp.bfloat16


def split(x):
    high = x.astype(bf16)
    rest = x - high.astype(jnp.float32)
    middle = rest.astype(bf16)
    low = (rest - middle.astype(jnp.float32)).astype(bf16)
    return high, middle, low


def left_terms(x):
    a, b, c = split(x)
    return jnp.concatenate([a, a, b, b, a, c], axis=1)


def right_terms(x, axis=0):
    a, b, c = split(x)
    return jnp.concatenate([a, b, a, b, c, a], axis=axis)


def store_split(ref, rows, cols, x):
    for n, part in enumerate(split(x)):
        ref[n, rows, cols] = part


def load_left(ref, rows, cols):
    a, b, c = (ref[n, rows, cols] for n in range(3))
    return jnp.concatenate([a, a, b, b, a, c], axis=1)


def load_right(ref, rows, cols, axis=0):
    a, b, c = (ref[n, rows, cols] for n in range(3))
    return jnp.concatenate([a, b, a, b, c, a], axis=axis)


whole = slice(None)


def dot(left, right, right_dim=0):
    return lax.dot_general(
        left, right, (((1,), (right_dim,)), ((), ())), preferred_element_type=jnp.float32
    )


def spread_row(block, row):
    return jnp.broadcast_to(block[row : row + 1], (group, lanes))


def spread_col(block, col):
    return jnp.broadcast_to(block[:, col : col + 1], (group, lanes))


def total(terms):
    while len(terms) > 1:
        paired = [terms[i] + terms[i + 1] for i in range(0, len(terms) - 1, 2)]
        terms = paired + terms[len(paired) * 2 :]
    return terms[0]


def inverse_128(block, ride):
    count = lanes // group
    inner = 4
    slabs = [block[group * i : group * (i + 1)] for i in range(count)]
    sub_ids = lax.broadcasted_iota(jnp.int32, (group, lanes), 0)
    lane_ids = lax.broadcasted_iota(jnp.int32, (group, lanes), 1)
    late = None
    for b in range(count // inner):
        base = group * inner * b
        work = slabs[inner * b : inner * (b + 1)]
        ahead = []
        for s in range(inner):
            start = base + group * s
            more = s + 1 < inner
            top = ahead + [spread_col(work[s], start + j) for j in range(len(ahead), group)]
            riders, low = [], []
            if more:
                riders = [spread_col(work[s], start + group + j) for j in range(ride)]
                low = [spread_col(work[s + 1], start + group + j) for j in range(ride)]
            own = (lane_ids >= start) & (lane_ids < start + group)
            wide = jnp.where(own, jnp.where(lane_ids == sub_ids + start, 1.0, 0.0), work[s])
            factors = [
                None if i == s else [spread_col(work[i], start + j) for j in range(group)]
                for i in range(inner)
            ]
            for k in range(0, group, 2):
                u, v = top[k], top[k + 1]
                a, b_, c = spread_row(u, k), spread_row(u, k + 1), spread_row(v, k + 1)
                scale = pl.reciprocal(a * c - b_ * b_, approx=True)
                is_k, is_l = sub_ids == k, sub_ids == k + 1
                pair = is_k | is_l
                first = jnp.where(is_k, -c, jnp.where(is_l, b_, c * u - b_ * v))
                second = jnp.where(is_k, b_, jnp.where(is_l, -a, a * v - b_ * u))

                def pivoted(x):
                    row_k, row_l = spread_row(x, k), spread_row(x, k + 1)
                    return jnp.where(pair, 0.0, x) - scale * (first * row_k + second * row_l)

                top = [x if j <= k + 1 else pivoted(x) for j, x in enumerate(top)]
                riders = [pivoted(x) for x in riders]
                wide = pivoted(wide)
                yield
            rows = [spread_row(wide, j) for j in range(group)]
            ahead = [
                x - total([factors[s + 1][j] * spread_row(riders[n], j) for j in range(group)])
                for n, x in enumerate(low)
            ]
            for i in range(inner):
                if i != s:
                    change = total([factors[i][j] * rows[j] for j in range(group)])
                    work[i] = jnp.where(own, 0.0, work[i]) - change
            work[s] = wide
            if s == 1 and late is not None:
                late()
                late = None
            yield
        slabs[inner * b : inner * (b + 1)] = work
        zero = jnp.zeros((group, lanes), jnp.float32)
        in_block = (lane_ids >= base) & (lane_ids < base + group * inner)
        solved = [zero] * (inner * b) + work + [zero] * (count - inner * (b + 1))
        solved = right_terms(jnp.concatenate(solved, axis=0))

        def merge(first, last, solved=solved, in_block=in_block):
            if first == last:
                return
            here = jnp.concatenate([jnp.where(in_block, x, 0.0) for x in slabs[first:last]], axis=0)
            change = dot(left_terms(here), solved)
            for i in range(first, last):
                at = group * (i - first)
                slabs[i] = jnp.where(in_block, 0.0, slabs[i]) - change[at : at + group]

        soon = min(inner * (b + 2), count)
        merge(inner * (b + 1), soon)

        def late(b=b, soon=soon, merge=merge):
            merge(0, inner * b)
            merge(soon, count)

    late()
    return jnp.concatenate(slabs, axis=0)


inverse_yields = 80


class Queue:
    def __init__(self):
        self.tasks = []

    def add(self, task):
        self.tasks.append(task)

    def between(self, left, keep=0):
        for _ in range(-(-(len(self.tasks) - keep) // max(left, 1))):
            if self.tasks:
                self.tasks.pop(0)()

    def flush(self, keep=0):
        while len(self.tasks) > keep:
            self.tasks.pop(0)()


def inverses(blocks, queue, keep):
    ride = 4 if len(blocks) == 1 else 0
    runs = [inverse_128(block, ride) for block in blocks]
    results = [None] * len(runs)
    left = inverse_yields // 5
    count = 0
    while any(result is None for result in results):
        for n, run in enumerate(runs):
            try:
                next(run)
            except StopIteration as stop:
                results[n] = stop.value
        count += 1
        if count % 5 == 0:
            queue.between(left, keep)
            left -= 1
    queue.flush(keep)
    return results


def span(first, last):
    return slice(lanes * first, lanes * last)


class System:
    def __init__(self, top, bottom, right, out, terms_left, terms_right):
        self.top, self.bottom, self.right, self.out = top, bottom, right, out
        self.terms_left, self.terms_right = terms_left, terms_right
        self.panels = top.shape[-2] // lanes
        self.blocks = top.shape[-1] // lanes

    def at(self, rows, cols):
        if rows[0] < self.panels:
            return self.top, (span(*rows), span(*cols))
        low = self.panels
        return self.bottom, (span(rows[0] - low, rows[1] - low), span(cols[0] - low, cols[1] - low))

    def load(self, rows, cols):
        ref, where = self.at(rows, cols)
        return ref[where]

    def store(self, rows, cols, value):
        ref, where = self.at(rows, cols)
        ref[where] = value

    def prepare(self, p, q):
        store_split(self.terms_left, span(q, q + 1), whole, self.load((p, p + 1), (q, q + 1)).T)

    def solve(self, p, cols, inverse):
        solved = dot(inverse, right_terms(self.load((p, p + 1), cols)))
        self.store((p, p + 1), cols, solved)
        store_split(self.terms_right, whole, span(*cols), solved)

    def update(self, rows, cols):
        change = dot(
            load_left(self.terms_left, span(*rows), whole),
            load_right(self.terms_right, whole, span(*cols)),
        )
        self.store(rows, cols, self.load(rows, cols) - change)

    def forward(self, p, inverse):
        here = left_terms(self.right[:, span(p, p + 1)])
        self.out[:, span(p, p + 1)] = dot(here, inverse)
        if p + 1 < self.blocks:
            later = span(p + 1, self.blocks)
            change = dot(here, load_right(self.terms_right, whole, later))
            self.right[:, later] = self.right[:, later] - change

    def diagonal(self, p):
        return self.load((p, p + 1), (p, p + 1))

    def ready(self, p):
        if p + 1 < self.blocks:
            self.prepare(p, p + 1)
            block = self.load((p, p + 1), (p + 1, p + 2))
            store_split(self.terms_right, whole, span(p + 1, p + 2), block)

    def next_pivot(self, p, inverse):
        after = (p + 1, p + 2)
        if p + 1 < self.blocks:
            solved = dot(left_terms(inverse), load_right(self.terms_right, whole, span(*after)))
            terms = right_terms(solved)
            change = dot(load_left(self.terms_left, span(*after), whole), terms)
            self.store(after, after, self.load(after, after) - change)
            self.store((p, p + 1), after, solved)
            store_split(self.terms_right, whole, span(*after), solved)
        self.store((p, p + 1), (p, p + 1), inverse)

    def background(self, p, inverse, queue):
        terms = left_terms(inverse)
        after = p + 1
        strips = []
        q = after + 1
        while q < self.blocks:
            end = min(self.blocks, q + 2 if q % 2 == 0 else q + 1)
            strips.append((q, end))
            q = end
        for strip in strips:
            for q in range(*strip):
                queue.add(functools.partial(self.prepare, p, q))
            queue.add(functools.partial(self.solve, p, strip, terms))
        for strip in strips:
            start = after
            while start < strip[1]:
                end = min(strip[1], start + 8)
                if start < self.panels:
                    end = min(end, self.panels)
                queue.add(functools.partial(self.update, (start, end), strip))
                start = end
        queue.add(functools.partial(self.forward, p, right_terms(inverse)))

    def back(self, known, x):
        for p in reversed(range(self.panels)):
            here = self.out[:, span(p, p + 1)]
            for n, terms in enumerate(known):
                low = self.panels * (n + 1)
                factor = self.top[span(p, p + 1), span(low, low + self.panels)]
                here = here - dot(terms, right_terms(factor, 1), 1)
            if p + 1 < self.panels:
                later = span(p + 1, self.panels)
                factor = self.top[span(p, p + 1), later]
                here = here - dot(left_terms(x[:, later]), right_terms(factor, 1), 1)
            x[:, span(p, p + 1)] = here


def eliminate(systems, queue, keep_first=0, fresh=True):
    for p in range(systems[0].panels):
        keep = keep_first if p == 0 else 0
        for system in systems:
            if p == 0 and fresh:
                system.ready(p)
            else:
                queue.add(functools.partial(system.ready, p))
        found = inverses([system.diagonal(p) for system in systems], queue, keep)
        for system, inverse in zip(systems, found):
            system.next_pivot(p, inverse)
        for system, inverse in zip(systems, found):
            system.background(p, inverse, queue)


def load_factor(slab, terms, s):
    value = slab(s)
    store_split(terms, slice(value.shape[0] * s, value.shape[0] * (s + 1)), whole, value)


def gram_rows(terms, rows):
    return dot(load_left(terms, rows, whole), load_right(terms, whole, whole, 1), 1)


def gram_cols(terms, cols):
    return dot(load_left(terms, whole, whole), load_right(terms, cols, whole, 1), 1)


def gram_tasks(queue, slab, parts, out, terms):
    rows = out.shape[0] // parts

    def multiply(s):
        here = slice(rows * s, rows * (s + 1))
        out[here, :] = gram_rows(terms, here)

    for s in range(parts):
        queue.add(functools.partial(load_factor, slab, terms, s))
    for s in range(parts):
        queue.add(functools.partial(multiply, s))


def slab_of(edge, block=0):
    rows = edge.shape[2] - group
    return lambda s: edge[block, s, :rows, :]


def on_diagonal(mass, rows):
    ids = (rows, rows)
    diag = lax.broadcasted_iota(jnp.int32, ids, 0) == lax.broadcasted_iota(jnp.int32, ids, 1)
    return jnp.where(diag, mass, 0.0)


def add_mass(table, mass, rows):
    for s in range(mass.shape[1]):
        here = slice(rows * s, rows * (s + 1))
        table[here, here] = table[here, here] + on_diagonal(mass[0, s, :1, :rows], rows)


def add_rhs(right, rhs, first, block=0):
    for q in range(rhs.shape[1] // lanes):
        right[:, span(first + q, first + q + 1)] = rhs[block, span(q, q + 1), :].T


def pack_sent(side, sent, reduced, reduced_right, ready):
    for part, pieces in enumerate(packed_pieces(reduced.shape[0])):

        @pl.when(ready & (side[2] == part))
        def _():
            at = 0
            for p, first, last in pieces:
                width = lanes * (last - first)
                sent[:, at : at + width] = reduced[span(p, p + 1), span(first, last)]
                at += width
            sent[:, at:] = reduced_right[...]


def packed_pieces(size):
    panels = size // lanes
    order = [[p for p in range(panels) if p % 4 in (0, 3)], [p for p in range(panels) if p % 4 in (1, 2)]]
    return [[(p, p, panels) for p in rows] for rows in order]


def chain_kernel(
    side, start_edge, first_edge, next_edge, first_mass, next_mass, first_rhs, next_rhs,
    solved, solved_right, reduced, reduced_right, sent,
    edge, right_rows, edge_terms, terms_left, terms_right,
):
    size = reduced.shape[0]
    parts = start_edge.shape[1]
    quarter = start_edge.shape[2] - group
    step, steps = pl.program_id(0), pl.num_programs(0)

    @pl.when(step == 0)
    def _():
        queue = Queue()
        gram_tasks(queue, slab_of(start_edge), parts, edge, edge_terms)
        queue.flush()
        reduced[...] = jnp.where(side[0] == 0, edge[...], 0.0)
        add_mass(reduced, first_mass, quarter)
        gram_tasks(queue, slab_of(first_edge), parts, edge, edge_terms)
        queue.flush()
        add_rhs(reduced_right, first_rhs, 0)

    top = solved.at[0]
    top[:, :size] = reduced[...] + edge[...]
    top[:, size:] = -edge[...]
    reduced[...] = edge[...]
    add_mass(reduced, next_mass, quarter)
    right_rows[:, :size] = reduced_right[...]
    add_rhs(right_rows, next_rhs, size // lanes)

    queue = Queue()
    gram_tasks(queue, slab_of(next_edge), parts, edge, edge_terms)
    system = System(top, reduced, right_rows, solved_right.at[0], terms_left, terms_right)
    eliminate([system], queue)
    queue.flush()
    reduced_right[...] = right_rows[:, size:]
    pack_sent(side, sent, reduced, reduced_right, step == steps - 1)


def pair_kernel(
    side, gathered, rhs,
    first_hbm, third_hbm, second_hbm, first_right, third_right, second_right,
    reduced, reduced_right, sent,
    first_top, third_top, rest, rights, *scratch,
):
    edge_terms, terms, sems = scratch[:4], scratch[4:8], scratch[8]
    size = reduced.shape[0]
    parts = gathered.shape[1]
    quarter = gathered.shape[2] - group
    steps = gathered.shape[0] - 1
    own, after = slice(0, size), slice(size, 2 * size)
    edges = [jnp.where(side[0] == 0, i + 1, steps - i) for i in range(steps)]
    blocks = [jnp.where(side[0] == 0, i, steps - i) for i in range(steps + 1)]

    def strip(n, c):
        here = slice(size // 2 * c, size // 2 * (c + 1))
        near = slice(size + here.start, size + here.stop)
        far = slice(2 * size + here.start, 2 * size + here.stop)
        gram = gram_cols(edge_terms[n], here)

        def with_mass(ref, first, i):
            for s in range(parts // 2 * c, parts // 2 * (c + 1)):
                at = slice(first + quarter * s, first + quarter * (s + 1))
                mass = gathered[blocks[i], s, quarter : quarter + 1, :quarter]
                ref[at, at] = ref[at, at] + on_diagonal(mass, quarter)

        if n == 0:
            first_top[:, here] = jnp.where(side[0] == 0, gram, 0.0)
            with_mass(first_top, 0, 0)
        elif n == 1:
            first_top[:, here] = first_top[:, here] + gram
            first_top[:, near] = -gram
            rest[own, here] = gram
            with_mass(rest, 0, 1)
        elif n == 2:
            rest[own, here] = rest[own, here] + gram
            third_top[:, here] = gram
            third_top[:, near] = -gram
            with_mass(third_top, 0, 2)
        else:
            third_top[:, here] = third_top[:, here] + gram
            third_top[:, far] = -gram
            rest[own, near] = jnp.zeros((size, size // 2), jnp.float32)
            rest[after, near] = gram
            with_mass(rest, size, 3)

    for n in range(4):
        for s in range(parts):
            load_factor(slab_of(gathered, 0 if n == 0 else edges[n - 1]), edge_terms[n], s)
        strip(n, 0)
    rights[0, :, 2 * size :] = jnp.zeros_like(reduced_right)
    rights[0, :, after] = jnp.zeros_like(reduced_right)
    for n, first, i in ((0, 0, 0), (1, 0, 2), (1, 1, 1), (1, 2, 3)):
        add_rhs(rights.at[n], rhs, first * (size // lanes), blocks[i] ^ side[3])

    queue = Queue()
    for n in range(4):
        queue.add(functools.partial(strip, n, 1))
    first = System(
        first_top, rest.at[own, own], rights.at[0, :, : 2 * size], first_right, terms[0], terms[1]
    )
    third = System(third_top, rest, rights.at[1], third_right, terms[2], terms[3])
    eliminate([first, third], queue, 4)

    def hand_over():
        rights[1, :, after] = rights[1, :, after] + rights[0, :, after]

    leaving = [
        pltpu.make_async_copy(first_top, first_hbm, sems.at[0]),
        pltpu.make_async_copy(third_top, third_hbm, sems.at[1]),
        pltpu.make_async_copy(rest.at[own, :], second_hbm, sems.at[2]),
    ]
    queue.add(hand_over)
    queue.add(leaving[0].start)
    queue.add(leaving[1].start)
    second = System(
        rest.at[own, :], rest.at[after, after], rights.at[1, :, size:], second_right, terms[0], terms[1]
    )
    eliminate([second], queue, 0, False)
    queue.flush()
    leaving[2].start()
    reduced[...] = rest[after, after]
    reduced_right[...] = rights[1, :, 2 * size :]
    pack_sent(side, sent, reduced, reduced_right, True)
    for copy in leaving:
        copy.wait()


def middle_kernel(
    side, own_edge, sent_edge, reduced, reduced_right,
    solved, solved_right, target, target_right,
    right_rows, edge_terms, terms_left, terms_right,
):
    size = reduced.shape[0]
    parts = own_edge.shape[1]
    own, sent = slab_of(own_edge), slab_of(sent_edge)

    def strip(c):
        here = slice(size // 2 * c, size // 2 * (c + 1))
        gram = gram_cols(edge_terms, here)
        solved[:, here] = reduced[:, here] + gram
        solved[:, size + here.start : size + here.stop] = -gram
        target[:, here] = gram

    for s in range(parts):
        load_factor(lambda s: jnp.where(side[0] == 0, sent(s), own(s)), edge_terms, s)
    strip(0)
    right_rows[:, :size] = reduced_right[...]
    right_rows[:, size:] = jnp.zeros_like(target_right)
    queue = Queue()
    queue.add(functools.partial(strip, 1))
    system = System(solved, target, right_rows, solved_right, terms_left, terms_right)
    eliminate([system], queue, 1)
    queue.flush()
    target_right[...] = right_rows[:, size:]


def receive(side, top, right_rows, target, target_right, mine, other):
    half_cols = other.shape[1]
    for part, pieces in enumerate(packed_pieces(target.shape[0])):
        at = 0
        for p, first, last in pieces:
            cols = slice(at, at + lanes * (last - first))
            received = jnp.where(side[2] == part, mine[:, cols], other[:, cols])
            here = (span(p, p + 1), span(first, last))
            top[here] = target[here] + received
            at = cols.stop
    right_rows[...] = target_right[...] + mine[:, half_cols:]


def hand_out(out, x):
    for q in range(out.shape[0] // lanes):
        out[span(q, q + 1), :] = x[:, span(q, q + 1)].T


def pair_final_kernel(
    side, target, target_right, mine, other, middle_right, first_right, third_right, second_right,
    middle_hbm, first_hbm, third_hbm, second_hbm,
    out, top, right_rows, ended, x, terms_left, terms_right, middle, first, third, second, sems,
):
    place = side[1]
    pairs = ((middle_hbm, middle), (first_hbm, first), (third_hbm, third), (second_hbm, second))
    coming = [pltpu.make_async_copy(a, b, sems.at[n]) for n, (a, b) in enumerate(pairs)]
    for copy in coming:
        copy.start()
    receive(side, top, right_rows, target, target_right, mine, other)
    queue = Queue()
    eliminate([System(top, None, right_rows, ended, terms_left, terms_right)], queue)
    queue.flush()
    for copy in coming:
        copy.wait()

    def back(top, right, known):
        System(top, None, None, right, None, None).back(known, x)
        return left_terms(x[...])

    def give(i):
        @pl.when(place == i)
        def _():
            hand_out(out, x)

    far = back(top, ended, [])
    near = back(middle, middle_right, [far])
    give(3)
    last = back(second, second_right, [near])
    give(1)

    @pl.when(place == 0)
    def _():
        back(first, first_right, [last])
        hand_out(out, x)

    @pl.when(place == 2)
    def _():
        back(third, third_right, [last, near])
        hand_out(out, x)


def final_kernel(
    side, target, target_right, mine, other, middle, middle_right, chain, chain_right,
    out, top, right_rows, ended, x, terms_left, terms_right,
):
    place = side[1]
    steps = chain.shape[0]
    receive(side, top, right_rows, target, target_right, mine, other)
    queue = Queue()
    eliminate([System(top, None, right_rows, ended, terms_left, terms_right)], queue)
    queue.flush()

    def back(top, right, known):
        System(top, None, None, right, None, None).back(known, x)
        return left_terms(x[...])

    def give(i):
        @pl.when(place == i)
        def _():
            hand_out(out, x)

    known = back(top, ended, [])
    back(middle, middle_right, [known])
    give(steps)

    def walk(n, _):
        i = steps - 1 - n
        back(chain.at[i], chain_right.at[i], [left_terms(x[...])])
        give(i)
        return 0

    lax.fori_loop(0, steps, walk, 0)


def local(edge_factor, mass, rhs):
    _, quarter, size = edge_factor.shape
    cols = rhs.shape[2]
    blocks, parts = lax.axis_size("tm"), lax.axis_size("row")
    half = blocks // 2
    steps = half - 1
    mine = lax.axis_index("tm")
    right = (mine >= half).astype(jnp.int32)
    place = jnp.where(right == 0, mine, blocks - 1 - mine)
    parity = lax.axis_index("row") % 2
    side = jnp.stack([right, place, parity, mine % half]).astype(jnp.int32)

    halves = [[part * half + i for i in range(half)] for part in range(2)]
    halves_all = [[t * parts + r for t in ids for r in range(parts)] for ids in halves]
    swap = [(r, r ^ 1) for r in range(parts)]
    mass_rows = jnp.pad(mass, ((0, group - 1), (0, size - quarter)))
    packed = jnp.concatenate([edge_factor[0], mass_rows], axis=0)
    gathered = lax.all_gather(packed, ("tm", "row"), axis_index_groups=halves_all)
    gathered = gathered.reshape(half, parts, quarter + group, size)
    rhs_slots = [rhs[0]] + [
        lax.ppermute(rhs[0], "tm", [(t, t ^ d) for t in range(blocks)]) for d in range(1, half)
    ]
    rhs_half = jnp.stack(rhs_slots)
    gathered, rhs_half = lax.optimization_barrier((gathered, rhs_half))
    down = [(t + half, t) for t in range(half)]
    sent_edge = lax.ppermute(gathered[:1], "tm", down)

    vmem = pl.BlockSpec(memory_space=pltpu.VMEM)
    smem = pl.BlockSpec(memory_space=pltpu.SMEM)
    f32 = lambda *shape: jax.ShapeDtypeStruct(shape, jnp.float32)
    scratch = lambda *shape: pltpu.VMEM(shape, jnp.float32)
    terms = lambda *shape: pltpu.VMEM(shape, bf16)
    half_cols = sum(lanes * (b - a) for _, a, b in packed_pieces(size)[0])

    def edge_at(i, s):
        return jnp.where(s[0] == 0, i + 1, steps - i)

    def block_at(i, s):
        return jnp.where(s[0] == 0, i, steps - i)

    edge_block = (1, parts, quarter + group, size)
    mass_block = (1, parts, group, size)
    rhs_block = (1, size, cols)
    last = steps - 1
    if steps == 3:
        *stored, reduced, reduced_right, sent = pl.pallas_call(
            pair_kernel,
            in_specs=[smem, vmem, vmem],
            out_specs=(pl.BlockSpec(memory_space=pl.ANY),) * 3 + (vmem,) * 6,
            out_shape=(
                f32(size, 2 * size),
                f32(size, 3 * size),
                f32(size, 2 * size),
                f32(cols, size),
                f32(cols, size),
                f32(cols, size),
                f32(size, size),
                f32(cols, size),
                f32(lanes, half_cols + size),
            ),
            scratch_shapes=[
                scratch(size, 2 * size),
                scratch(size, 3 * size),
                scratch(2 * size, 2 * size),
                scratch(2, cols, 3 * size),
            ]
            + [terms(3, size, size)] * 4
            + [terms(3, 2 * size, lanes), terms(3, lanes, 2 * size)]
            + [terms(3, 3 * size, lanes), terms(3, lanes, 3 * size)]
            + [pltpu.SemaphoreType.DMA((3,))],
            compiler_params=pltpu.CompilerParams(vmem_limit_bytes=vmem_bytes),
        )(side, gathered, rhs_half)
    else:
        *stored, reduced, reduced_right, sent = pl.pallas_call(
            chain_kernel,
            grid_spec=pltpu.PrefetchScalarGridSpec(
                num_scalar_prefetch=1,
                grid=(steps,),
                in_specs=[
                    pl.BlockSpec(edge_block, lambda i, s: (0, 0, 0, 0)),
                    pl.BlockSpec(edge_block, lambda i, s: (edge_at(0, s), 0, 0, 0)),
                    pl.BlockSpec(edge_block, lambda i, s: (edge_at(jnp.minimum(i + 1, last), s), 0, 0, 0)),
                    pl.BlockSpec(mass_block, lambda i, s: (block_at(0, s), 0, quarter // group, 0)),
                    pl.BlockSpec(mass_block, lambda i, s: (block_at(i + 1, s), 0, quarter // group, 0)),
                    pl.BlockSpec(rhs_block, lambda i, s: (block_at(0, s) ^ s[3], 0, 0)),
                    pl.BlockSpec(rhs_block, lambda i, s: (block_at(i + 1, s) ^ s[3], 0, 0)),
                ],
                out_specs=(
                    pl.BlockSpec((1, size, 2 * size), lambda i, s: (i, 0, 0)),
                    pl.BlockSpec((1, cols, size), lambda i, s: (i, 0, 0)),
                    pl.BlockSpec((size, size), lambda i, s: (0, 0)),
                    pl.BlockSpec((cols, size), lambda i, s: (0, 0)),
                    pl.BlockSpec((lanes, half_cols + size), lambda i, s: (0, 0)),
                ),
                scratch_shapes=[
                    scratch(size, size),
                    scratch(cols, 2 * size),
                    terms(3, size, size),
                    terms(3, 2 * size, lanes),
                    terms(3, lanes, 2 * size),
                ],
            ),
            out_shape=(
                f32(steps, size, 2 * size),
                f32(steps, cols, size),
                f32(size, size),
                f32(cols, size),
                f32(lanes, half_cols + size),
            ),
            compiler_params=pltpu.CompilerParams(vmem_limit_bytes=vmem_bytes),
        )(side, gathered, gathered, gathered, gathered, gathered, rhs_half, rhs_half)

    across = [(t, (t + half) % blocks) for t in range(blocks)]
    received = lax.ppermute(sent, "tm", across)
    middle, middle_right, target, target_right = pl.pallas_call(
        middle_kernel,
        out_shape=(f32(size, 2 * size), f32(cols, size), f32(size, size), f32(cols, size)),
        grid=(1,),
        in_specs=[smem, pl.BlockSpec(edge_block, lambda i: (0, 0, 0, 0))] + [vmem] * 3,
        out_specs=(vmem,) * 4,
        scratch_shapes=[
            scratch(cols, 2 * size),
            terms(3, size, size),
            terms(3, 2 * size, lanes),
            terms(3, lanes, 2 * size),
        ],
        compiler_params=pltpu.CompilerParams(vmem_limit_bytes=vmem_bytes),
    )(side, gathered, sent_edge, reduced, reduced_right)

    received, target = lax.optimization_barrier((received, target))
    received_other = lax.ppermute(received[:, :half_cols], "row", swap)
    final_scratch = [
        scratch(size, size),
        scratch(cols, size),
        scratch(cols, size),
        scratch(cols, size),
        terms(3, size, lanes),
        terms(3, lanes, size),
    ]
    arrived = (target, target_right, received, received_other)
    if steps == 3:
        first, third, second, first_right, third_right, second_right = stored
        solution = pl.pallas_call(
            pair_final_kernel,
            out_shape=f32(size, cols),
            in_specs=[smem] + [vmem] * 8 + [pl.BlockSpec(memory_space=pl.ANY)] * 4,
            out_specs=vmem,
            scratch_shapes=final_scratch
            + [scratch(size, 2 * size), scratch(size, 2 * size)]
            + [scratch(size, 3 * size), scratch(size, 2 * size)]
            + [pltpu.SemaphoreType.DMA((4,))],
            compiler_params=pltpu.CompilerParams(vmem_limit_bytes=vmem_bytes),
        )(
            side, *arrived, middle_right, first_right, third_right, second_right,
            middle, first, third, second,
        )
    else:
        solution = pl.pallas_call(
            final_kernel,
            out_shape=f32(size, cols),
            in_specs=[smem] + [vmem] * 8,
            out_specs=vmem,
            scratch_shapes=final_scratch,
            compiler_params=pltpu.CompilerParams(vmem_limit_bytes=vmem_bytes),
        )(side, *arrived, middle, middle_right, *stored)
    return solution[None]


def solution(mesh):
    placed = (P("tm", "row", None), P("tm", "row"), P("tm", None, "row"))
    return jax.shard_map(
        local, mesh=mesh, in_specs=placed, out_specs=P("tm", None, "row"), check_vma=False
    )
```
